256 devices in a mesh: grp: 8 (over y, core), dev: 32 (over z, x).
Axes of the slice: x: 4, y: 4, z: 8, core: 2. Of those that a mesh axis runs over, the one named last changes fastest.
Arguments:
- fine_input: bfloat16 [512, 64, 4096], P(('grp', 'dev')), may hold values from -6 to 6
- conv_weight: bfloat16 [27, 64, 64], replicated, may hold values from -0.15625 to 0.15625
- down_weight: bfloat16 [8, 128, 64], replicated, may hold values from -0.25 to 0.25
- coarse_cot: bfloat16 [256, 128, 4096], P(('grp', 'dev')), may hold values from -6 to 6
- neighbours: int32 [512, 26], P(('grp', 'dev')), may hold values from -1 to 511, as said below
- children: int32 [256, 8], P(('grp', 'dev')), may hold values from -1 to 511, as said below
Outputs:
- coarse_features: bfloat16 [256, 128, 4096], P(('grp', 'dev'))
- input_grad: bfloat16 [512, 64, 4096], P(('grp', 'dev'))
- conv_grad: float32 [27, 64, 64], replicated
- down_grad: float32 [8, 128, 64], replicated
The draws below stay inside these ranges and needn't reach their ends.
Inputs may be any that keep to these rules, and one draw needn't show every extreme that they name: `neighbours`: entry -1 means no brick at that offset. A brick named for offset (dx, dy, dz) of a brick on device (g, d) lies on device (g, d + dy); the relation is symmetric. Entry -1 means no child. The children of a coarse slot on device (g, d) lie on devices (g, 2 (d // 2)) and (g, 2 (d // 2) + 1), the child of octant (ox, oy, oz) on the one with dev index 2 (d // 2) + oy. Every fine brick is the child of exactly one coarse slot and octant.
All inputs are finite; a program needn't handle non-finite values.
Results may differ from the reference program's by a relative error of at most 0.005.
Values may be sent and summed in bfloat16 or wider, within the bound.
No kernel may reach another device: no remote copies, remote signals or barrier semaphores. Data moves between devices by JAX's collectives and lax.ppermute only.
A program may use at most 128 MiB of HBM per device.

```python
import jax
import jax.numpy as jnp
import numpy as np
from jax import lax

SIDE = 16
C0 = 64
C1 = 128
B0 = 2
CROPS = 8
ROWS = 32
NB0 = 512
NB1 = 256


def geometry(key):
    pairs = ROWS // 2
    per_crop = ROWS * B0
    key_x, key_z, key_coarse, key_fine = jax.random.split(key, 4)
    start_x = jax.random.randint(key_x, (CROPS,), 0, 15)
    start_z = jax.random.randint(key_z, (CROPS,), 0, 17 - B0)
    coarse_keys = jax.random.split(key_coarse, CROPS * pairs)
    spots = jax.vmap(lambda subkey: jax.random.permutation(subkey, 2 * B0))(coarse_keys)[:, :B0]
    spots = spots.reshape(CROPS, pairs, B0)
    fine_keys = jax.random.split(key_fine, CROPS * ROWS)
    codes = jax.vmap(lambda subkey: jax.random.permutation(subkey, 4 * B0))(fine_keys)[:, :B0]
    codes = codes.reshape(CROPS, ROWS, B0)
    row_pair = jnp.arange(ROWS) // 2
    pair_spots = spots[:, row_pair, :]
    chosen = jnp.take_along_axis(pair_spots, codes // 4, axis=2)
    pos_x = 2 * (start_x[:, None, None] + chosen // B0) + codes // 2 % 2
    pos_y = jnp.broadcast_to(jnp.arange(ROWS)[None, :, None], codes.shape)
    pos_z = 2 * (start_z[:, None, None] + chosen % B0) + codes % 2
    coords = jnp.stack([pos_x, pos_y, pos_z], axis=-1).reshape(CROPS, per_crop, 3)
    offsets = jnp.asarray(np.array([(t // 9 - 1, t // 3 % 3 - 1, t % 3 - 1) for t in range(27) if t != 13], dtype=np.int32))
    wanted = coords[:, :, None, :] + offsets[None, None, :, :]
    match = jnp.all(wanted[:, :, :, None, :] == coords[:, None, None, :, :], axis=-1)
    local = jnp.sum(match.astype(jnp.int32) * (jnp.arange(per_crop) + 1), axis=-1) - 1
    base = (jnp.arange(CROPS) * per_crop)[:, None, None]
    neighbour_list = jnp.where(local >= 0, base + local, -1).reshape(NB0, 26)
    octs = jnp.arange(8)
    octs_y = octs // 2 % 2
    codes_pair = codes.reshape(CROPS, pairs, 2, B0)
    want_code = 4 * jnp.arange(B0)[:, None] + 2 * (octs // 4)[None, :] + (octs % 2)[None, :]
    candidate = codes_pair[:, :, octs_y, :]
    hit = candidate[:, :, None, :, :] == want_code[None, None, :, :, None]
    slot = jnp.sum(hit.astype(jnp.int32) * (jnp.arange(B0) + 1), axis=-1) - 1
    device = jnp.arange(CROPS)[:, None, None, None] * ROWS + 2 * jnp.arange(pairs)[None, :, None, None] + octs_y[None, None, None, :]
    child_list = jnp.where(slot >= 0, device * B0 + slot, -1).reshape(NB1, 8)
    return (neighbour_list.astype(jnp.int32), child_list.astype(jnp.int32))


def draw_neighbours(key, part):
    found = geometry(key)
    return found[0]


def draw_children(key, part):
    found = geometry(key)
    return found[1]


def level_of(stream_key, extent, shards, least, top_value):
    def one(dim, blocks):
        heights = jax.random.uniform(jax.random.fold_in(jax.random.fold_in(stream_key, 6), dim), (blocks,), jnp.float32, least / len(shards), top_value / len(shards))
        return jnp.repeat(jnp.exp(heights), extent[dim] // blocks).reshape((-1,) + (1,) * (len(extent) - dim - 1))

    gain = one(*shards[0])
    for cut in shards[1:]:
        gain = gain * one(*cut)
    return gain


def bell_draw(key, shape, scale, bound, shards=(), held_as=jnp.bfloat16):
    drawn = scale * jax.random.normal(key, shape, jnp.float32)
    if shards:
        drawn = drawn * level_of(key, shape, shards, -0.22, 0.18)
    return jnp.clip(drawn, -bound, bound).astype(held_as)


def setup_inputs(seed: int = 0) -> dict:
    key_list = jax.random.split(jax.random.key(seed), 7)
    return {
        "fine_input": bell_draw(key_list[0], (NB0, C0, SIDE**3), 1.0, 6.0, ((0, 256),)),
        "conv_weight": bell_draw(key_list[1], (27, C0, C0), (27 * C0) ** -0.5, 0.15625),
        "down_weight": bell_draw(key_list[2], (8, C1, C0), (8 * C0) ** -0.5, 0.25),
        "coarse_cot": bell_draw(key_list[3], (NB1, C1, SIDE**3), 1.0, 6.0, ((0, 256),)),
        "neighbours": draw_neighbours(jax.random.fold_in(key_list[6], 71), 0),
        "children": draw_children(jax.random.fold_in(key_list[6], 71), 0),
    }


def face_sets(bricks_in):
    last = bricks_in.shape[-1] - 1
    x_faces = jnp.stack([bricks_in[:, :, 0], bricks_in[:, :, last]], axis=1)
    y_faces = jnp.stack([bricks_in[:, :, :, 0], bricks_in[:, :, :, last]], axis=1)
    z_faces = jnp.stack([bricks_in[..., 0], bricks_in[..., last]], axis=1)
    return x_faces, y_faces, z_faces


def ranges(offset, edge):
    if offset == 0:
        return slice(1, edge + 1), slice(0, edge)
    if offset == 1:
        return slice(edge + 1, edge + 2), slice(0, 1)
    return slice(0, 1), slice(edge - 1, edge)


def assemble(bricks_in, lookup):
    number, channels, edge = bricks_in.shape[0], bricks_in.shape[1], bricks_in.shape[2]
    padded = jnp.zeros((number, channels, edge + 2, edge + 2, edge + 2), bricks_in.dtype)
    padded = padded.at[:, :, 1:edge + 1, 1:edge + 1, 1:edge + 1].set(bricks_in)
    column = 0
    for step_x in (-1, 0, 1):
        for step_y in (-1, 0, 1):
            for step_z in (-1, 0, 1):
                if step_x == 0 and step_y == 0 and step_z == 0:
                    continue
                put_x, take_x = ranges(step_x, edge)
                put_y, take_y = ranges(step_y, edge)
                put_z, take_z = ranges(step_z, edge)
                if step_y != 0:
                    plane = lookup(1, step_y, column)
                    block = plane[:, :, take_x, take_z][:, :, :, None, :]
                elif step_x != 0:
                    plane = lookup(0, step_x, column)
                    block = plane[:, :, take_y, take_z][:, :, None, :, :]
                else:
                    plane = lookup(2, step_z, column)
                    block = plane[:, :, take_x, take_y][:, :, :, :, None]
                padded = padded.at[:, :, put_x, put_y, put_z].set(block)
                column += 1
    return padded


def make_lookup(tables, near):
    def lookup(face_axis, offset, column):
        entry = near[:, column]
        facing = 0 if offset == 1 else 1
        plane = tables[face_axis][jnp.clip(entry, 0), facing]
        return jnp.where((entry >= 0)[:, None, None, None], plane, jnp.zeros_like(plane))
    return lookup


def conv_taps(padded, weights):
    number, channels = padded.shape[0], padded.shape[1]
    edge = padded.shape[2] - 2
    outs = weights.shape[1]
    grouped = weights.reshape(3, 3, 3, outs, channels).transpose(0, 1, 3, 2, 4).reshape(9, outs, 3 * channels)
    total = jnp.zeros((number, outs, edge, edge, edge), jnp.float32)
    for first in range(3):
        for second in range(3):
            stacked = jnp.concatenate([padded[:, :, first:first + edge, second:second + edge, third:third + edge] for third in range(3)], axis=1)
            total = total + jnp.einsum('ok,bkxyz->boxyz', grouped[3 * first + second].astype(jnp.float32), stacked.astype(jnp.float32))
    return total.reshape(number, outs, edge ** 3)


def tap_grads(padded, grads):
    number, channels = padded.shape[0], padded.shape[1]
    edge = padded.shape[2] - 2
    outs = grads.shape[1]
    shaped = grads.reshape(number, outs, edge, edge, edge).astype(jnp.float32)
    pieces = []
    for first in range(3):
        for second in range(3):
            stacked = jnp.concatenate([padded[:, :, first:first + edge, second:second + edge, third:third + edge] for third in range(3)], axis=1)
            pieces.append(jnp.einsum('boxyz,bkxyz->ok', shaped, stacked.astype(jnp.float32)))
    joined = jnp.stack(pieces).reshape(3, 3, outs, 3, channels)
    return joined.transpose(0, 1, 3, 2, 4).reshape(27, outs, channels)


def to_octants(bricks_in):
    number, channels, edge = bricks_in.shape[0], bricks_in.shape[1], bricks_in.shape[2]
    half_side = edge // 2
    shaped = bricks_in.reshape(number, channels, half_side, 2, half_side, 2, half_side, 2)
    return shaped.transpose(0, 3, 5, 7, 1, 2, 4, 6).reshape(number, 8 * channels, half_side ** 3)


def from_octants(parts, channels, edge):
    number = parts.shape[0]
    half_side = edge // 2
    shaped = parts.reshape(number, 2, 2, 2, channels, half_side, half_side, half_side)
    return shaped.transpose(0, 4, 5, 1, 6, 2, 7, 3).reshape(number, channels, edge ** 3)


def reference(fine_input, conv_weight, down_weight, coarse_cot, neighbours, children):
    total, channels = fine_input.shape[0], fine_input.shape[1]
    coarse_width = down_weight.shape[1]
    coarse_total = coarse_cot.shape[0]
    half_side = SIDE // 2
    all_bricks = fine_input.reshape(total, channels, SIDE, SIDE, SIDE)
    input_tables = face_sets(all_bricks)
    blocks = total // B0
    block_ids = jnp.arange(blocks, dtype=jnp.int32)
    down_flat = down_weight.transpose(1, 0, 2).reshape(coarse_width, 8 * channels).astype(jnp.float32)

    def forward_block(block):
        start = (block * B0).astype(jnp.int32)
        local = lax.dynamic_slice_in_dim(all_bricks, start, B0, 0)
        near = lax.dynamic_slice_in_dim(neighbours, start, B0, 0)
        padded = assemble(local, make_lookup(input_tables, near))
        preact = conv_taps(padded, conv_weight)
        active = jax.nn.silu(preact).astype(jnp.bfloat16)
        parts = to_octants(active.reshape(B0, channels, SIDE, SIDE, SIDE))
        return padded, preact, parts

    def octant_block(block):
        unused_pad, unused_pre, parts = forward_block(block)
        return jnp.einsum('ok,bkv->bov', down_flat, parts.astype(jnp.float32)).astype(jnp.bfloat16)

    octants = lax.map(octant_block, block_ids).reshape(total, coarse_width, half_side ** 3)
    child_list = children.reshape(-1)
    picked = octants[jnp.clip(child_list, 0)]
    picked = jnp.where((child_list >= 0)[:, None, None], picked, jnp.zeros_like(picked))
    picked = picked.reshape(coarse_total, 2, 2, 2, coarse_width, half_side, half_side, half_side)
    coarse_features = picked.transpose(0, 4, 1, 5, 2, 6, 3, 7).reshape(coarse_total, coarse_width, SIDE ** 3)

    cot_parts = coarse_cot.reshape(coarse_total, coarse_width, 2, half_side, 2, half_side, 2, half_side)
    cot_parts = cot_parts.transpose(0, 2, 4, 6, 1, 3, 5, 7).reshape(coarse_total * 8, coarse_width, half_side ** 3)
    target = jnp.where(child_list >= 0, child_list, total).astype(jnp.int32)
    octant_grad = jnp.zeros((total, coarse_width, half_side ** 3), coarse_cot.dtype).at[target].set(cot_parts, mode="drop")

    def backward_block(carry, block):
        conv_sum, down_sum = carry
        padded, preact, parts = forward_block(block)
        start = (block * B0).astype(jnp.int32)
        grads_here = lax.dynamic_slice_in_dim(octant_grad, start, B0, 0).astype(jnp.float32)
        down_sum = down_sum + jnp.einsum('bov,bkv->ok', grads_here, parts.astype(jnp.float32))
        active_grad = from_octants(jnp.einsum('ok,bov->bkv', down_flat, grads_here), channels, SIDE)
        sigmoid_pre = jax.nn.sigmoid(preact)
        preact_grad = (active_grad * sigmoid_pre * (1.0 + preact * (1.0 - sigmoid_pre))).astype(jnp.bfloat16)
        conv_sum = conv_sum + tap_grads(padded, preact_grad)
        return (conv_sum, down_sum), preact_grad

    start_carry = (jnp.zeros((27, channels, channels), jnp.float32), jnp.zeros((coarse_width, 8 * channels), jnp.float32))
    (conv_grad, down_sum), grad_blocks = lax.scan(backward_block, start_carry, block_ids)
    grad_bricks = grad_blocks.reshape(total, channels, SIDE, SIDE, SIDE)
    grad_tables = face_sets(grad_bricks)
    flipped = conv_weight[::-1].transpose(0, 2, 1)

    def input_block(block):
        start = (block * B0).astype(jnp.int32)
        local = lax.dynamic_slice_in_dim(grad_bricks, start, B0, 0)
        near = lax.dynamic_slice_in_dim(neighbours, start, B0, 0)
        padded = assemble(local, make_lookup(grad_tables, near))
        return conv_taps(padded, flipped).astype(jnp.bfloat16)

    input_grad = lax.map(input_block, block_ids).reshape(total, channels, SIDE ** 3)
    down_grad = down_sum.reshape(coarse_width, 8, channels).transpose(1, 0, 2)
    return coarse_features, input_grad, conv_grad, down_grad
```

```python
import functools

import jax
import jax.numpy as jnp
from jax import lax
from jax.experimental import pallas as pl
from jax.experimental.pallas import tpu as pltpu
from jax.sharding import PartitionSpec as P

SIDE = 16
HALF = 8
LANES = 128
F32 = jnp.float32
BF16 = jnp.bfloat16
CONV_ROWS = 960
DOWN_ROWS = 512
SHARE = 8

VMEM_SPEC = pl.BlockSpec(memory_space=pltpu.VMEM)
SMEM_SPEC = pl.BlockSpec(memory_space=pltpu.SMEM)


def params(mib):
    return pltpu.CompilerParams(vmem_limit_bytes=mib * 1024 * 1024)


def low_half(shape):
    return lax.broadcasted_iota(jnp.int32, shape, len(shape) - 1) < 64


def swap_halves(x):
    return pltpu.roll(x, 64, x.ndim - 1)


def faces_kernel(x_ref, v_ref, low_ref, high_ref):
    def plane(i, carry):
        columns = pl.ds(pl.multiple_of(i * 256, 256), 256)
        turned = x_ref[:, columns].astype(F32).T.astype(BF16).reshape(SIDE, SIDE, LANES)
        v_ref[i] = turned
        low_ref[i] = turned[0]
        high_ref[i] = turned[SIDE - 1]
        return carry

    lax.fori_loop(0, SIDE, plane, 0)


def faces_call(x):
    face = jax.ShapeDtypeStruct((SIDE, SIDE, LANES), BF16)
    return pl.pallas_call(
        faces_kernel,
        out_shape=(jax.ShapeDtypeStruct((SIDE, SIDE, SIDE, LANES), BF16), face, face),
        in_specs=[VMEM_SPEC],
        out_specs=(VMEM_SPEC,) * 3,
        compiler_params=params(16),
        cost_estimate=pl.CostEstimate(flops=0, bytes_accessed=4_000_000, transcendentals=0),
        name="faces",
    )(x)


def find_octant(child_ref, wanted):
    place = jnp.int32(0)
    found = jnp.int32(0)
    for o in range(8):
        hit = (child_ref[0, o] == wanted).astype(jnp.int32)
        place = place + hit * o
        found = found + hit
    return place, found


def cot_kernel(child_ref, rank_ref, cot_ref, own_ref, send_ref, turned_ref):
    def plane(i, carry):
        columns = pl.ds(pl.multiple_of(i * 256, 256), 256)
        turned = cot_ref[:, columns].astype(F32).T
        turned_ref[i // HALF, i % HALF] = turned.reshape(2, HALF, 2, HALF, LANES)
        return carry

    lax.fori_loop(0, SIDE, plane, 0)
    rank = rank_ref[0]
    for out_ref, holder in ((own_ref, rank), (send_ref, rank ^ 1)):
        for slot in range(2):
            place, found = find_octant(child_ref, holder * 2 + slot)
            block = turned_ref[place // 4, :, place // 2 % 2, :, place % 2]
            block = jnp.where(found > 0, block, jnp.zeros_like(block))
            out_ref[slot] = block.reshape(512, LANES).astype(BF16)


def cot_call(children, rank, cot):
    blocks = jax.ShapeDtypeStruct((2, 512, LANES), BF16)
    return pl.pallas_call(
        cot_kernel,
        out_shape=(blocks, blocks),
        in_specs=[SMEM_SPEC, SMEM_SPEC, VMEM_SPEC],
        out_specs=(VMEM_SPEC,) * 2,
        scratch_shapes=[pltpu.VMEM((2, HALF, 2, HALF, 2, HALF, LANES), F32)],
        compiler_params=params(20),
        cost_estimate=pl.CostEstimate(flops=0, bytes_accessed=4_000_000, transcendentals=0),
        name="cot",
    )(children, rank, cot)


def coarse_kernel(child_ref, rank_ref, mine_ref, theirs_ref, out_ref, whole_ref):
    rank = rank_ref[0]
    for o in range(8):
        entry = child_ref[0, o]
        slot = jnp.maximum(entry, 0) % 2
        here = jnp.maximum(entry, 0) // 2 == rank
        mine = mine_ref[slot].astype(F32)
        theirs = theirs_ref[slot].astype(F32)
        block = jnp.where(here, mine, theirs)
        block = jnp.where(entry >= 0, block, jnp.zeros_like(block))
        whole_ref[o // 4, :, o // 2 % 2, :, o % 2] = block.reshape(HALF, HALF, HALF, LANES)

    def plane(i, carry):
        columns = pl.ds(pl.multiple_of(i * 256, 256), 256)
        turned = whole_ref[i // HALF, i % HALF].reshape(256, LANES).T
        out_ref[:, columns] = turned.astype(BF16)
        return carry

    lax.fori_loop(0, SIDE, plane, 0)


def coarse_call(children, rank, mine, theirs):
    return pl.pallas_call(
        coarse_kernel,
        out_shape=jax.ShapeDtypeStruct((LANES, SIDE**3), BF16),
        in_specs=[SMEM_SPEC, SMEM_SPEC, VMEM_SPEC, VMEM_SPEC],
        out_specs=VMEM_SPEC,
        scratch_shapes=[pltpu.VMEM((2, HALF, 2, HALF, 2, HALF, LANES), F32)],
        compiler_params=params(20),
        cost_estimate=pl.CostEstimate(flops=0, bytes_accessed=4_000_000, transcendentals=0),
        name="coarse",
    )(children, rank, mine, theirs)


def spans(step):
    if step == 0:
        return slice(1, SIDE + 1), slice(0, SIDE)
    if step == 1:
        return slice(SIDE + 1, SIDE + 2), slice(0, 1)
    return slice(0, 1), slice(SIDE - 1, SIDE)


def shifted(span):
    return slice(span.start + 1, span.stop + 1)


def assemble(near_ref, v_ref, before_ref, after_ref, face_ref, pad_ref):
    def clear(i, carry):
        pad_ref[i, :, 0:8] = jnp.zeros((SIDE + 2, 8, LANES), F32)
        pad_ref[i, :, 16:24] = jnp.zeros((SIDE + 2, 8, LANES), F32)
        return carry

    lax.fori_loop(0, SIDE + 2, clear, 0)

    def core(i, carry):
        pad_ref[i + 1, 1 : SIDE + 1, 1 : SIDE + 1] = v_ref[i].astype(F32)
        return carry

    lax.fori_loop(0, SIDE, core, 0)
    face_ref[0] = before_ref[...].astype(F32)
    face_ref[1] = after_ref[...].astype(F32)
    lower = low_half((1, LANES))
    column = 0
    for step_x in (-1, 0, 1):
        for step_y in (-1, 0, 1):
            for step_z in (-1, 0, 1):
                if step_x == 0 and step_y == 0 and step_z == 0:
                    continue
                first, second = near_ref[0, column], near_ref[1, column]
                column += 1
                straight = [
                    jnp.logical_and(e >= 0, jnp.maximum(e, 0) % 2 == n).astype(F32)
                    for n, e in enumerate((first, second))
                ]
                crossed = [
                    jnp.logical_and(e >= 0, jnp.maximum(e, 0) % 2 != n).astype(F32)
                    for n, e in enumerate((first, second))
                ]
                keep = jnp.where(lower, straight[0], straight[1])
                cross = jnp.where(lower, crossed[0], crossed[1])
                put_x, take_x = spans(step_x)
                put_y, take_y = spans(step_y)
                put_z, take_z = spans(step_z)

                def choose(x):
                    shape = (1,) * (x.ndim - 1) + (LANES,)
                    return x * keep.reshape(shape) + swap_halves(x) * cross.reshape(shape)

                if step_y != 0:
                    side = 0 if step_y < 0 else 1
                    pad_ref[put_x, put_y.start, put_z] = choose(face_ref[side, take_x, take_z])
                elif step_x != 0:
                    pad_ref[put_x.start, put_y, put_z] = choose(
                        pad_ref[take_x.start + 1, shifted(take_y), shifted(take_z)]
                    )
                else:

                    def line(i, carry):
                        pad_ref[i + 1, put_y, put_z] = choose(
                            pad_ref[i + 1, shifted(take_y), shifted(take_z)]
                        )
                        return carry

                    lax.fori_loop(0, SIDE, line, 0)


def gather_taps(pad_ref, a0_ref, a1_ref):
    lower = low_half((SIDE, LANES))

    def plane(i, carry):
        for j in range(SIDE + 2):
            for pair in range(2):
                near = pad_ref[i, j, 2 * pair : 2 * pair + SIDE]
                far = pad_ref[i, j, 2 * pair + 1 : 2 * pair + 1 + SIDE]
                lanes = slice(pair * LANES, (pair + 1) * LANES)
                a0_ref[i, j, :, lanes] = jnp.where(lower, near, swap_halves(far)).astype(BF16)
                a1_ref[i, j, :, lanes] = jnp.where(lower, swap_halves(near), far).astype(BF16)
        return carry

    lax.fori_loop(0, SIDE + 2, plane, 0)


def convolve(a_refs, w_ref, acc_ref, group=2):
    rows = group * 256

    def clear(i, carry):
        acc_ref[i] = jnp.zeros((256, LANES), F32)
        return carry

    lax.fori_loop(0, SIDE + 4, clear, 0)
    lower = low_half((256, LANES))

    def planes(g, carry):
        start = g * group
        results = []
        for n in range(2):
            total = None
            for b in range(3):
                lhs = a_refs[n][pl.ds(start, group), b : b + SIDE].reshape(rows, 256)
                part = jnp.dot(lhs, w_ref[n, b], preferred_element_type=F32)
                total = part if total is None else total + part
            results.append(total)
        zero, one = results
        for p in range(group):
            own = slice(p * 256, (p + 1) * 256)
            z, o = zero[own], one[own]
            acc_ref[start + p + 2] += jnp.where(lower, z[:, :LANES], o[:, :LANES])
            acc_ref[start + p + 1] += swap_halves(jnp.where(lower, o[:, :LANES], z[:, :LANES]))
            acc_ref[start + p] += z[:, LANES:] + o[:, LANES:]
        return carry

    lax.fori_loop(0, (SIDE + 2) // group, planes, 0)


def taps():
    return [(t, t // 4, t // 2 % 2, t % 2) for t in range(8)]


def middle_kernel(
    near_ref,
    v_ref,
    before_ref,
    after_ref,
    w_ref,
    down_ref,
    down_t_ref,
    own_ref,
    came_ref,
    oct_ref,
    g_ref,
    low_ref,
    high_ref,
    sums_ref,
    face_ref,
    pad_ref,
    a0_ref,
    a1_ref,
    acc_ref,
    fine_ref,
    act_ref,
    turned_ref,
    cg_ref,
):
    assemble(near_ref, v_ref, before_ref, after_ref, face_ref, pad_ref)
    gather_taps(pad_ref, a0_ref, a1_ref)
    convolve((a0_ref, a1_ref), w_ref, acc_ref)

    def activate(i, carry):
        preact = acc_ref[i + 2]
        gate = 1.0 / (1.0 + jnp.exp(-preact))
        fine_ref[i // 2, i % 2] = (preact * gate).reshape(HALF, 2, SIDE, LANES)
        acc_ref[i + 2] = gate * (1.0 + preact * (1.0 - gate))
        return carry

    lax.fori_loop(0, SIDE, activate, 0)
    for t, a, b, c in taps():
        picked = fine_ref[:, a, :, b, pl.ds(c, HALF, stride=2), :]
        act_ref[:, t * LANES : (t + 1) * LANES] = picked.reshape(512, LANES).astype(BF16)
    octants = jnp.dot(act_ref[...], down_ref[...], preferred_element_type=F32).astype(BF16)
    oct_ref[0] = octants[:, :LANES]
    oct_ref[1] = octants[:, LANES:]

    grads = [own_ref[n].astype(F32) + came_ref[n].astype(F32) for n in range(2)]
    lower = low_half((LANES, LANES))
    turned_grads = [grad.T.astype(BF16) for grad in grads]
    grads = jnp.concatenate([grad.astype(BF16) for grad in grads], axis=1)
    folded = []
    for t, a, b, c in taps():
        lanes = slice(t * LANES, (t + 1) * LANES)
        spread = jnp.dot(grads, down_t_ref[:, lanes], preferred_element_type=F32)
        fine_ref[:, a, :, b, pl.ds(c, HALF, stride=2), :] = spread.reshape(HALF, HALF, HALF, LANES)
        parts = [
            jnp.dot(turned, act_ref[:, lanes], preferred_element_type=F32)
            for turned in turned_grads
        ]
        both = jnp.where(lower, parts[0], parts[1])
        folded.append(both + swap_halves(both))
    for t in range(4):
        rows = slice(CONV_ROWS + t * LANES, CONV_ROWS + (t + 1) * LANES)
        sums_ref[rows] = jnp.where(lower, folded[t], folded[t + 4]).astype(BF16)

    for p in (0, 1, SIDE + 2, SIDE + 3):
        turned_ref[p] = jnp.zeros((LANES, 256), BF16)

    def back(i, carry):
        grad = fine_ref[i // 2, i % 2].reshape(256, LANES) * acc_ref[i + 2]
        turned_ref[i + 2] = grad.T.astype(BF16)
        rounded = grad.astype(BF16).reshape(SIDE, SIDE, LANES)
        g_ref[i] = rounded
        low_ref[i] = rounded[0]
        high_ref[i] = rounded[SIDE - 1]
        return carry

    lax.fori_loop(0, SIDE, back, 0)

    cg_ref[...] = jnp.zeros_like(cg_ref)

    def weigh(i, carry):
        lhs = [
            jnp.concatenate(
                [turned_ref[i + 2 - a, n * 64 : (n + 1) * 64] for a in range(3)], axis=0
            )
            for n in range(2)
        ]
        for b in range(3):
            total = cg_ref[b]
            for n, a_ref in enumerate((a0_ref, a1_ref)):
                rhs = a_ref[i, b : b + SIDE].reshape(256, 256)
                total += jnp.dot(lhs[n], rhs, preferred_element_type=F32)
            cg_ref[b] = total
        return carry

    lax.fori_loop(0, SIDE + 2, weigh, 0)
    lower = low_half((192, LANES))
    for b in range(3):
        sums_ref[b * 192 : (b + 1) * 192] = cg_ref[b, :, :LANES].astype(BF16)
    last = [cg_ref[b, :, LANES:] for b in range(3)]
    sums_ref[576:768] = jnp.where(lower, last[0], swap_halves(last[1])).astype(BF16)
    sums_ref[768:960] = jnp.where(lower, last[2], 0.0).astype(BF16)
    sums_ref[CONV_ROWS + DOWN_ROWS :] = jnp.zeros(
        (sums_ref.shape[0] - CONV_ROWS - DOWN_ROWS, LANES), BF16
    )


def tap_scratch():
    return [
        pltpu.VMEM((2, SIDE, SIDE, LANES), F32),
        pltpu.VMEM((SIDE + 2, SIDE + 2, 24, LANES), F32),
        pltpu.VMEM((SIDE + 2, SIDE + 2, SIDE, 256), BF16),
        pltpu.VMEM((SIDE + 2, SIDE + 2, SIDE, 256), BF16),
        pltpu.VMEM((SIDE + 4, 256, LANES), F32),
    ]


def middle_call(near, v, before, after, weights, down, down_t, own, came, rows):
    face = jax.ShapeDtypeStruct((SIDE, SIDE, LANES), BF16)
    return pl.pallas_call(
        middle_kernel,
        out_shape=(
            jax.ShapeDtypeStruct((2, 512, LANES), BF16),
            jax.ShapeDtypeStruct((SIDE, SIDE, SIDE, LANES), BF16),
            face,
            face,
            jax.ShapeDtypeStruct((rows, LANES), BF16),
        ),
        in_specs=[SMEM_SPEC] + [VMEM_SPEC] * 8,
        out_specs=(VMEM_SPEC,) * 5,
        scratch_shapes=tap_scratch()
        + [
            pltpu.VMEM((HALF, 2, HALF, 2, SIDE, LANES), F32),
            pltpu.VMEM((512, 8 * LANES), BF16),
            pltpu.VMEM((SIDE + 4, LANES, 256), BF16),
            pltpu.VMEM((3, 192, 256), F32),
        ],
        compiler_params=params(44),
        cost_estimate=pl.CostEstimate(
            flops=8_000_000_000, bytes_accessed=6_000_000, transcendentals=600_000
        ),
        name="middle",
    )(near, v, before, after, weights, down, down_t, own, came)


def input_kernel(
    near_ref,
    g_ref,
    before_ref,
    after_ref,
    w_ref,
    out_ref,
    face_ref,
    pad_ref,
    a0_ref,
    a1_ref,
    acc_ref,
):
    assemble(near_ref, g_ref, before_ref, after_ref, face_ref, pad_ref)
    gather_taps(pad_ref, a0_ref, a1_ref)
    convolve((a0_ref, a1_ref), w_ref, acc_ref)

    def plane(i, carry):
        columns = pl.ds(pl.multiple_of(i * 256, 256), 256)
        out_ref[:, columns] = acc_ref[i + 2].T.astype(BF16)
        return carry

    lax.fori_loop(0, SIDE, plane, 0)


def input_call(near, g, before, after, weights):
    return pl.pallas_call(
        input_kernel,
        out_shape=jax.ShapeDtypeStruct((LANES, SIDE**3), BF16),
        in_specs=[SMEM_SPEC] + [VMEM_SPEC] * 4,
        out_specs=VMEM_SPEC,
        scratch_shapes=tap_scratch(),
        compiler_params=params(32),
        cost_estimate=pl.CostEstimate(
            flops=4_000_000_000, bytes_accessed=3_000_000, transcendentals=0
        ),
        name="input_grad",
    )(near, g, before, after, weights)


def split_kernel(sums_ref, conv_ref, down_ref):
    for a in range(3):
        rows = slice(a * 64, (a + 1) * 64)
        for b in range(3):
            for c in range(3):
                chunk, upper = (b, c) if c < 2 else ((3, b) if b < 2 else (4, 0))
                base = chunk * 192
                block = sums_ref[base + rows.start : base + rows.stop].astype(F32)
                block = swap_halves(block) if upper else block
                conv_ref[9 * a + 3 * b + c] = block[:, :64]
    for t in range(4):
        block = sums_ref[CONV_ROWS + t * LANES : CONV_ROWS + (t + 1) * LANES].astype(F32)
        down_ref[t] = block[:, :64]
        down_ref[t + 4] = swap_halves(block)[:, :64]


def split_call(sums):
    return pl.pallas_call(
        split_kernel,
        out_shape=(
            jax.ShapeDtypeStruct((27, 64, 64), F32),
            jax.ShapeDtypeStruct((8, LANES, 64), F32),
        ),
        in_specs=[VMEM_SPEC],
        out_specs=(VMEM_SPEC,) * 2,
        compiler_params=params(16),
        name="split",
    )(sums)


def tap_weights(weights):
    shaped = weights.transpose(1, 2, 3, 0, 4)
    shaped = jnp.pad(shaped, ((0, 0), (0, 1), (0, 0), (0, 1), (0, 0)))
    first = shaped.reshape(3, 256, 256)
    second = shaped[:, :, :, jnp.array([1, 0, 3, 2])].reshape(3, 256, 256)
    return jnp.stack([first, second])


def both_ways(array, axis):
    peers = lax.axis_size(axis)
    up = [(i, i + 1) for i in range(peers - 1)]
    down = [(j, i) for i, j in up]
    low, high = array
    return lax.ppermute(high, axis, up), lax.ppermute(low, axis, down)


def from_partner(array, axis):
    return lax.ppermute(array, axis, [(i, i ^ 1) for i in range(lax.axis_size(axis))])


def total_sums(sums):
    axes = ("grp", "dev")
    peers = lax.axis_size("grp") * lax.axis_size("dev")
    shares = lax.all_to_all(sums.reshape(peers, SHARE, LANES), axes, 0, 0)
    mine = jnp.sum(shares.astype(F32), axis=0).astype(BF16)
    return lax.all_gather(mine, axes, axis=0, tiled=True)


def body(fine_input, conv_weight, down_weight, coarse_cot, neighbours, children):
    rank = lax.axis_index("grp") * lax.axis_size("dev") + lax.axis_index("dev")
    rank = rank.reshape(1).astype(jnp.int32)
    peers = lax.axis_size("grp") * lax.axis_size("dev")

    own, send = cot_call(children, rank, coarse_cot.reshape(LANES, SIDE**3))
    came = from_partner(send, "dev")
    voxels, low, high = faces_call(fine_input.reshape(LANES, SIDE**3))
    before, after = both_ways((low, high), "dev")

    taps_in = conv_weight.reshape(3, 3, 3, 64, 64)
    forward = tap_weights(taps_in.transpose(0, 1, 2, 4, 3))
    backward = tap_weights(taps_in[::-1, ::-1, ::-1])
    eye = jnp.eye(2, dtype=BF16)
    down_t = (
        down_weight.transpose(1, 0, 2)[None, :, :, None, :] * eye[:, None, None, :, None]
    ).reshape(256, 8 * LANES)
    down = down_t.T

    octants, grads, grad_low, grad_high, sums = middle_call(
        neighbours, voxels, before, after, forward, down, down_t, own, came, peers * SHARE
    )
    grad_before, grad_after = both_ways((grad_low, grad_high), "dev")
    theirs = from_partner(octants, "dev")
    gathered = total_sums(sums)
    coarse = coarse_call(children, rank, octants, theirs)
    input_grad = input_call(neighbours, grads, grad_before, grad_after, backward)
    conv_grad, down_grad = split_call(gathered)
    return (
        coarse.reshape(1, LANES, SIDE**3),
        input_grad.reshape(2, 64, SIDE**3),
        conv_grad,
        down_grad,
    )


def solution(mesh):
    in_specs = (
        P(("grp", "dev"), None, None),
        P(),
        P(),
        P(("grp", "dev"), None, None),
        P(("grp", "dev"), None),
        P(("grp", "dev"), None),
    )
    out_specs = (P(("grp", "dev"), None, None), P(("grp", "dev"), None, None), P(), P())
    return jax.shard_map(body, mesh=mesh, in_specs=in_specs, out_specs=out_specs, check_vma=False)
```

```python
import jax
import jax.numpy as jnp
from jax import lax
from jax.experimental import pallas as pl
from jax.experimental.pallas import tpu as pltpu
from jax.sharding import PartitionSpec as P

SIDE = 16
HALF = 8
LANES = 128
F32 = jnp.float32
BF16 = jnp.bfloat16
CONV_ROWS = 960
DOWN_ROWS = 512
SHARE = 8

VMEM_SPEC = pl.BlockSpec(memory_space=pltpu.VMEM)
SMEM_SPEC = pl.BlockSpec(memory_space=pltpu.SMEM)


def params(mib):
    return pltpu.CompilerParams(vmem_limit_bytes=mib * 1024 * 1024)


def low_half(shape):
    return lax.broadcasted_iota(jnp.int32, shape, len(shape) - 1) < 64


def swap_halves(x):
    return pltpu.roll(x, 64, x.ndim - 1)


def place_faces(rank_ref, i, planes, pair_ref, other_ref):
    even = rank_ref[0] % 2 == 0
    low, high = planes[0], planes[SIDE - 1]
    pair_ref[pl.ds(pl.multiple_of(1024 + i * SIDE, SIDE), SIDE)] = jnp.where(even, high, low)
    other_ref[pl.ds(pl.multiple_of(i * SIDE, SIDE), SIDE)] = jnp.where(even, low, high)


def find_octant(child_ref, wanted):
    place = jnp.int32(0)
    found = jnp.int32(0)
    for o in range(8):
        hit = (child_ref[0, o] == wanted).astype(jnp.int32)
        place = place + hit * o
        found = found + hit
    return place, found


def first_kernel(
    child_ref, rank_ref, cot_ref, x_ref, own_ref, v_ref, pair_ref, other_ref, turned_ref
):
    def plane(i, carry):
        columns = pl.ds(pl.multiple_of(i * 256, 256), 256)
        turned = cot_ref[:, columns].astype(F32).T
        turned_ref[i // HALF, i % HALF] = turned.reshape(2, HALF, 2, HALF, LANES)
        voxels = x_ref[:, columns].astype(F32).T.astype(BF16).reshape(SIDE, SIDE, LANES)
        v_ref[i] = voxels
        place_faces(rank_ref, i, voxels, pair_ref, other_ref)
        return carry

    lax.fori_loop(0, SIDE, plane, 0)
    rank = rank_ref[0]
    for out_ref, holder in ((own_ref, rank), (pair_ref, rank ^ 1)):
        for slot in range(2):
            place, found = find_octant(child_ref, holder * 2 + slot)
            block = turned_ref[place // 4, :, place // 2 % 2, :, place % 2]
            block = jnp.where(found > 0, block, jnp.zeros_like(block))
            out_ref[slot * 512 : (slot + 1) * 512] = block.reshape(512, LANES).astype(BF16)


def first_call(children, rank, cot, x):
    return pl.pallas_call(
        first_kernel,
        out_shape=(
            jax.ShapeDtypeStruct((1024, LANES), BF16),
            jax.ShapeDtypeStruct((SIDE, SIDE, SIDE, LANES), BF16),
            jax.ShapeDtypeStruct((1280, LANES), BF16),
            jax.ShapeDtypeStruct((256, LANES), BF16),
        ),
        in_specs=[SMEM_SPEC, SMEM_SPEC, VMEM_SPEC, VMEM_SPEC],
        out_specs=(VMEM_SPEC,) * 4,
        scratch_shapes=[pltpu.VMEM((2, HALF, 2, HALF, 2, HALF, LANES), F32)],
        compiler_params=params(20),
        cost_estimate=pl.CostEstimate(flops=0, bytes_accessed=8_000_000, transcendentals=0),
        name="first",
    )(children, rank, cot, x)


def weights_kernel(
    conv_ref, down_in_ref, forward_ref, backward_ref, down_ref, down_t_ref
):
    blank = jnp.zeros((64, 64), F32)
    for b in range(3):
        for c in range(4):
            rows = slice(b * 256 + c * 64, b * 256 + (c + 1) * 64)
            if c == 3:
                for n in range(2):
                    forward_ref[n, rows] = jnp.zeros((64, 256), BF16)
                    backward_ref[n, rows] = jnp.zeros((64, 256), BF16)
                continue
            ahead = [conv_ref[9 * a + 3 * b + c].astype(F32) for a in range(3)]
            behind = [conv_ref[26 - (9 * a + 3 * b + c)].astype(F32) for a in range(3)]
            for n in range(2):
                order = (0, 1, 2, None) if n == 0 else (1, 0, None, 2)
                for half in range(2):
                    pair = order[2 * half : 2 * half + 2]
                    lanes = slice(half * LANES, (half + 1) * LANES)
                    taps = [blank if a is None else ahead[a] for a in pair]
                    forward_ref[n, rows, lanes] = jnp.concatenate(taps, axis=0).T.astype(BF16)
                    taps = [blank if a is None else behind[a] for a in pair]
                    backward_ref[n, rows, lanes] = jnp.concatenate(taps, axis=1).astype(BF16)
    for t in range(8):
        tap = down_in_ref[t]
        blank = jnp.zeros((64, LANES), BF16)
        rows = [jnp.concatenate([tap, blank], axis=1), jnp.concatenate([blank, tap], axis=1)]
        block = jnp.concatenate(rows, axis=0)
        down_ref[t * LANES : (t + 1) * LANES] = block
        down_t_ref[:, t * LANES : (t + 1) * LANES] = block.astype(F32).T.astype(BF16)


def weights_call(conv_weight, down_weight):
    conv = jax.ShapeDtypeStruct((2, 768, 256), BF16)
    return pl.pallas_call(
        weights_kernel,
        out_shape=(
            conv,
            conv,
            jax.ShapeDtypeStruct((8 * LANES, 256), BF16),
            jax.ShapeDtypeStruct((256, 8 * LANES), BF16),
        ),
        in_specs=[VMEM_SPEC] * 2,
        out_specs=(VMEM_SPEC,) * 4,
        compiler_params=params(16),
        cost_estimate=pl.CostEstimate(flops=0, bytes_accessed=8_000_000, transcendentals=0),
        name="weights",
    )(conv_weight, down_weight)


def coarse_kernel(child_ref, rank_ref, mine_ref, theirs_ref, out_ref, whole_ref):
    rank = rank_ref[0]
    for o in range(8):
        entry = child_ref[0, o]
        slot = jnp.maximum(entry, 0) % 2
        here = jnp.maximum(entry, 0) // 2 == rank
        rows = pl.ds(pl.multiple_of(slot * 512, 512), 512)
        mine = mine_ref[rows].astype(F32)
        theirs = theirs_ref[rows].astype(F32)
        block = jnp.where(here, mine, theirs)
        block = jnp.where(entry >= 0, block, jnp.zeros_like(block))
        whole_ref[o // 4, :, o // 2 % 2, :, o % 2] = block.reshape(HALF, HALF, HALF, LANES)

    def plane(i, carry):
        columns = pl.ds(pl.multiple_of(i * 256, 256), 256)
        turned = whole_ref[i // HALF, i % HALF].reshape(256, LANES).T
        out_ref[:, columns] = turned.astype(BF16)
        return carry

    lax.fori_loop(0, SIDE, plane, 0)


def coarse_call(children, rank, mine, theirs):
    return pl.pallas_call(
        coarse_kernel,
        out_shape=jax.ShapeDtypeStruct((LANES, SIDE**3), BF16),
        in_specs=[SMEM_SPEC, SMEM_SPEC, VMEM_SPEC, VMEM_SPEC],
        out_specs=VMEM_SPEC,
        scratch_shapes=[pltpu.VMEM((2, HALF, 2, HALF, 2, HALF, LANES), F32)],
        compiler_params=params(20),
        cost_estimate=pl.CostEstimate(flops=0, bytes_accessed=4_000_000, transcendentals=0),
        name="coarse",
    )(children, rank, mine, theirs)


def spans(step):
    if step == 0:
        return slice(1, SIDE + 1), slice(0, SIDE)
    if step == 1:
        return slice(SIDE + 1, SIDE + 2), slice(0, 1)
    return slice(0, 1), slice(SIDE - 1, SIDE)


def shifted(span):
    return slice(span.start + 1, span.stop + 1)


def assemble(near_ref, rank_ref, v_ref, pair_ref, other_ref, face_ref, pad_ref):
    def core(i, carry):
        pad_ref[i, :, 16:24] = jnp.zeros((SIDE + 2, 8, LANES), F32)

        @pl.when(jnp.logical_and(i >= 1, i <= SIDE))
        def _():
            pad_ref[i, 1 : SIDE + 1, 1 : SIDE + 1] = v_ref[i - 1].astype(F32)

        return carry

    lax.fori_loop(0, SIDE + 2, core, 0)
    even = rank_ref[0] % 2 == 0
    pair = pair_ref[1024:1280].astype(F32).reshape(SIDE, SIDE, LANES)
    other = other_ref[...].astype(F32).reshape(SIDE, SIDE, LANES)
    face_ref[0] = jnp.where(even, other, pair)
    face_ref[1] = jnp.where(even, pair, other)
    lower = low_half((1, LANES))
    column = 0
    ends = []
    for step_x in (-1, 0, 1):
        for step_y in (-1, 0, 1):
            for step_z in (-1, 0, 1):
                if step_x == 0 and step_y == 0 and step_z == 0:
                    continue
                entries = near_ref[0, column], near_ref[1, column]
                column += 1
                straight = [
                    jnp.logical_and(e >= 0, jnp.maximum(e, 0) % 2 == n).astype(F32)
                    for n, e in enumerate(entries)
                ]
                crossed = [
                    jnp.logical_and(e >= 0, jnp.maximum(e, 0) % 2 != n).astype(F32)
                    for n, e in enumerate(entries)
                ]
                keep = jnp.where(lower, straight[0], straight[1])
                cross = jnp.where(lower, crossed[0], crossed[1])
                put_x, take_x = spans(step_x)
                put_y, take_y = spans(step_y)
                put_z, take_z = spans(step_z)

                def choose(x, keep=keep, cross=cross):
                    shape = (1,) * (x.ndim - 1) + (LANES,)
                    return x * keep.reshape(shape) + swap_halves(x) * cross.reshape(shape)

                if step_y != 0:
                    side = 0 if step_y < 0 else 1
                    pad_ref[put_x, put_y.start, put_z] = choose(face_ref[side, take_x, take_z])
                elif step_x != 0:
                    pad_ref[put_x.start, put_y, put_z] = choose(
                        pad_ref[take_x.start + 1, shifted(take_y), shifted(take_z)]
                    )
                else:
                    ends.append((choose, put_z, shifted(take_z)))

    def line(i, carry):
        for choose, put_z, take_z in ends:
            pad_ref[i + 1, 1 : SIDE + 1, put_z] = choose(pad_ref[i + 1, 1 : SIDE + 1, take_z])
        return carry

    lax.fori_loop(0, SIDE, line, 0)


def gather_taps(pad_ref, a0_ref, a1_ref):
    lower = low_half((SIDE, LANES))

    def plane(i, carry):
        for j in range(SIDE + 2):
            for pair in range(2):
                near = pad_ref[i, j, 2 * pair : 2 * pair + SIDE]
                far = pad_ref[i, j, 2 * pair + 1 : 2 * pair + 1 + SIDE]
                lanes = slice(pair * LANES, (pair + 1) * LANES)
                a0_ref[i, j, :, lanes] = jnp.where(lower, near, swap_halves(far)).astype(BF16)
                a1_ref[i, j, :, lanes] = jnp.where(lower, swap_halves(near), far).astype(BF16)
        return carry

    lax.fori_loop(0, SIDE + 2, plane, 0)


def convolve(a_refs, w_ref, acc_ref, group=3):
    rows = group * 256

    def clear(i, carry):
        acc_ref[i] = jnp.zeros((256, LANES), F32)
        return carry

    lax.fori_loop(0, SIDE + 4, clear, 0)
    lower = low_half((256, LANES))

    def planes(g, carry):
        start = g * group
        results = []
        for n in range(2):
            lhs = [
                a_refs[n][pl.ds(start, group), b : b + SIDE].reshape(rows, 256) for b in range(3)
            ]
            lhs = jnp.concatenate(lhs, axis=1)
            results.append(jnp.dot(lhs, w_ref[n], preferred_element_type=F32))
        zero, one = results
        for p in range(group):
            own = slice(p * 256, (p + 1) * 256)
            z, o = zero[own], one[own]
            acc_ref[start + p + 2] += jnp.where(lower, z[:, :LANES], o[:, :LANES])
            acc_ref[start + p + 1] += swap_halves(jnp.where(lower, o[:, :LANES], z[:, :LANES]))
            acc_ref[start + p] += z[:, LANES:] + o[:, LANES:]
        return carry

    lax.fori_loop(0, (SIDE + 2) // group, planes, 0)


def taps():
    return [(t, t // 4, t // 2 % 2, t % 2) for t in range(8)]


def middle_kernel(
    near_ref,
    rank_ref,
    v_ref,
    pair_ref,
    other_ref,
    w_ref,
    down_ref,
    down_t_ref,
    own_ref,
    pair_out_ref,
    other_out_ref,
    g_ref,
    a0_ref,
    a1_ref,
    act_ref,
    turned_ref,
    spun_ref,
    face_ref,
    pad_ref,
    acc_ref,
    fine_ref,
):
    assemble(near_ref, rank_ref, v_ref, pair_ref, other_ref, face_ref, pad_ref)
    gather_taps(pad_ref, a0_ref, a1_ref)
    convolve((a0_ref, a1_ref), w_ref, acc_ref)

    def activate(i, carry):
        preact = acc_ref[i + 2]
        gate = 1.0 / (1.0 + jnp.exp(-preact))
        fine_ref[i // 2, i % 2] = (preact * gate).reshape(HALF, 2, SIDE, LANES)
        acc_ref[i + 2] = gate * (1.0 + preact * (1.0 - gate))
        return carry

    lax.fori_loop(0, SIDE, activate, 0)
    for t, a, b, c in taps():
        picked = fine_ref[:, a, :, b, pl.ds(c, HALF, stride=2), :]
        act_ref[:, t * LANES : (t + 1) * LANES] = picked.reshape(512, LANES).astype(BF16)
    octants = jnp.dot(act_ref[...], down_ref[...], preferred_element_type=F32).astype(BF16)
    pair_out_ref[0:512] = octants[:, :LANES]
    pair_out_ref[512:1024] = octants[:, LANES:]

    grads = []
    for n in range(2):
        rows = slice(n * 512, (n + 1) * 512)
        grad = own_ref[rows].astype(F32) + pair_ref[rows].astype(F32)
        spun_ref[n] = grad.T.astype(BF16)
        grads.append(grad.astype(BF16))
    grads = jnp.concatenate(grads, axis=1)
    for pair in range(4):
        lanes = slice(pair * 256, (pair + 1) * 256)
        spread = jnp.dot(grads, down_t_ref[:, lanes], preferred_element_type=F32)
        for c in range(2):
            part = spread[:, c * LANES : (c + 1) * LANES].reshape(HALF, HALF, HALF, LANES)
            fine_ref[:, pair // 2, :, pair % 2, pl.ds(c, HALF, stride=2), :] = part

    for p in (0, 1, SIDE + 2, SIDE + 3):
        turned_ref[p] = jnp.zeros((LANES, 256), BF16)

    def back(i, carry):
        grad = fine_ref[i // 2, i % 2].reshape(256, LANES) * acc_ref[i + 2]
        turned_ref[i + 2] = grad.T.astype(BF16)
        rounded = grad.astype(BF16).reshape(SIDE, SIDE, LANES)
        g_ref[i] = rounded
        place_faces(rank_ref, i, rounded, pair_out_ref, other_out_ref)
        return carry

    lax.fori_loop(0, SIDE, back, 0)


def weigh_kernel(a0_ref, a1_ref, act_ref, turned_ref, spun_ref, sums_ref, cg_ref):
    lower = low_half((LANES, LANES))
    whole = [jnp.dot(spun_ref[n], act_ref[...], preferred_element_type=F32) for n in range(2)]
    folded = []
    for t in range(8):
        lanes = slice(t * LANES, (t + 1) * LANES)
        both = jnp.where(lower, whole[0][:, lanes], whole[1][:, lanes])
        folded.append(both + swap_halves(both))
    for t in range(4):
        rows = slice(CONV_ROWS + t * LANES, CONV_ROWS + (t + 1) * LANES)
        sums_ref[rows] = jnp.where(lower, folded[t], folded[t + 4]).astype(BF16)

    cg_ref[...] = jnp.zeros_like(cg_ref)

    def weigh(g, carry):
        lhs = []
        for i in (2 * g, 2 * g + 1):
            for n in range(2):
                own = slice(n * 64, (n + 1) * 64)
                lhs.append(
                    jnp.concatenate([turned_ref[i + 2 - a, own] for a in range(3)], axis=0)
                )
        lhs = jnp.concatenate(lhs, axis=1)
        for b in range(3):
            rhs = []
            for i in (2 * g, 2 * g + 1):
                for a_ref in (a0_ref, a1_ref):
                    rhs.append(a_ref[i, b : b + SIDE].reshape(256, 256))
            rhs = jnp.concatenate(rhs, axis=0)
            cg_ref[b] += jnp.dot(lhs, rhs, preferred_element_type=F32)
        return carry

    lax.fori_loop(0, SIDE // 2 + 1, weigh, 0)
    lower = low_half((192, LANES))
    for b in range(3):
        sums_ref[b * 192 : (b + 1) * 192] = cg_ref[b, :, :LANES].astype(BF16)
    last = [cg_ref[b, :, LANES:] for b in range(3)]
    sums_ref[576:768] = jnp.where(lower, last[0], swap_halves(last[1])).astype(BF16)
    sums_ref[768:960] = jnp.where(lower, last[2], 0.0).astype(BF16)
    sums_ref[CONV_ROWS + DOWN_ROWS :] = jnp.zeros(
        (sums_ref.shape[0] - CONV_ROWS - DOWN_ROWS, LANES), BF16
    )


TAPPED = (SIDE + 2, SIDE + 2, SIDE, 256)
PAD_SCRATCH = [
    pltpu.VMEM((2, SIDE, SIDE, LANES), F32),
    pltpu.VMEM((SIDE + 2, SIDE + 2, 24, LANES), F32),
    pltpu.VMEM((SIDE + 4, 256, LANES), F32),
]


def middle_call(near, rank, v, pair, other, weights, down, down_t, own):
    return pl.pallas_call(
        middle_kernel,
        out_shape=(
            jax.ShapeDtypeStruct((1280, LANES), BF16),
            jax.ShapeDtypeStruct((256, LANES), BF16),
            jax.ShapeDtypeStruct((SIDE, SIDE, SIDE, LANES), BF16),
            jax.ShapeDtypeStruct(TAPPED, BF16),
            jax.ShapeDtypeStruct(TAPPED, BF16),
            jax.ShapeDtypeStruct((512, 8 * LANES), BF16),
            jax.ShapeDtypeStruct((SIDE + 4, LANES, 256), BF16),
            jax.ShapeDtypeStruct((2, LANES, 512), BF16),
        ),
        in_specs=[SMEM_SPEC] * 2 + [VMEM_SPEC] * 7,
        out_specs=(VMEM_SPEC,) * 8,
        scratch_shapes=PAD_SCRATCH + [pltpu.VMEM((HALF, 2, HALF, 2, SIDE, LANES), F32)],
        compiler_params=params(32),
        cost_estimate=pl.CostEstimate(
            flops=4_000_000_000, bytes_accessed=16_000_000, transcendentals=600_000
        ),
        name="middle",
    )(near, rank, v, pair, other, weights, down, down_t, own)


def weigh_call(a0, a1, act, turned, spun, rows):
    return pl.pallas_call(
        weigh_kernel,
        out_shape=jax.ShapeDtypeStruct((rows, LANES), BF16),
        in_specs=[VMEM_SPEC] * 5,
        out_specs=VMEM_SPEC,
        scratch_shapes=[pltpu.VMEM((3, 192, 256), F32)],
        compiler_params=params(20),
        cost_estimate=pl.CostEstimate(
            flops=4_000_000_000, bytes_accessed=10_000_000, transcendentals=0
        ),
        name="weigh",
    )(a0, a1, act, turned, spun)


def input_kernel(
    near_ref,
    rank_ref,
    g_ref,
    pair_ref,
    other_ref,
    w_ref,
    out_ref,
    face_ref,
    pad_ref,
    acc_ref,
    a0_ref,
    a1_ref,
):
    assemble(near_ref, rank_ref, g_ref, pair_ref, other_ref, face_ref, pad_ref)
    gather_taps(pad_ref, a0_ref, a1_ref)
    convolve((a0_ref, a1_ref), w_ref, acc_ref)

    def plane(i, carry):
        columns = pl.ds(pl.multiple_of(i * 256, 256), 256)
        out_ref[:, columns] = acc_ref[i + 2].T.astype(BF16)
        return carry

    lax.fori_loop(0, SIDE, plane, 0)


def input_call(near, rank, g, pair, other, weights):
    return pl.pallas_call(
        input_kernel,
        out_shape=jax.ShapeDtypeStruct((LANES, SIDE**3), BF16),
        in_specs=[SMEM_SPEC] * 2 + [VMEM_SPEC] * 4,
        out_specs=VMEM_SPEC,
        scratch_shapes=PAD_SCRATCH + [pltpu.VMEM(TAPPED, BF16)] * 2,
        compiler_params=params(28),
        cost_estimate=pl.CostEstimate(
            flops=4_000_000_000, bytes_accessed=3_000_000, transcendentals=0
        ),
        name="input_grad",
    )(near, rank, g, pair, other, weights)


def add_kernel(shares_ref, out_ref):
    peers = shares_ref.shape[0]
    lanes = 16
    total = jnp.sum(shares_ref[0:lanes].astype(F32), axis=0)
    for start in range(lanes, peers, lanes):
        total = total + jnp.sum(shares_ref[start : start + lanes].astype(F32), axis=0)
    total = total.astype(BF16)
    for start in range(0, peers, lanes):
        out_ref[start : start + lanes] = jnp.broadcast_to(total[None], (lanes, SHARE, LANES))


def add_call(shares):
    return pl.pallas_call(
        add_kernel,
        out_shape=jax.ShapeDtypeStruct(shares.shape, BF16),
        in_specs=[VMEM_SPEC],
        out_specs=VMEM_SPEC,
        compiler_params=params(16),
        cost_estimate=pl.CostEstimate(flops=0, bytes_accessed=2_000_000, transcendentals=0),
        name="add",
    )(shares)


def split_kernel(sums_ref, conv_ref, down_ref):
    for a in range(3):
        for b in range(3):
            for c in range(3):
                chunk, upper = (b, c) if c < 2 else ((3, b) if b < 2 else (4, 0))
                base = chunk * 192 + a * 64
                block = sums_ref[base : base + 64].astype(F32)
                block = swap_halves(block) if upper else block
                conv_ref[9 * a + 3 * b + c] = block[:, :64]
    for t in range(4):
        block = sums_ref[CONV_ROWS + t * LANES : CONV_ROWS + (t + 1) * LANES].astype(F32).T
        down_ref[t] = block[:64]
        down_ref[t + 4] = block[64:]


def split_call(sums):
    return pl.pallas_call(
        split_kernel,
        out_shape=(
            jax.ShapeDtypeStruct((27, 64, 64), F32),
            jax.ShapeDtypeStruct((8, 64, LANES), F32),
        ),
        in_specs=[VMEM_SPEC],
        out_specs=(VMEM_SPEC,) * 2,
        compiler_params=params(16),
        name="split",
    )(sums)


def exchange(pair, other, axis):
    peers = lax.axis_size(axis)
    across = [(i, i + 1) for i in range(1, peers - 1, 2)]
    return (
        lax.ppermute(pair, axis, [(i, i ^ 1) for i in range(peers)]),
        lax.ppermute(other, axis, across + [(j, i) for i, j in across]),
    )


def total_sums(sums):
    axes = ("grp", "dev")
    peers = lax.axis_size("grp") * lax.axis_size("dev")
    shares = lax.all_to_all(sums.reshape(peers, SHARE, LANES), axes, 0, 0)
    return lax.all_to_all(add_call(shares), axes, 0, 0).reshape(peers * SHARE, LANES)


def body(fine_input, conv_weight, down_weight, coarse_cot, neighbours, children):
    rank = lax.axis_index("grp") * lax.axis_size("dev") + lax.axis_index("dev")
    rank = rank.reshape(1).astype(jnp.int32)
    peers = lax.axis_size("grp") * lax.axis_size("dev")

    own, voxels, pair, other = first_call(
        children, rank, coarse_cot.reshape(LANES, SIDE**3), fine_input.reshape(LANES, SIDE**3)
    )
    pair, other = exchange(pair, other, "dev")
    forward, backward, down, down_t = weights_call(conv_weight, down_weight.transpose(0, 2, 1))
    mine, other_out, grads, a0, a1, act, turned, spun = middle_call(
        neighbours, rank, voxels, pair, other, forward, down, down_t, own
    )
    theirs, grad_other = exchange(mine, other_out, "dev")
    sums = weigh_call(a0, a1, act, turned, spun, peers * SHARE)
    gathered = total_sums(sums)
    coarse = coarse_call(children, rank, mine, theirs)
    input_grad = input_call(neighbours, rank, grads, theirs, grad_other, backward)
    conv_grad, down_grad = split_call(gathered)
    return (
        coarse.reshape(1, LANES, SIDE**3),
        input_grad.reshape(2, 64, SIDE**3),
        conv_grad,
        down_grad.transpose(0, 2, 1),
    )


def solution(mesh):
    in_specs = (
        P(("grp", "dev"), None, None),
        P(),
        P(),
        P(("grp", "dev"), None, None),
        P(("grp", "dev"), None),
        P(("grp", "dev"), None),
    )
    out_specs = (P(("grp", "dev"), None, None), P(("grp", "dev"), None, None), P(), P())
    return jax.shard_map(body, mesh=mesh, in_specs=in_specs, out_specs=out_specs, check_vma=False)
```

```python
import functools

import jax
import jax.numpy as jnp
from jax import lax
from jax.experimental import pallas as pl
from jax.experimental.pallas import tpu as pltpu
from jax.sharding import PartitionSpec as P

SIDE = 16
HALF = 8
LANES = 128
F32 = jnp.float32
BF16 = jnp.bfloat16
CONV_ROWS = 960
DOWN_ROWS = 512
GROUPS = 8
SHARE = (CONV_ROWS + DOWN_ROWS) // GROUPS

VMEM_SPEC = pl.BlockSpec(memory_space=pltpu.VMEM)
SMEM_SPEC = pl.BlockSpec(memory_space=pltpu.SMEM)
ANY_SPEC = pl.BlockSpec(memory_space=pl.ANY)
TOKEN = jax.ShapeDtypeStruct((8, LANES), F32)


def params(mib):
    return pltpu.CompilerParams(vmem_limit_bytes=mib * 1024 * 1024)


def loop(count, body, unroll):
    def step(g, carry):
        for p in range(unroll):
            body(g * unroll + p)
        return carry

    lax.fori_loop(0, count // unroll, step, 0)


def low_half(shape):
    return lax.broadcasted_iota(jnp.int32, shape, len(shape) - 1) < 64


def swap_halves(x):
    return pltpu.roll(x, 64, x.ndim - 1)


def place_faces(info_ref, i, planes, pair_ref, other_ref, first=0):
    even = info_ref[0] % 2 == 0
    low, high = planes[0], planes[SIDE - 1]
    pair_ref[pl.ds(pl.multiple_of(first + i * SIDE, SIDE), SIDE)] = jnp.where(even, high, low)
    other_ref[pl.ds(pl.multiple_of(i * SIDE, SIDE), SIDE)] = jnp.where(even, low, high)


def faces_kernel(info_ref, x_ref, v_ref, pair_ref, other_ref, token_ref):
    def plane(i):
        columns = pl.ds(pl.multiple_of(i * 256, 256), 256)
        voxels = x_ref[:, columns].astype(F32).T.astype(BF16).reshape(SIDE, SIDE, LANES)
        v_ref[i] = voxels
        place_faces(info_ref, i, voxels, pair_ref, other_ref)

    loop(SIDE, plane, 4)
    token_ref[...] = jnp.zeros_like(token_ref)


def faces_call(info, x):
    face = jax.ShapeDtypeStruct((256, LANES), BF16)
    return pl.pallas_call(
        faces_kernel,
        out_shape=(jax.ShapeDtypeStruct((SIDE, SIDE, SIDE, LANES), BF16), face, face, TOKEN),
        in_specs=[SMEM_SPEC, VMEM_SPEC],
        out_specs=(VMEM_SPEC,) * 4,
        compiler_params=params(16),
        cost_estimate=pl.CostEstimate(flops=0, bytes_accessed=4_000_000, transcendentals=0),
        name="faces",
    )(info, x)


def find_octant(info_ref, wanted):
    place = jnp.int32(0)
    found = jnp.int32(0)
    for o in range(8):
        hit = (info_ref[2 + o] == wanted).astype(jnp.int32)
        place = place + hit * o
        found = found + hit
    return place, found


def cot_kernel(after_ref, info_ref, cot_ref, own_ref, send_ref, turned_ref):
    def plane(i):
        columns = pl.ds(pl.multiple_of(i * 256, 256), 256)
        turned = cot_ref[:, columns].astype(F32).T
        turned_ref[i // HALF, i % HALF] = turned.reshape(2, HALF, 2, HALF, LANES)

    loop(SIDE, plane, 4)
    rank = info_ref[0]
    for out_ref, holder in ((own_ref, rank), (send_ref, rank ^ 1)):
        for slot in range(2):
            place, found = find_octant(info_ref, holder * 2 + slot)
            block = turned_ref[place // 4, :, place // 2 % 2, :, place % 2]
            block = jnp.where(found > 0, block, jnp.zeros_like(block))
            out_ref[slot * 512 : (slot + 1) * 512] = block.reshape(512, LANES).astype(BF16)


def cot_call(after, info, cot):
    blocks = jax.ShapeDtypeStruct((1024, LANES), BF16)
    return pl.pallas_call(
        cot_kernel,
        out_shape=(blocks, blocks),
        in_specs=[ANY_SPEC, SMEM_SPEC, VMEM_SPEC],
        out_specs=(VMEM_SPEC,) * 2,
        scratch_shapes=[pltpu.VMEM((2, HALF, 2, HALF, 2, HALF, LANES), F32)],
        compiler_params=params(20),
        cost_estimate=pl.CostEstimate(flops=0, bytes_accessed=8_000_000, transcendentals=0),
        name="cot",
    )(after, info, cot)


def weights_kernel(
    conv_ref, down_in_ref, forward_ref, backward_ref, down_ref, down_t_ref
):
    blank = jnp.zeros((64, 64), F32)
    for b in range(3):
        for c in range(3):
            rows = slice(b * 256 + c * 64, b * 256 + (c + 1) * 64)
            ahead = [conv_ref[9 * a + 3 * b + c].astype(F32) for a in range(3)]
            behind = [conv_ref[26 - (9 * a + 3 * b + c)].astype(F32) for a in range(3)]
            for n in range(2):
                order = (0, 1, 2, None) if n == 0 else (1, 0, None, 2)
                if c == 2:
                    rows = slice(b * 256 + 128 + n * 64, b * 256 + 192 + n * 64)
                    unused = slice(b * 256 + 192 - n * 64, b * 256 + 256 - n * 64)
                    forward_ref[n, unused] = jnp.zeros((64, 256), BF16)
                    backward_ref[n, unused] = jnp.zeros((64, 256), BF16)
                for half in range(2):
                    pair = order[2 * half : 2 * half + 2]
                    lanes = slice(half * LANES, (half + 1) * LANES)
                    taps = [blank if a is None else ahead[a] for a in pair]
                    forward_ref[n, rows, lanes] = jnp.concatenate(taps, axis=0).T.astype(BF16)
                    taps = [blank if a is None else behind[a] for a in pair]
                    backward_ref[n, rows, lanes] = jnp.concatenate(taps, axis=1).astype(BF16)
    for t in range(8):
        tap = down_in_ref[t]
        blank = jnp.zeros((64, LANES), BF16)
        rows = [jnp.concatenate([tap, blank], axis=1), jnp.concatenate([blank, tap], axis=1)]
        block = jnp.concatenate(rows, axis=0)
        down_ref[t * LANES : (t + 1) * LANES] = block
        down_t_ref[:, t * LANES : (t + 1) * LANES] = block.astype(F32).T.astype(BF16)


def weights_call(conv_weight, down_weight):
    conv = jax.ShapeDtypeStruct((2, 768, 256), BF16)
    return pl.pallas_call(
        weights_kernel,
        out_shape=(
            conv,
            conv,
            jax.ShapeDtypeStruct((8 * LANES, 256), BF16),
            jax.ShapeDtypeStruct((256, 8 * LANES), BF16),
        ),
        in_specs=[VMEM_SPEC] * 2,
        out_specs=(VMEM_SPEC,) * 4,
        compiler_params=params(16),
        cost_estimate=pl.CostEstimate(flops=0, bytes_accessed=8_000_000, transcendentals=0),
        name="weights",
    )(conv_weight, down_weight)


def coarse_half_kernel(half, *refs):
    _, info_ref, mine_ref, theirs_ref = refs[:4]
    out_ref, token_ref, whole_ref = refs[-3:]
    token_ref[...] = jnp.zeros_like(token_ref)
    for o in range(4):
        entry = info_ref[2 + half * 4 + o]
        slot = jnp.maximum(entry, 0) % 2
        here = jnp.maximum(entry, 0) // 2 == info_ref[0]
        rows = pl.ds(pl.multiple_of(slot * 512, 512), 512)
        block = jnp.where(here, mine_ref[rows], theirs_ref[rows])
        block = jnp.where(entry >= 0, block, jnp.zeros_like(block)).astype(F32)
        whole_ref[:, o // 2, :, o % 2] = block.reshape(HALF, HALF, HALF, LANES)

    for i in range(HALF):
        turned = whole_ref[i].reshape(256, LANES).T
        out_ref[:, i * 256 : (i + 1) * 256] = turned.astype(BF16)


def coarse_half_call(after, info, mine, theirs, half, begun=()):
    return pl.pallas_call(
        functools.partial(coarse_half_kernel, half),
        grid=(1,),
        out_shape=(jax.ShapeDtypeStruct((LANES, SIDE**3), BF16), TOKEN),
        in_specs=[ANY_SPEC, SMEM_SPEC, VMEM_SPEC, VMEM_SPEC] + [ANY_SPEC] * len(begun),
        out_specs=(
            pl.BlockSpec((LANES, SIDE**3 // 2), lambda g: (0, half)),
            pl.BlockSpec((8, LANES), lambda g: (0, 0)),
        ),
        input_output_aliases={4: 0} if begun else {},
        scratch_shapes=[pltpu.VMEM((HALF, 2, HALF, 2, HALF, LANES), F32)],
        compiler_params=params(16),
        cost_estimate=pl.CostEstimate(flops=0, bytes_accessed=4_000_000, transcendentals=0),
        name="coarse_half",
    )(after, info, mine, theirs, *begun)


def spans(step):
    if step == 0:
        return slice(1, SIDE + 1), slice(0, SIDE)
    if step == 1:
        return slice(SIDE + 1, SIDE + 2), slice(0, 1)
    return slice(0, 1), slice(SIDE - 1, SIDE)


def assemble(info_ref, v_ref, pair_ref, other_ref, face_ref, core_ref, ends_ref):
    def fill(i):
        core_ref[i + 1, SIDE : 17 * SIDE] = v_ref[i].astype(F32).reshape(256, LANES)

    loop(SIDE, fill, 4)
    even = info_ref[0] % 2 == 0
    pair = pair_ref[pair_ref.shape[0] - 256 :].astype(F32).reshape(SIDE, SIDE, LANES)
    other = other_ref[...].astype(F32).reshape(SIDE, SIDE, LANES)
    face_ref[0] = jnp.where(even, other, pair)
    face_ref[1] = jnp.where(even, pair, other)
    lower = low_half((1, LANES))
    column = 0
    lines = []
    for step_x in (-1, 0, 1):
        for step_y in (-1, 0, 1):
            for step_z in (-1, 0, 1):
                if step_x == 0 and step_y == 0 and step_z == 0:
                    continue
                entries = info_ref[10 + column], info_ref[36 + column]
                column += 1
                straight = [
                    jnp.logical_and(e >= 0, jnp.maximum(e, 0) % 2 == n).astype(F32)
                    for n, e in enumerate(entries)
                ]
                crossed = [
                    jnp.logical_and(e >= 0, jnp.maximum(e, 0) % 2 != n).astype(F32)
                    for n, e in enumerate(entries)
                ]
                keep = jnp.where(lower, straight[0], straight[1])
                cross = jnp.where(lower, crossed[0], crossed[1])
                put_x, take_x = spans(step_x)

                def choose(x, keep=keep, cross=cross):
                    shape = (1,) * (x.ndim - 1) + (LANES,)
                    return x * keep.reshape(shape) + swap_halves(x) * cross.reshape(shape)

                end = 0 if step_z < 0 else 1
                row = SIDE - 1 if step_z < 0 else 0
                strided = pl.ds(SIDE + row, SIDE, stride=SIDE)
                if step_y != 0:
                    side = 0 if step_y < 0 else 1
                    y = 0 if step_y < 0 else SIDE + 1
                    if step_z == 0:
                        core_ref[put_x, y * SIDE : (y + 1) * SIDE] = choose(face_ref[side, take_x])
                    else:
                        ends_ref[end, put_x, y : y + 1] = choose(
                            face_ref[side, take_x, row : row + 1]
                        )
                elif step_x != 0:
                    taken = take_x.start + 1
                    if step_z == 0:
                        core_ref[put_x.start, SIDE : 17 * SIDE] = choose(
                            core_ref[taken, SIDE : 17 * SIDE]
                        )
                    else:
                        ends_ref[end, put_x.start, 1 : SIDE + 1] = choose(core_ref[taken, strided])
                else:
                    lines.append((choose, end, strided))

    def line(i):
        for choose, end, strided in lines:
            ends_ref[end, i + 1, 1 : SIDE + 1] = choose(core_ref[i + 1, strided])

    loop(SIDE, line, 4)


def gather_taps(core_ref, ends_ref, tap_refs):
    lower = low_half((SIDE, LANES))
    rows = lax.broadcasted_iota(jnp.int32, (8, LANES), 0)
    top, bottom = rows == 0, rows == 7

    def plane(i):
        for j in range(SIDE + 2):
            first = core_ref[i, j * SIDE : j * SIDE + 8]
            second = core_ref[i, j * SIDE + 8 : (j + 1) * SIDE]
            down_first, down_second = pltpu.roll(first, 1, 0), pltpu.roll(second, 1, 0)
            up_first, up_second = pltpu.roll(first, 7, 0), pltpu.roll(second, 7, 0)
            before = jnp.concatenate(
                [
                    jnp.where(top, ends_ref[0, i, j : j + 1], down_first),
                    jnp.where(top, down_first, down_second),
                ],
                axis=0,
            )
            after = jnp.concatenate(
                [
                    jnp.where(bottom, up_second, up_first),
                    jnp.where(bottom, ends_ref[1, i, j : j + 1], up_second),
                ],
                axis=0,
            )
            here = jnp.concatenate([first, second], axis=0)
            tap_refs[0][i, j] = jnp.where(lower, before, swap_halves(here)).astype(BF16)
            tap_refs[1][i, j] = jnp.where(lower, swap_halves(before), here).astype(BF16)
            tap_refs[2][i, j] = after.astype(BF16)

    loop(SIDE + 2, plane, 3)


def convolve(tap_refs, w_ref, acc_ref, first=0, planes=SIDE + 2, group=6):
    rows = group * 256

    def clear(i):
        acc_ref[i] = jnp.zeros((256, LANES), F32)

    loop(planes + 2, clear, 4)
    lower = low_half((256, LANES))

    def step(g, carry):
        start = g * group
        results = []
        for n in range(2):
            lhs = [
                tap_refs[chunk][pl.ds(first + start, group), b : b + SIDE].reshape(rows, LANES)
                for b in range(3)
                for chunk in (n, 2)
            ]
            lhs = jnp.concatenate(lhs, axis=1)
            results.append(jnp.dot(lhs, w_ref[n], preferred_element_type=F32))
        zero, one = results
        for p in range(group):
            own = slice(p * 256, (p + 1) * 256)
            z, o = zero[own], one[own]
            acc_ref[start + p + 2] += jnp.where(lower, z[:, :LANES], o[:, :LANES])
            acc_ref[start + p + 1] += swap_halves(jnp.where(lower, o[:, :LANES], z[:, :LANES]))
            acc_ref[start + p] += z[:, LANES:] + o[:, LANES:]
        return carry

    lax.fori_loop(0, planes // group, step, 0)


def taps():
    return [(t, t // 4, t // 2 % 2, t % 2) for t in range(8)]


def forward_kernel(
    info_ref,
    v_ref,
    pair_ref,
    other_ref,
    w_ref,
    down_ref,
    oct_ref,
    slope_ref,
    act_ref,
    zero_ref,
    one_ref,
    both_ref,
    face_ref,
    core_ref,
    ends_ref,
    acc_ref,
    fine_ref,
):
    tap_refs = (zero_ref, one_ref, both_ref)
    assemble(info_ref, v_ref, pair_ref, other_ref, face_ref, core_ref, ends_ref)
    gather_taps(core_ref, ends_ref, tap_refs)
    convolve(tap_refs, w_ref, acc_ref)

    def activate(i):
        preact = acc_ref[i + 2]
        gate = 1.0 / (1.0 + jnp.exp(-preact))
        fine_ref[i // 2, i % 2] = (preact * gate).reshape(HALF, 2, SIDE, LANES)
        slope_ref[i] = gate * (1.0 + preact * (1.0 - gate))

    loop(SIDE, activate, 4)
    for t, a, b, c in taps():
        picked = fine_ref[:, a, :, b, pl.ds(c, HALF, stride=2), :]
        act_ref[:, t * LANES : (t + 1) * LANES] = picked.reshape(512, LANES).astype(BF16)
    octants = jnp.dot(act_ref[...], down_ref[...], preferred_element_type=F32).astype(BF16)
    oct_ref[0:512] = octants[:, :LANES]
    oct_ref[512:1024] = octants[:, LANES:]


def back_kernel(
    info_ref,
    own_ref,
    came_ref,
    down_t_ref,
    slope_ref,
    oct_ref,
    pair_ref,
    other_ref,
    g_ref,
    turned_ref,
    spun_ref,
    fine_ref,
):
    pair_ref[0:1024] = oct_ref[...]
    grads = []
    for n in range(2):
        rows = slice(n * 512, (n + 1) * 512)
        grad = own_ref[rows].astype(F32) + came_ref[rows].astype(F32)
        spun_ref[n] = grad.T.astype(BF16)
        grads.append(grad.astype(BF16))
    grads = jnp.concatenate(grads, axis=1)
    for pair in range(4):
        lanes = slice(pair * 256, (pair + 1) * 256)
        spread = jnp.dot(grads, down_t_ref[:, lanes], preferred_element_type=F32)
        for c in range(2):
            part = spread[:, c * LANES : (c + 1) * LANES].reshape(HALF, HALF, HALF, LANES)
            fine_ref[:, pair // 2, :, pair % 2, pl.ds(c, HALF, stride=2), :] = part

    for p in (0, 1, SIDE + 2, SIDE + 3):
        turned_ref[p] = jnp.zeros((LANES, 256), BF16)

    def back(i):
        grad = fine_ref[i // 2, i % 2].reshape(256, LANES) * slope_ref[i]
        turned_ref[i + 2] = grad.T.astype(BF16)
        rounded = grad.astype(BF16).reshape(SIDE, SIDE, LANES)
        g_ref[i] = rounded
        place_faces(info_ref, i, rounded, pair_ref, other_ref, 1024)

    loop(SIDE, back, 4)


def weigh_kernel(info_ref, zero_ref, one_ref, both_ref, act_ref, turned_ref, spun_ref, *refs):
    kept_ref, sent_ref, token_ref, sums_ref, total_ref = refs
    token_ref[...] = jnp.zeros_like(token_ref)
    lower = low_half((LANES, LANES))
    whole = [jnp.dot(spun_ref[n], act_ref[...], preferred_element_type=F32) for n in range(2)]
    folded = []
    for t in range(8):
        lanes = slice(t * LANES, (t + 1) * LANES)
        both = jnp.where(lower, whole[0][:, lanes], whole[1][:, lanes])
        folded.append(both + swap_halves(both))
    for t in range(4):
        rows = slice(CONV_ROWS + t * LANES, CONV_ROWS + (t + 1) * LANES)
        sums_ref[rows] = jnp.where(lower, folded[t], folded[t + 4])

    total_ref[...] = jnp.zeros_like(total_ref)

    def weigh(g, carry):
        planes = [3 * g + p for p in range(3)]
        for n, brick_ref in enumerate((zero_ref, one_ref)):
            lhs = [
                jnp.concatenate(
                    [turned_ref[i + 2 - a, n * 64 : (n + 1) * 64] for a in range(3)], axis=0
                )
                for i in planes
            ]
            rhs = [
                jnp.concatenate(
                    [
                        ref[i, b : b + SIDE].reshape(256, LANES)
                        for ref in (brick_ref, both_ref)
                        for b in range(3)
                    ],
                    axis=1,
                )
                for i in planes
            ]
            total_ref[n] += jnp.dot(
                jnp.concatenate(lhs, axis=1),
                jnp.concatenate(rhs, axis=0),
                preferred_element_type=F32,
            )
        return carry

    lax.fori_loop(0, (SIDE + 2) // 3, weigh, 0)
    lower = low_half((192, LANES))
    last = []
    for b in range(3):
        lanes = slice(b * LANES, (b + 1) * LANES)
        sums_ref[b * 192 : (b + 1) * 192] = total_ref[0, :, lanes] + total_ref[1, :, lanes]
        lanes = slice((3 + b) * LANES, (4 + b) * LANES)
        both = jnp.where(lower, total_ref[0, :, lanes], total_ref[1, :, lanes])
        last.append(both + swap_halves(both))
    sums_ref[576:768] = jnp.where(lower, last[0], last[1])
    sums_ref[768:960] = jnp.where(lower, last[2], 0.0)
    core = info_ref[1] % 2
    for y in range(GROUPS // 2):
        kept_ref[y] = sums_ref[share_rows(2 * y + core)]
        sent_ref[y] = sums_ref[share_rows(2 * y + 1 - core)].astype(BF16)


def share_rows(group):
    return pl.ds(pl.multiple_of(group * SHARE, 8), SHARE)


TAPPED = (SIDE + 2, SIDE + 2, SIDE, LANES)
PAD_SCRATCH = [
    pltpu.VMEM((2, SIDE, SIDE, LANES), F32),
    pltpu.VMEM((SIDE + 2, 18 * SIDE, LANES), F32),
    pltpu.VMEM((2, SIDE + 2, 24, LANES), F32),
    pltpu.VMEM((SIDE + 4, 256, LANES), F32),
]
FINE_SCRATCH = pltpu.VMEM((HALF, 2, HALF, 2, SIDE, LANES), F32)


def forward_call(info, v, pair, other, weights, down):
    return pl.pallas_call(
        forward_kernel,
        out_shape=(
            jax.ShapeDtypeStruct((1024, LANES), BF16),
            jax.ShapeDtypeStruct((SIDE, 256, LANES), F32),
            jax.ShapeDtypeStruct((512, 8 * LANES), BF16),
        )
        + (jax.ShapeDtypeStruct(TAPPED, BF16),) * 3,
        in_specs=[SMEM_SPEC] + [VMEM_SPEC] * 5,
        out_specs=(VMEM_SPEC,) * 6,
        scratch_shapes=PAD_SCRATCH + [FINE_SCRATCH],
        compiler_params=params(28),
        cost_estimate=pl.CostEstimate(
            flops=4_000_000_000, bytes_accessed=16_000_000, transcendentals=600_000
        ),
        name="forward",
    )(info, v, pair, other, weights, down)


def back_call(info, own, came, down_t, slope, octants):
    return pl.pallas_call(
        back_kernel,
        out_shape=(
            jax.ShapeDtypeStruct((1280, LANES), BF16),
            jax.ShapeDtypeStruct((256, LANES), BF16),
            jax.ShapeDtypeStruct((SIDE, SIDE, SIDE, LANES), BF16),
            jax.ShapeDtypeStruct((SIDE + 4, LANES, 256), BF16),
            jax.ShapeDtypeStruct((2, LANES, 512), BF16),
        ),
        in_specs=[SMEM_SPEC] + [VMEM_SPEC] * 5,
        out_specs=(VMEM_SPEC,) * 5,
        scratch_shapes=[FINE_SCRATCH],
        compiler_params=params(24),
        cost_estimate=pl.CostEstimate(
            flops=300_000_000, bytes_accessed=8_000_000, transcendentals=0
        ),
        name="back",
    )(info, own, came, down_t, slope, octants)


def weigh_call(info, zero, one, both, act, turned, spun):
    return pl.pallas_call(
        weigh_kernel,
        out_shape=(
            jax.ShapeDtypeStruct((GROUPS // 2, SHARE, LANES), F32),
            jax.ShapeDtypeStruct((GROUPS // 2, SHARE, LANES), BF16),
            TOKEN,
        ),
        in_specs=[SMEM_SPEC] + [VMEM_SPEC] * 6,
        out_specs=(VMEM_SPEC,) * 3,
        scratch_shapes=[
            pltpu.VMEM((CONV_ROWS + DOWN_ROWS, LANES), F32),
            pltpu.VMEM((2, 192, 768), F32),
        ],
        compiler_params=params(20),
        cost_estimate=pl.CostEstimate(
            flops=4_000_000_000, bytes_accessed=10_000_000, transcendentals=0
        ),
        name="weigh",
    )(info, zero, one, both, act, turned, spun)


def input_taps_kernel(
    after_ref,
    info_ref,
    g_ref,
    pair_ref,
    other_ref,
    zero_ref,
    one_ref,
    both_ref,
    token_ref,
    face_ref,
    core_ref,
    ends_ref,
):
    assemble(info_ref, g_ref, pair_ref, other_ref, face_ref, core_ref, ends_ref)
    gather_taps(core_ref, ends_ref, (zero_ref, one_ref, both_ref))
    token_ref[...] = jnp.zeros_like(token_ref)


def input_taps_call(after, info, g, pair, other):
    return pl.pallas_call(
        input_taps_kernel,
        out_shape=(jax.ShapeDtypeStruct(TAPPED, BF16),) * 3 + (TOKEN,),
        in_specs=[ANY_SPEC, SMEM_SPEC] + [VMEM_SPEC] * 3,
        out_specs=(VMEM_SPEC,) * 4,
        scratch_shapes=PAD_SCRATCH[:3],
        compiler_params=params(20),
        cost_estimate=pl.CostEstimate(
            flops=2_000_000_000, bytes_accessed=8_000_000, transcendentals=0
        ),
        name="input_taps",
    )(after, info, g, pair, other)


def input_half_kernel(half, *refs):
    _, zero_ref, one_ref, both_ref, w_ref = refs[:5]
    out_ref, token_ref, acc_ref = refs[-3:]
    convolve((zero_ref, one_ref, both_ref), w_ref, acc_ref, half * HALF, HALF + 2, 5)

    for i in range(HALF):
        out_ref[:, i * 256 : (i + 1) * 256] = acc_ref[i + 2].T.astype(BF16)
    token_ref[...] = jnp.zeros_like(token_ref)


def input_half_call(after, taps, weights, half, begun=()):
    return pl.pallas_call(
        functools.partial(input_half_kernel, half),
        grid=(1,),
        out_shape=(jax.ShapeDtypeStruct((LANES, SIDE**3), BF16), TOKEN),
        in_specs=[ANY_SPEC] + [VMEM_SPEC] * 4 + [ANY_SPEC] * len(begun),
        out_specs=(
            pl.BlockSpec((LANES, SIDE**3 // 2), lambda g: (0, half)),
            pl.BlockSpec((8, LANES), lambda g: (0, 0)),
        ),
        input_output_aliases={5: 0} if begun else {},
        scratch_shapes=[pltpu.VMEM((HALF + 4, 256, LANES), F32)],
        compiler_params=params(16),
        cost_estimate=pl.CostEstimate(
            flops=2_500_000_000, bytes_accessed=6_000_000, transcendentals=0
        ),
        name="input_half",
    )(after, *taps, weights, *begun)


def deal_kernel(after_ref, info_ref, kept_ref, came_ref, own_ref, *refs):
    share_refs, total_ref = refs[:-1], refs[-1]
    total_ref[...] = kept_ref[...] + came_ref[...].astype(F32)
    y = info_ref[1] // 2
    own_ref[...] = total_ref[y]
    for s, share_ref in enumerate(share_refs):
        share_ref[...] = total_ref[y ^ (s + 1)].astype(BF16)


def deal_call(after, info, kept, came):
    return pl.pallas_call(
        deal_kernel,
        out_shape=(jax.ShapeDtypeStruct((SHARE, LANES), F32),)
        + (jax.ShapeDtypeStruct((SHARE, LANES), BF16),) * 3,
        in_specs=[ANY_SPEC, SMEM_SPEC, VMEM_SPEC, VMEM_SPEC],
        out_specs=(VMEM_SPEC,) * 4,
        scratch_shapes=[pltpu.VMEM((GROUPS // 2, SHARE, LANES), F32)],
        compiler_params=params(16),
        cost_estimate=pl.CostEstimate(flops=0, bytes_accessed=500_000, transcendentals=0),
        name="deal",
    )(after, info, kept, came)


def add_kernel(after_ref, *refs):
    parts = [ref[...].astype(F32) for ref in refs[:-1]]
    while len(parts) > 1:
        parts = [first + second for first, second in zip(parts[::2], parts[1::2])]
    refs[-1][...] = parts[0].astype(refs[-1].dtype)


def add_call(after, parts, dtype=BF16):
    return pl.pallas_call(
        add_kernel,
        out_shape=jax.ShapeDtypeStruct(parts[0].shape, dtype),
        in_specs=[ANY_SPEC] + [VMEM_SPEC] * len(parts),
        out_specs=VMEM_SPEC,
        compiler_params=params(16),
        cost_estimate=pl.CostEstimate(flops=0, bytes_accessed=500_000, transcendentals=0),
        name="add",
    )(after, *parts)


def collect_kernel(info_ref, *refs):
    y = info_ref[1] // 2
    for s, share_ref in enumerate(refs[:-1]):
        refs[-1][y ^ s] = share_ref[...]


def collect_call(info, shares):
    return pl.pallas_call(
        collect_kernel,
        out_shape=jax.ShapeDtypeStruct((GROUPS // 2, SHARE, LANES), BF16),
        in_specs=[SMEM_SPEC] + [VMEM_SPEC] * len(shares),
        out_specs=VMEM_SPEC,
        compiler_params=params(16),
        cost_estimate=pl.CostEstimate(flops=0, bytes_accessed=500_000, transcendentals=0),
        name="collect",
    )(info, *shares)


def split_kernel(after_ref, info_ref, mine_ref, theirs_ref, conv_ref, down_ref, sums_ref):
    core = info_ref[1] % 2
    for y in range(GROUPS // 2):
        sums_ref[share_rows(2 * y + core)] = mine_ref[y].astype(F32)
        sums_ref[share_rows(2 * y + 1 - core)] = theirs_ref[y].astype(F32)
    for a in range(3):
        for b in range(3):
            for c in range(3):
                chunk, upper = (b, c) if c < 2 else ((3, b) if b < 2 else (4, 0))
                base = chunk * 192 + a * 64
                block = sums_ref[base : base + 64]
                block = swap_halves(block) if upper else block
                conv_ref[9 * a + 3 * b + c] = block[:, :64]
    for t in range(4):
        block = sums_ref[CONV_ROWS + t * LANES : CONV_ROWS + (t + 1) * LANES].T
        down_ref[t] = block[:64]
        down_ref[t + 4] = block[64:]


def split_call(after, info, mine, theirs):
    return pl.pallas_call(
        split_kernel,
        out_shape=(
            jax.ShapeDtypeStruct((27, 64, 64), F32),
            jax.ShapeDtypeStruct((8, 64, LANES), F32),
        ),
        in_specs=[ANY_SPEC, SMEM_SPEC] + [VMEM_SPEC] * 2,
        out_specs=(VMEM_SPEC,) * 2,
        scratch_shapes=[pltpu.VMEM((CONV_ROWS + DOWN_ROWS, LANES), F32)],
        compiler_params=params(16),
        name="split",
    )(after, info, mine, theirs)


def swaps(axis, step=1):
    return [(i, i ^ step) for i in range(lax.axis_size(axis))]


def swapped(array, axis, steps):
    return [lax.ppermute(array, axis, swaps(axis, step)) for step in steps]


def exchange(pair, other, axis):
    peers = lax.axis_size(axis)
    across = [(i, (i + 1) % peers) for i in range(1, peers, 2)]
    return (
        lax.ppermute(pair, axis, swaps(axis)),
        lax.ppermute(other, axis, across + [(j, i) for i, j in across]),
    )


def body(fine_input, conv_weight, down_weight, coarse_cot, neighbours, children):
    rank = lax.axis_index("grp") * lax.axis_size("dev") + lax.axis_index("dev")
    info = [rank.reshape(1), lax.axis_index("grp").reshape(1), children.reshape(8)]
    info = jnp.concatenate([part.astype(jnp.int32) for part in info + [neighbours.reshape(52)]])

    voxels, pair, other, token = faces_call(info, fine_input.reshape(LANES, SIDE**3))
    own, send = cot_call(token, info, coarse_cot.reshape(LANES, SIDE**3))
    pair, other = exchange(pair, other, "dev")
    came = lax.ppermute(send, "dev", swaps("dev"))
    forward, backward, down, down_t = weights_call(conv_weight, down_weight.transpose(0, 2, 1))
    octants, slope, act, zero, one, both = forward_call(
        info, voxels, pair, other, forward, down
    )
    mine, other_out, grads, turned, spun = back_call(info, own, came, down_t, slope, octants)
    theirs, grad_other = exchange(mine, other_out, "dev")
    kept, sent, token = weigh_call(info, zero, one, both, act, turned, spun)

    (came,) = swapped(sent, "grp", (1,))
    coarse, token = coarse_half_call(token, info, mine, theirs, 0)
    own, *shares = deal_call(token, info, kept, came)
    came = [lax.ppermute(share, "grp", swaps("grp", 2 * s + 2)) for s, share in enumerate(shares)]
    *input_taps, token = input_taps_call(own, info, grads, theirs, grad_other)
    part = add_call(token, [own, *came], F32)
    came = swapped(part, "dev", (1, 2, 3))
    input_grad, token = input_half_call(part, input_taps, backward, 0)
    part = add_call(token, [part, *came])
    came = swapped(part, "dev", (4, 8, 12))
    input_grad, token = input_half_call(part, input_taps, backward, 1, (input_grad,))
    part = add_call(token, [part, *came])
    came = swapped(part, "dev", (16,))
    coarse, token = coarse_half_call(part, info, mine, theirs, 1, (coarse,))
    part = add_call(token, [part, *came])
    shares = collect_call(info, [part, *swapped(part, "grp", (2, 4, 6))])
    (came,) = swapped(shares, "grp", (1,))
    conv_grad, down_grad = split_call(token, info, shares, came)
    return (
        coarse.reshape(1, LANES, SIDE**3),
        input_grad.reshape(2, 64, SIDE**3),
        conv_grad,
        down_grad.transpose(0, 2, 1),
    )


def solution(mesh):
    in_specs = (
        P(("grp", "dev"), None, None),
        P(),
        P(),
        P(("grp", "dev"), None, None),
        P(("grp", "dev"), None),
        P(("grp", "dev"), None),
    )
    out_specs = (P(("grp", "dev"), None, None), P(("grp", "dev"), None, None), P(), P())
    return jax.shard_map(body, mesh=mesh, in_specs=in_specs, out_specs=out_specs, check_vma=False)
```

```python
import jax
import jax.numpy as jnp
from jax import lax
from jax.experimental import pallas as pl
from jax.experimental.pallas import tpu as pltpu
from jax.sharding import PartitionSpec as P

SIDE = 16
HALF = 8
LANES = 128
F32 = jnp.float32
BF16 = jnp.bfloat16
CONV_ROWS = 960
DOWN_ROWS = 512
SHARE = 96
PIECE = 8

VMEM_SPEC = pl.BlockSpec(memory_space=pltpu.VMEM)
SMEM_SPEC = pl.BlockSpec(memory_space=pltpu.SMEM)
ANY_SPEC = pl.BlockSpec(memory_space=pl.ANY)
TOKEN = jax.ShapeDtypeStruct((8, LANES), F32)


def params(mib):
    return pltpu.CompilerParams(vmem_limit_bytes=mib * 1024 * 1024)


def loop(count, body, unroll):
    def step(g, carry):
        for p in range(unroll):
            body(g * unroll + p)
        return carry

    lax.fori_loop(0, count // unroll, step, 0)


def low_half(shape):
    return lax.broadcasted_iota(jnp.int32, shape, len(shape) - 1) < 64


def swap_halves(x):
    return pltpu.roll(x, 64, x.ndim - 1)


def place_faces(rank_ref, i, planes, pair_ref, other_ref, first=0):
    even = rank_ref[0] % 2 == 0
    low, high = planes[0], planes[SIDE - 1]
    pair_ref[pl.ds(pl.multiple_of(first + i * SIDE, SIDE), SIDE)] = jnp.where(even, high, low)
    other_ref[pl.ds(pl.multiple_of(i * SIDE, SIDE), SIDE)] = jnp.where(even, low, high)


def faces_kernel(rank_ref, child_ref, near_ref, x_ref, v_ref, pair_ref, other_ref, token_ref):
    def plane(i):
        columns = pl.ds(pl.multiple_of(i * 256, 256), 256)
        voxels = x_ref[:, columns].astype(F32).T.astype(BF16).reshape(SIDE, SIDE, LANES)
        v_ref[i] = voxels
        place_faces(rank_ref, i, voxels, pair_ref, other_ref)

    loop(SIDE, plane, 4)
    token_ref[...] = jnp.zeros_like(token_ref)


def faces_call(rank, children, near, x):
    face = jax.ShapeDtypeStruct((256, LANES), BF16)
    return pl.pallas_call(
        faces_kernel,
        out_shape=(jax.ShapeDtypeStruct((SIDE, SIDE, SIDE, LANES), BF16), face, face, TOKEN),
        in_specs=[SMEM_SPEC] * 3 + [VMEM_SPEC],
        out_specs=(VMEM_SPEC,) * 4,
        compiler_params=params(16),
        cost_estimate=pl.CostEstimate(flops=0, bytes_accessed=4_000_000, transcendentals=0),
        name="faces",
    )(rank, children, near, x)


def find_octant(child_ref, wanted):
    place = jnp.int32(0)
    found = jnp.int32(0)
    for o in range(8):
        hit = (child_ref[0, o] == wanted).astype(jnp.int32)
        place = place + hit * o
        found = found + hit
    return place, found


def cot_kernel(after_ref, child_ref, rank_ref, cot_ref, own_ref, send_ref, turned_ref):
    def plane(i):
        columns = pl.ds(pl.multiple_of(i * 256, 256), 256)
        turned = cot_ref[:, columns].astype(F32).T
        turned_ref[i // HALF, i % HALF] = turned.reshape(2, HALF, 2, HALF, LANES)

    loop(SIDE, plane, 4)
    rank = rank_ref[0]
    for out_ref, holder in ((own_ref, rank), (send_ref, rank ^ 1)):
        for slot in range(2):
            place, found = find_octant(child_ref, holder * 2 + slot)
            block = turned_ref[place // 4, :, place // 2 % 2, :, place % 2]
            block = jnp.where(found > 0, block, jnp.zeros_like(block))
            out_ref[slot * 512 : (slot + 1) * 512] = block.reshape(512, LANES).astype(BF16)


def cot_call(after, children, rank, cot):
    blocks = jax.ShapeDtypeStruct((1024, LANES), BF16)
    return pl.pallas_call(
        cot_kernel,
        out_shape=(blocks, blocks),
        in_specs=[ANY_SPEC, SMEM_SPEC, SMEM_SPEC, VMEM_SPEC],
        out_specs=(VMEM_SPEC,) * 2,
        scratch_shapes=[pltpu.VMEM((2, HALF, 2, HALF, 2, HALF, LANES), F32)],
        compiler_params=params(20),
        cost_estimate=pl.CostEstimate(flops=0, bytes_accessed=8_000_000, transcendentals=0),
        name="cot",
    )(after, children, rank, cot)


def weights_kernel(
    conv_ref, down_in_ref, forward_ref, backward_ref, down_ref, down_t_ref
):
    blank = jnp.zeros((64, 64), F32)
    for b in range(3):
        for c in range(3):
            rows = slice(b * 256 + c * 64, b * 256 + (c + 1) * 64)
            ahead = [conv_ref[9 * a + 3 * b + c].astype(F32) for a in range(3)]
            behind = [conv_ref[26 - (9 * a + 3 * b + c)].astype(F32) for a in range(3)]
            for n in range(2):
                order = (0, 1, 2, None) if n == 0 else (1, 0, None, 2)
                if c == 2:
                    rows = slice(b * 256 + 128 + n * 64, b * 256 + 192 + n * 64)
                    unused = slice(b * 256 + 192 - n * 64, b * 256 + 256 - n * 64)
                    forward_ref[n, unused] = jnp.zeros((64, 256), BF16)
                    backward_ref[n, unused] = jnp.zeros((64, 256), BF16)
                for half in range(2):
                    pair = order[2 * half : 2 * half + 2]
                    lanes = slice(half * LANES, (half + 1) * LANES)
                    taps = [blank if a is None else ahead[a] for a in pair]
                    forward_ref[n, rows, lanes] = jnp.concatenate(taps, axis=0).T.astype(BF16)
                    taps = [blank if a is None else behind[a] for a in pair]
                    backward_ref[n, rows, lanes] = jnp.concatenate(taps, axis=1).astype(BF16)
    for t in range(8):
        tap = down_in_ref[t]
        blank = jnp.zeros((64, LANES), BF16)
        rows = [jnp.concatenate([tap, blank], axis=1), jnp.concatenate([blank, tap], axis=1)]
        block = jnp.concatenate(rows, axis=0)
        down_ref[t * LANES : (t + 1) * LANES] = block
        down_t_ref[:, t * LANES : (t + 1) * LANES] = block.astype(F32).T.astype(BF16)


def weights_call(conv_weight, down_weight):
    conv = jax.ShapeDtypeStruct((2, 768, 256), BF16)
    return pl.pallas_call(
        weights_kernel,
        out_shape=(
            conv,
            conv,
            jax.ShapeDtypeStruct((8 * LANES, 256), BF16),
            jax.ShapeDtypeStruct((256, 8 * LANES), BF16),
        ),
        in_specs=[VMEM_SPEC] * 2,
        out_specs=(VMEM_SPEC,) * 4,
        compiler_params=params(16),
        cost_estimate=pl.CostEstimate(flops=0, bytes_accessed=8_000_000, transcendentals=0),
        name="weights",
    )(conv_weight, down_weight)


def coarse_kernel(after_ref, child_ref, rank_ref, mine_ref, theirs_ref, out_ref, whole_ref):
    for o in range(8):
        entry = child_ref[0, o]
        slot = jnp.maximum(entry, 0) % 2
        here = jnp.maximum(entry, 0) // 2 == rank_ref[0]
        rows = pl.ds(pl.multiple_of(slot * 512, 512), 512)
        block = jnp.where(here, mine_ref[rows], theirs_ref[rows])
        block = jnp.where(entry >= 0, block, jnp.zeros_like(block)).astype(F32)
        whole_ref[o // 4, :, o // 2 % 2, :, o % 2] = block.reshape(HALF, HALF, HALF, LANES)

    def plane(i):
        columns = pl.ds(pl.multiple_of(i * 256, 256), 256)
        turned = whole_ref[i // HALF, i % HALF].reshape(256, LANES).T
        out_ref[:, columns] = turned.astype(BF16)

    loop(SIDE, plane, 4)


def coarse_call(after, children, rank, mine, theirs):
    return pl.pallas_call(
        coarse_kernel,
        out_shape=jax.ShapeDtypeStruct((LANES, SIDE**3), BF16),
        in_specs=[ANY_SPEC, SMEM_SPEC, SMEM_SPEC, VMEM_SPEC, VMEM_SPEC],
        out_specs=VMEM_SPEC,
        scratch_shapes=[pltpu.VMEM((2, HALF, 2, HALF, 2, HALF, LANES), F32)],
        compiler_params=params(20),
        cost_estimate=pl.CostEstimate(flops=0, bytes_accessed=4_000_000, transcendentals=0),
        name="coarse",
    )(after, children, rank, mine, theirs)


def spans(step):
    if step == 0:
        return slice(1, SIDE + 1), slice(0, SIDE)
    if step == 1:
        return slice(SIDE + 1, SIDE + 2), slice(0, 1)
    return slice(0, 1), slice(SIDE - 1, SIDE)


def assemble(near_ref, rank_ref, v_ref, pair_ref, other_ref, face_ref, core_ref, ends_ref):
    def fill(i):
        core_ref[i + 1, SIDE : 17 * SIDE] = v_ref[i].astype(F32).reshape(256, LANES)

    loop(SIDE, fill, 4)
    even = rank_ref[0] % 2 == 0
    pair = pair_ref[pair_ref.shape[0] - 256 :].astype(F32).reshape(SIDE, SIDE, LANES)
    other = other_ref[...].astype(F32).reshape(SIDE, SIDE, LANES)
    face_ref[0] = jnp.where(even, other, pair)
    face_ref[1] = jnp.where(even, pair, other)
    lower = low_half((1, LANES))
    column = 0
    lines = []
    for step_x in (-1, 0, 1):
        for step_y in (-1, 0, 1):
            for step_z in (-1, 0, 1):
                if step_x == 0 and step_y == 0 and step_z == 0:
                    continue
                entries = near_ref[0, column], near_ref[1, column]
                column += 1
                straight = [
                    jnp.logical_and(e >= 0, jnp.maximum(e, 0) % 2 == n).astype(F32)
                    for n, e in enumerate(entries)
                ]
                crossed = [
                    jnp.logical_and(e >= 0, jnp.maximum(e, 0) % 2 != n).astype(F32)
                    for n, e in enumerate(entries)
                ]
                keep = jnp.where(lower, straight[0], straight[1])
                cross = jnp.where(lower, crossed[0], crossed[1])
                put_x, take_x = spans(step_x)

                def choose(x, keep=keep, cross=cross):
                    shape = (1,) * (x.ndim - 1) + (LANES,)
                    return x * keep.reshape(shape) + swap_halves(x) * cross.reshape(shape)

                end = 0 if step_z < 0 else 1
                row = SIDE - 1 if step_z < 0 else 0
                strided = pl.ds(SIDE + row, SIDE, stride=SIDE)
                if step_y != 0:
                    side = 0 if step_y < 0 else 1
                    y = 0 if step_y < 0 else SIDE + 1
                    if step_z == 0:
                        core_ref[put_x, y * SIDE : (y + 1) * SIDE] = choose(face_ref[side, take_x])
                    else:
                        ends_ref[end, put_x, y : y + 1] = choose(
                            face_ref[side, take_x, row : row + 1]
                        )
                elif step_x != 0:
                    taken = take_x.start + 1
                    if step_z == 0:
                        core_ref[put_x.start, SIDE : 17 * SIDE] = choose(
                            core_ref[taken, SIDE : 17 * SIDE]
                        )
                    else:
                        ends_ref[end, put_x.start, 1 : SIDE + 1] = choose(core_ref[taken, strided])
                else:
                    lines.append((choose, end, strided))

    def line(i):
        for choose, end, strided in lines:
            ends_ref[end, i + 1, 1 : SIDE + 1] = choose(core_ref[i + 1, strided])

    loop(SIDE, line, 4)


def gather_taps(core_ref, ends_ref, tap_refs):
    lower = low_half((SIDE, LANES))
    rows = lax.broadcasted_iota(jnp.int32, (8, LANES), 0)
    top, bottom = rows == 0, rows == 7

    def plane(i):
        for j in range(SIDE + 2):
            first = core_ref[i, j * SIDE : j * SIDE + 8]
            second = core_ref[i, j * SIDE + 8 : (j + 1) * SIDE]
            down_first, down_second = pltpu.roll(first, 1, 0), pltpu.roll(second, 1, 0)
            up_first, up_second = pltpu.roll(first, 7, 0), pltpu.roll(second, 7, 0)
            before = jnp.concatenate(
                [
                    jnp.where(top, ends_ref[0, i, j : j + 1], down_first),
                    jnp.where(top, down_first, down_second),
                ],
                axis=0,
            )
            after = jnp.concatenate(
                [
                    jnp.where(bottom, up_second, up_first),
                    jnp.where(bottom, ends_ref[1, i, j : j + 1], up_second),
                ],
                axis=0,
            )
            here = jnp.concatenate([first, second], axis=0)
            tap_refs[0][i, j] = jnp.where(lower, before, swap_halves(here)).astype(BF16)
            tap_refs[1][i, j] = jnp.where(lower, swap_halves(before), here).astype(BF16)
            tap_refs[2][i, j] = after.astype(BF16)

    loop(SIDE + 2, plane, 3)


def convolve(tap_refs, w_ref, acc_ref, first=0, planes=SIDE + 2, group=6):
    rows = group * 256

    def clear(i):
        acc_ref[i] = jnp.zeros((256, LANES), F32)

    loop(planes + 2, clear, 4)
    lower = low_half((256, LANES))

    def step(g, carry):
        start = g * group
        results = []
        for n in range(2):
            lhs = [
                tap_refs[chunk][pl.ds(first + start, group), b : b + SIDE].reshape(rows, LANES)
                for b in range(3)
                for chunk in (n, 2)
            ]
            lhs = jnp.concatenate(lhs, axis=1)
            results.append(jnp.dot(lhs, w_ref[n], preferred_element_type=F32))
        zero, one = results
        for p in range(group):
            own = slice(p * 256, (p + 1) * 256)
            z, o = zero[own], one[own]
            acc_ref[start + p + 2] += jnp.where(lower, z[:, :LANES], o[:, :LANES])
            acc_ref[start + p + 1] += swap_halves(jnp.where(lower, o[:, :LANES], z[:, :LANES]))
            acc_ref[start + p] += z[:, LANES:] + o[:, LANES:]
        return carry

    lax.fori_loop(0, planes // group, step, 0)


def taps():
    return [(t, t // 4, t // 2 % 2, t % 2) for t in range(8)]


def forward_kernel(
    near_ref,
    rank_ref,
    v_ref,
    pair_ref,
    other_ref,
    w_ref,
    down_ref,
    oct_ref,
    slope_ref,
    act_ref,
    zero_ref,
    one_ref,
    both_ref,
    face_ref,
    core_ref,
    ends_ref,
    acc_ref,
    fine_ref,
):
    tap_refs = (zero_ref, one_ref, both_ref)
    assemble(near_ref, rank_ref, v_ref, pair_ref, other_ref, face_ref, core_ref, ends_ref)
    gather_taps(core_ref, ends_ref, tap_refs)
    convolve(tap_refs, w_ref, acc_ref)

    def activate(i):
        preact = acc_ref[i + 2]
        gate = 1.0 / (1.0 + jnp.exp(-preact))
        fine_ref[i // 2, i % 2] = (preact * gate).reshape(HALF, 2, SIDE, LANES)
        slope_ref[i] = gate * (1.0 + preact * (1.0 - gate))

    loop(SIDE, activate, 4)
    for t, a, b, c in taps():
        picked = fine_ref[:, a, :, b, pl.ds(c, HALF, stride=2), :]
        act_ref[:, t * LANES : (t + 1) * LANES] = picked.reshape(512, LANES).astype(BF16)
    octants = jnp.dot(act_ref[...], down_ref[...], preferred_element_type=F32).astype(BF16)
    oct_ref[0:512] = octants[:, :LANES]
    oct_ref[512:1024] = octants[:, LANES:]


def back_kernel(
    rank_ref,
    own_ref,
    came_ref,
    down_t_ref,
    slope_ref,
    oct_ref,
    pair_ref,
    other_ref,
    g_ref,
    turned_ref,
    spun_ref,
    fine_ref,
):
    pair_ref[0:1024] = oct_ref[...]
    grads = []
    for n in range(2):
        rows = slice(n * 512, (n + 1) * 512)
        grad = own_ref[rows].astype(F32) + came_ref[rows].astype(F32)
        spun_ref[n] = grad.T.astype(BF16)
        grads.append(grad.astype(BF16))
    grads = jnp.concatenate(grads, axis=1)
    for pair in range(4):
        lanes = slice(pair * 256, (pair + 1) * 256)
        spread = jnp.dot(grads, down_t_ref[:, lanes], preferred_element_type=F32)
        for c in range(2):
            part = spread[:, c * LANES : (c + 1) * LANES].reshape(HALF, HALF, HALF, LANES)
            fine_ref[:, pair // 2, :, pair % 2, pl.ds(c, HALF, stride=2), :] = part

    for p in (0, 1, SIDE + 2, SIDE + 3):
        turned_ref[p] = jnp.zeros((LANES, 256), BF16)

    def back(i):
        grad = fine_ref[i // 2, i % 2].reshape(256, LANES) * slope_ref[i]
        turned_ref[i + 2] = grad.T.astype(BF16)
        rounded = grad.astype(BF16).reshape(SIDE, SIDE, LANES)
        g_ref[i] = rounded
        place_faces(rank_ref, i, rounded, pair_ref, other_ref, 1024)

    loop(SIDE, back, 4)


def weigh_kernel(
    zero_ref, one_ref, both_ref, act_ref, turned_ref, spun_ref, sums_ref, total_ref
):
    lower = low_half((LANES, LANES))
    whole = [jnp.dot(spun_ref[n], act_ref[...], preferred_element_type=F32) for n in range(2)]
    folded = []
    for t in range(8):
        lanes = slice(t * LANES, (t + 1) * LANES)
        both = jnp.where(lower, whole[0][:, lanes], whole[1][:, lanes])
        folded.append(both + swap_halves(both))
    for t in range(4):
        rows = slice(CONV_ROWS + t * LANES, CONV_ROWS + (t + 1) * LANES)
        sums_ref[rows] = jnp.where(lower, folded[t], folded[t + 4]).astype(BF16)

    total_ref[...] = jnp.zeros_like(total_ref)

    def weigh(g, carry):
        planes = [3 * g + p for p in range(3)]
        for n, brick_ref in enumerate((zero_ref, one_ref)):
            lhs = [
                jnp.concatenate(
                    [turned_ref[i + 2 - a, n * 64 : (n + 1) * 64] for a in range(3)], axis=0
                )
                for i in planes
            ]
            rhs = [
                jnp.concatenate(
                    [
                        ref[i, b : b + SIDE].reshape(256, LANES)
                        for ref in (brick_ref, both_ref)
                        for b in range(3)
                    ],
                    axis=1,
                )
                for i in planes
            ]
            total_ref[n] += jnp.dot(
                jnp.concatenate(lhs, axis=1),
                jnp.concatenate(rhs, axis=0),
                preferred_element_type=F32,
            )
        return carry

    lax.fori_loop(0, (SIDE + 2) // 3, weigh, 0)
    lower = low_half((192, LANES))
    last = []
    for b in range(3):
        lanes = slice(b * LANES, (b + 1) * LANES)
        sums_ref[b * 192 : (b + 1) * 192] = (total_ref[0, :, lanes] + total_ref[1, :, lanes]).astype(
            BF16
        )
        lanes = slice((3 + b) * LANES, (4 + b) * LANES)
        both = jnp.where(lower, total_ref[0, :, lanes], total_ref[1, :, lanes])
        last.append(both + swap_halves(both))
    sums_ref[576:768] = jnp.where(lower, last[0], last[1]).astype(BF16)
    sums_ref[768:960] = jnp.where(lower, last[2], 0.0).astype(BF16)
    sums_ref[CONV_ROWS + DOWN_ROWS :] = jnp.zeros(
        (sums_ref.shape[0] - CONV_ROWS - DOWN_ROWS, LANES), BF16
    )


TAPPED = (SIDE + 2, SIDE + 2, SIDE, LANES)
PAD_SCRATCH = [
    pltpu.VMEM((2, SIDE, SIDE, LANES), F32),
    pltpu.VMEM((SIDE + 2, 18 * SIDE, LANES), F32),
    pltpu.VMEM((2, SIDE + 2, 24, LANES), F32),
    pltpu.VMEM((SIDE + 4, 256, LANES), F32),
]
FINE_SCRATCH = pltpu.VMEM((HALF, 2, HALF, 2, SIDE, LANES), F32)


def forward_call(near, rank, v, pair, other, weights, down):
    return pl.pallas_call(
        forward_kernel,
        out_shape=(
            jax.ShapeDtypeStruct((1024, LANES), BF16),
            jax.ShapeDtypeStruct((SIDE, 256, LANES), F32),
            jax.ShapeDtypeStruct((512, 8 * LANES), BF16),
        )
        + (jax.ShapeDtypeStruct(TAPPED, BF16),) * 3,
        in_specs=[SMEM_SPEC] * 2 + [VMEM_SPEC] * 5,
        out_specs=(VMEM_SPEC,) * 6,
        scratch_shapes=PAD_SCRATCH + [FINE_SCRATCH],
        compiler_params=params(28),
        cost_estimate=pl.CostEstimate(
            flops=4_000_000_000, bytes_accessed=16_000_000, transcendentals=600_000
        ),
        name="forward",
    )(near, rank, v, pair, other, weights, down)


def back_call(rank, own, came, down_t, slope, octants):
    return pl.pallas_call(
        back_kernel,
        out_shape=(
            jax.ShapeDtypeStruct((1280, LANES), BF16),
            jax.ShapeDtypeStruct((256, LANES), BF16),
            jax.ShapeDtypeStruct((SIDE, SIDE, SIDE, LANES), BF16),
            jax.ShapeDtypeStruct((SIDE + 4, LANES, 256), BF16),
            jax.ShapeDtypeStruct((2, LANES, 512), BF16),
        ),
        in_specs=[SMEM_SPEC] + [VMEM_SPEC] * 5,
        out_specs=(VMEM_SPEC,) * 5,
        scratch_shapes=[FINE_SCRATCH],
        compiler_params=params(24),
        cost_estimate=pl.CostEstimate(
            flops=300_000_000, bytes_accessed=8_000_000, transcendentals=0
        ),
        name="back",
    )(rank, own, came, down_t, slope, octants)


def weigh_call(zero, one, both, act, turned, spun, rows):
    return pl.pallas_call(
        weigh_kernel,
        out_shape=jax.ShapeDtypeStruct((rows, LANES), BF16),
        in_specs=[VMEM_SPEC] * 6,
        out_specs=VMEM_SPEC,
        scratch_shapes=[pltpu.VMEM((2, 192, 768), F32)],
        compiler_params=params(20),
        cost_estimate=pl.CostEstimate(
            flops=4_000_000_000, bytes_accessed=10_000_000, transcendentals=0
        ),
        name="weigh",
    )(zero, one, both, act, turned, spun)


def input_kernel(
    after_ref,
    near_ref,
    rank_ref,
    g_ref,
    pair_ref,
    other_ref,
    w_ref,
    out_ref,
    token_ref,
    face_ref,
    core_ref,
    ends_ref,
    acc_ref,
    *tap_refs,
):
    assemble(near_ref, rank_ref, g_ref, pair_ref, other_ref, face_ref, core_ref, ends_ref)
    gather_taps(core_ref, ends_ref, tap_refs)
    convolve(tap_refs, w_ref, acc_ref)

    def plane(i):
        columns = pl.ds(pl.multiple_of(i * 256, 256), 256)
        out_ref[:, columns] = acc_ref[i + 2].T.astype(BF16)

    loop(SIDE, plane, 4)
    token_ref[...] = jnp.zeros_like(token_ref)


def input_call(after, near, rank, g, pair, other, weights):
    return pl.pallas_call(
        input_kernel,
        out_shape=(jax.ShapeDtypeStruct((LANES, SIDE**3), BF16), TOKEN),
        in_specs=[ANY_SPEC] + [SMEM_SPEC] * 2 + [VMEM_SPEC] * 4,
        out_specs=(VMEM_SPEC,) * 2,
        scratch_shapes=PAD_SCRATCH + [pltpu.VMEM(TAPPED, BF16)] * 3,
        compiler_params=params(28),
        cost_estimate=pl.CostEstimate(
            flops=4_000_000_000, bytes_accessed=3_000_000, transcendentals=0
        ),
        name="input_grad",
    )(after, near, rank, g, pair, other, weights)


def add_shares_kernel(after_ref, shares_ref, out_ref, token_ref):
    total = shares_ref[0].astype(F32)
    for peer in range(1, shares_ref.shape[0]):
        total = total + shares_ref[peer].astype(F32)
    out_ref[0:SHARE] = total
    out_ref[SHARE:] = jnp.zeros((out_ref.shape[0] - SHARE, LANES), F32)
    token_ref[...] = jnp.zeros_like(token_ref)


def add_shares_call(after, shares, rows):
    return pl.pallas_call(
        add_shares_kernel,
        out_shape=(jax.ShapeDtypeStruct((rows, LANES), F32), TOKEN),
        in_specs=[ANY_SPEC, VMEM_SPEC],
        out_specs=(VMEM_SPEC,) * 2,
        compiler_params=params(16),
        cost_estimate=pl.CostEstimate(flops=0, bytes_accessed=500_000, transcendentals=0),
        name="add_shares",
    )(after, shares)


def add_pieces_kernel(after_ref, pieces_ref, out_ref, token_ref):
    total = jnp.sum(pieces_ref[...], axis=0).astype(BF16)
    out_ref[...] = jnp.broadcast_to(total[None], out_ref.shape)
    token_ref[...] = jnp.zeros_like(token_ref)


def add_pieces_call(after, pieces):
    return pl.pallas_call(
        add_pieces_kernel,
        out_shape=(jax.ShapeDtypeStruct(pieces.shape, BF16), TOKEN),
        in_specs=[ANY_SPEC, VMEM_SPEC],
        out_specs=(VMEM_SPEC,) * 2,
        compiler_params=params(16),
        cost_estimate=pl.CostEstimate(flops=0, bytes_accessed=500_000, transcendentals=0),
        name="add_pieces",
    )(after, pieces)


def spread_kernel(after_ref, rows_ref, out_ref, token_ref):
    kept = rows_ref[0:SHARE]
    for peer in range(out_ref.shape[0]):
        out_ref[peer] = kept
    token_ref[...] = jnp.zeros_like(token_ref)


def spread_call(after, rows, peers):
    return pl.pallas_call(
        spread_kernel,
        out_shape=(jax.ShapeDtypeStruct((peers, SHARE, LANES), BF16), TOKEN),
        in_specs=[ANY_SPEC, VMEM_SPEC],
        out_specs=(VMEM_SPEC,) * 2,
        compiler_params=params(16),
        cost_estimate=pl.CostEstimate(flops=0, bytes_accessed=500_000, transcendentals=0),
        name="spread",
    )(after, rows)


def pass_kernel(token_ref, out_ref):
    out_ref[...] = token_ref[...]


def pass_call(token):
    return pl.pallas_call(
        pass_kernel,
        out_shape=TOKEN,
        in_specs=[VMEM_SPEC],
        out_specs=VMEM_SPEC,
        compiler_params=params(16),
        name="pass",
    )(token)


def stamp_kernel(sums_ref, pair_ref, other_ref, out_ref):
    pass


def stamp_call(sums, pair, other):
    return pl.pallas_call(
        stamp_kernel,
        out_shape=jax.ShapeDtypeStruct(sums.shape, sums.dtype),
        in_specs=[ANY_SPEC] * 3,
        out_specs=ANY_SPEC,
        input_output_aliases={0: 0},
        compiler_params=params(16),
        name="stamp",
    )(sums, pair, other)


def split_kernel(sums_ref, conv_ref, down_ref):
    for a in range(3):
        for b in range(3):
            for c in range(3):
                chunk, upper = (b, c) if c < 2 else ((3, b) if b < 2 else (4, 0))
                base = chunk * 192 + a * 64
                block = sums_ref[base : base + 64].astype(F32)
                block = swap_halves(block) if upper else block
                conv_ref[9 * a + 3 * b + c] = block[:, :64]
    for t in range(4):
        block = sums_ref[CONV_ROWS + t * LANES : CONV_ROWS + (t + 1) * LANES].astype(F32).T
        down_ref[t] = block[:64]
        down_ref[t + 4] = block[64:]


def split_call(sums):
    return pl.pallas_call(
        split_kernel,
        out_shape=(
            jax.ShapeDtypeStruct((27, 64, 64), F32),
            jax.ShapeDtypeStruct((8, 64, LANES), F32),
        ),
        in_specs=[VMEM_SPEC],
        out_specs=(VMEM_SPEC,) * 2,
        compiler_params=params(16),
        name="split",
    )(sums)


def swaps(axis):
    return [(i, i ^ 1) for i in range(lax.axis_size(axis))]


def exchange(pair, other, axis):
    peers = lax.axis_size(axis)
    across = [(i, (i + 1) % peers) for i in range(1, peers, 2)]
    return (
        lax.ppermute(pair, axis, swaps(axis)),
        lax.ppermute(other, axis, across + [(j, i) for i, j in across]),
    )


def body(fine_input, conv_weight, down_weight, coarse_cot, neighbours, children):
    dev = ("z", "x")
    rank = lax.axis_index(("y", "core", "z", "x")).reshape(1).astype(jnp.int32)

    voxels, pair, other, token = faces_call(
        rank, children, neighbours, fine_input.reshape(LANES, SIDE**3)
    )
    own, send = cot_call(token, children, rank, coarse_cot.reshape(LANES, SIDE**3))
    pair, other = exchange(pair, other, dev)
    came = lax.ppermute(send, dev, swaps(dev))
    forward, backward, down, down_t = weights_call(conv_weight, down_weight.transpose(0, 2, 1))
    octants, slope, act, zero, one, both = forward_call(
        neighbours, rank, voxels, pair, other, forward, down
    )
    mine, other_out, grads, turned, spun = back_call(rank, own, came, down_t, slope, octants)
    theirs, grad_other = exchange(mine, other_out, dev)

    outer, inner = ("y", "x"), ("core", "z")
    shares, pieces = lax.axis_size(outer), lax.axis_size(inner)
    sums = weigh_call(zero, one, both, act, turned, spun, shares * SHARE)
    sums = stamp_call(sums, theirs, grad_other)
    came = lax.all_to_all(sums.reshape(shares, SHARE, LANES), outer, 0, 0)
    input_grad, token = input_call(sums, neighbours, rank, grads, theirs, grad_other, backward)
    part, token = add_shares_call(token, came, pieces * PIECE)
    came = lax.all_to_all(part.reshape(pieces, PIECE, LANES), inner, 0, 0)
    part, token = add_pieces_call(pass_call(token), came)
    came = lax.all_to_all(part, inner, 0, 0).reshape(pieces * PIECE, LANES)
    spread, token = spread_call(pass_call(token), came, shares)
    gathered = lax.all_to_all(spread, outer, 0, 0).reshape(shares * SHARE, LANES)
    coarse = coarse_call(token, children, rank, mine, theirs)
    conv_grad, down_grad = split_call(gathered)
    return (
        coarse.reshape(1, LANES, SIDE**3),
        input_grad.reshape(2, 64, SIDE**3),
        conv_grad,
        down_grad.transpose(0, 2, 1),
    )


def solution(mesh):
    grp, dev = mesh.devices.shape
    mesh = jax.sharding.Mesh(
        mesh.devices.reshape(grp // 2, 2, dev // 4, 4), ("y", "core", "z", "x")
    )
    bricks = ("y", "core", "z", "x")
    in_specs = (P(bricks, None, None), P(), P(), P(bricks, None, None), P(bricks, None), P(bricks, None))
    out_specs = (P(bricks, None, None), P(bricks, None, None), P(), P())
    return jax.shard_map(body, mesh=mesh, in_specs=in_specs, out_specs=out_specs, check_vma=False)
```

```python
import functools

import jax
import jax.numpy as jnp
from jax import lax
from jax.experimental import pallas as pl
from jax.experimental.pallas import tpu as pltpu
from jax.sharding import PartitionSpec as P

SIDE = 16
HALF = 8
LANES = 128
F32 = jnp.float32
BF16 = jnp.bfloat16
CONV_ROWS = 960
DOWN_ROWS = 512
GROUPS = 8
ROWS = 32
SHARE = (CONV_ROWS + DOWN_ROWS) // GROUPS

VMEM_SPEC = pl.BlockSpec(memory_space=pltpu.VMEM)
SMEM_SPEC = pl.BlockSpec(memory_space=pltpu.SMEM)
ANY_SPEC = pl.BlockSpec(memory_space=pl.ANY)
TOKEN = jax.ShapeDtypeStruct((8, LANES), F32)


def params(mib):
    return pltpu.CompilerParams(vmem_limit_bytes=mib * 1024 * 1024)


def loop(count, body, unroll):
    def step(g, carry):
        for p in range(unroll):
            body(g * unroll + p)
        return carry

    lax.fori_loop(0, count // unroll, step, 0)


def low_half(shape):
    return lax.broadcasted_iota(jnp.int32, shape, len(shape) - 1) < 64


def swap_halves(x):
    return pltpu.roll(x, 64, x.ndim - 1)


def place_faces(rank_ref, i, planes, pair_ref, other_ref, first=0):
    even = rank_ref[0] % 2 == 0
    low, high = planes[0], planes[SIDE - 1]
    pair_ref[pl.ds(pl.multiple_of(first + i * SIDE, SIDE), SIDE)] = jnp.where(even, high, low)
    other_ref[pl.ds(pl.multiple_of(i * SIDE, SIDE), SIDE)] = jnp.where(even, low, high)


def faces_kernel(rank_ref, x_ref, v_ref, pair_ref, other_ref, token_ref):
    def plane(i):
        columns = pl.ds(pl.multiple_of(i * 256, 256), 256)
        voxels = x_ref[:, columns].astype(F32).T.astype(BF16).reshape(SIDE, SIDE, LANES)
        v_ref[i] = voxels
        place_faces(rank_ref, i, voxels, pair_ref, other_ref)

    loop(SIDE, plane, 4)
    token_ref[...] = jnp.zeros_like(token_ref)


def faces_call(rank, x):
    face = jax.ShapeDtypeStruct((256, LANES), BF16)
    return pl.pallas_call(
        faces_kernel,
        out_shape=(jax.ShapeDtypeStruct((SIDE, SIDE, SIDE, LANES), BF16), face, face, TOKEN),
        in_specs=[SMEM_SPEC, VMEM_SPEC],
        out_specs=(VMEM_SPEC,) * 4,
        compiler_params=params(16),
        cost_estimate=pl.CostEstimate(flops=0, bytes_accessed=4_000_000, transcendentals=0),
        name="faces",
    )(rank, x)


def find_octant(child_ref, wanted):
    place = jnp.int32(0)
    found = jnp.int32(0)
    for o in range(8):
        hit = (child_ref[0, o] == wanted).astype(jnp.int32)
        place = place + hit * o
        found = found + hit
    return place, found


def cot_kernel(after_ref, child_ref, rank_ref, cot_ref, own_ref, send_ref, turned_ref):
    def plane(i):
        columns = pl.ds(pl.multiple_of(i * 256, 256), 256)
        turned = cot_ref[:, columns].astype(F32).T
        turned_ref[i // HALF, i % HALF] = turned.reshape(2, HALF, 2, HALF, LANES)

    loop(SIDE, plane, 4)
    rank = rank_ref[0]
    for out_ref, holder in ((own_ref, rank), (send_ref, rank ^ 1)):
        for slot in range(2):
            place, found = find_octant(child_ref, holder * 2 + slot)
            block = turned_ref[place // 4, :, place // 2 % 2, :, place % 2]
            block = jnp.where(found > 0, block, jnp.zeros_like(block))
            out_ref[slot * 512 : (slot + 1) * 512] = block.reshape(512, LANES).astype(BF16)


def cot_call(after, children, rank, cot):
    blocks = jax.ShapeDtypeStruct((1024, LANES), BF16)
    return pl.pallas_call(
        cot_kernel,
        out_shape=(blocks, blocks),
        in_specs=[ANY_SPEC, SMEM_SPEC, SMEM_SPEC, VMEM_SPEC],
        out_specs=(VMEM_SPEC,) * 2,
        scratch_shapes=[pltpu.VMEM((2, HALF, 2, HALF, 2, HALF, LANES), F32)],
        compiler_params=params(20),
        cost_estimate=pl.CostEstimate(flops=0, bytes_accessed=8_000_000, transcendentals=0),
        name="cot",
    )(after, children, rank, cot)


def weights_kernel(
    conv_ref, down_in_ref, forward_ref, backward_ref, down_ref, down_t_ref
):
    blank = jnp.zeros((64, 64), F32)
    for b in range(3):
        for c in range(3):
            rows = slice(b * 256 + c * 64, b * 256 + (c + 1) * 64)
            ahead = [conv_ref[9 * a + 3 * b + c].astype(F32) for a in range(3)]
            behind = [conv_ref[26 - (9 * a + 3 * b + c)].astype(F32) for a in range(3)]
            for n in range(2):
                order = (0, 1, 2, None) if n == 0 else (1, 0, None, 2)
                if c == 2:
                    rows = slice(b * 256 + 128 + n * 64, b * 256 + 192 + n * 64)
                    unused = slice(b * 256 + 192 - n * 64, b * 256 + 256 - n * 64)
                    forward_ref[n, unused] = jnp.zeros((64, 256), BF16)
                    backward_ref[n, unused] = jnp.zeros((64, 256), BF16)
                for half in range(2):
                    pair = order[2 * half : 2 * half + 2]
                    lanes = slice(half * LANES, (half + 1) * LANES)
                    taps = [blank if a is None else ahead[a] for a in pair]
                    forward_ref[n, rows, lanes] = jnp.concatenate(taps, axis=0).T.astype(BF16)
                    taps = [blank if a is None else behind[a] for a in pair]
                    backward_ref[n, rows, lanes] = jnp.concatenate(taps, axis=1).astype(BF16)
    for t in range(8):
        tap = down_in_ref[t]
        blank = jnp.zeros((64, LANES), BF16)
        rows = [jnp.concatenate([tap, blank], axis=1), jnp.concatenate([blank, tap], axis=1)]
        block = jnp.concatenate(rows, axis=0)
        down_ref[t * LANES : (t + 1) * LANES] = block
        down_t_ref[:, t * LANES : (t + 1) * LANES] = block.astype(F32).T.astype(BF16)


def weights_call(conv_weight, down_weight):
    conv = jax.ShapeDtypeStruct((2, 768, 256), BF16)
    return pl.pallas_call(
        weights_kernel,
        out_shape=(
            conv,
            conv,
            jax.ShapeDtypeStruct((8 * LANES, 256), BF16),
            jax.ShapeDtypeStruct((256, 8 * LANES), BF16),
        ),
        in_specs=[VMEM_SPEC] * 2,
        out_specs=(VMEM_SPEC,) * 4,
        compiler_params=params(16),
        cost_estimate=pl.CostEstimate(flops=0, bytes_accessed=8_000_000, transcendentals=0),
        name="weights",
    )(conv_weight, down_weight)


def coarse_half_kernel(half, *refs):
    _, child_ref, rank_ref, mine_ref, theirs_ref = refs[:5]
    out_ref, token_ref, whole_ref = refs[-3:]
    token_ref[...] = jnp.zeros_like(token_ref)
    for o in range(4):
        entry = child_ref[0, half * 4 + o]
        slot = jnp.maximum(entry, 0) % 2
        here = jnp.maximum(entry, 0) // 2 == rank_ref[0]
        rows = pl.ds(pl.multiple_of(slot * 512, 512), 512)
        block = jnp.where(here, mine_ref[rows], theirs_ref[rows])
        block = jnp.where(entry >= 0, block, jnp.zeros_like(block)).astype(F32)
        whole_ref[:, o // 2, :, o % 2] = block.reshape(HALF, HALF, HALF, LANES)

    for i in range(HALF):
        turned = whole_ref[i].reshape(256, LANES).T
        out_ref[:, i * 256 : (i + 1) * 256] = turned.astype(BF16)


def coarse_half_call(after, children, rank, mine, theirs, half, begun=()):
    return pl.pallas_call(
        functools.partial(coarse_half_kernel, half),
        grid=(1,),
        out_shape=(jax.ShapeDtypeStruct((LANES, SIDE**3), BF16), TOKEN),
        in_specs=[ANY_SPEC, SMEM_SPEC, SMEM_SPEC, VMEM_SPEC, VMEM_SPEC] + [ANY_SPEC] * len(begun),
        out_specs=(
            pl.BlockSpec((LANES, SIDE**3 // 2), lambda g: (0, half)),
            pl.BlockSpec((8, LANES), lambda g: (0, 0)),
        ),
        input_output_aliases={5: 0} if begun else {},
        scratch_shapes=[pltpu.VMEM((HALF, 2, HALF, 2, HALF, LANES), F32)],
        compiler_params=params(16),
        cost_estimate=pl.CostEstimate(flops=0, bytes_accessed=4_000_000, transcendentals=0),
        name="coarse_half",
    )(after, children, rank, mine, theirs, *begun)


def spans(step):
    if step == 0:
        return slice(1, SIDE + 1), slice(0, SIDE)
    if step == 1:
        return slice(SIDE + 1, SIDE + 2), slice(0, 1)
    return slice(0, 1), slice(SIDE - 1, SIDE)


def chooser(near_ref, column):
    lower = low_half((1, LANES))
    entries = near_ref[0, column], near_ref[1, column]
    straight = [
        jnp.logical_and(e >= 0, jnp.maximum(e, 0) % 2 == n).astype(F32)
        for n, e in enumerate(entries)
    ]
    crossed = [
        jnp.logical_and(e >= 0, jnp.maximum(e, 0) % 2 != n).astype(F32)
        for n, e in enumerate(entries)
    ]
    keep = jnp.where(lower, straight[0], straight[1])
    cross = jnp.where(lower, crossed[0], crossed[1])

    def choose(x):
        shape = (1,) * (x.ndim - 1) + (LANES,)
        return x * keep.reshape(shape) + swap_halves(x) * cross.reshape(shape)

    return choose


def offsets():
    steps = [(x, y, z) for x in (-1, 0, 1) for y in (-1, 0, 1) for z in (-1, 0, 1)]
    steps.remove((0, 0, 0))
    return list(enumerate(steps))


def assemble_inner(near_ref, v_ref, core_ref, ends_ref):
    def fill(i):
        core_ref[i + 1] = v_ref[i].astype(F32).reshape(256, LANES)

    loop(SIDE, fill, 4)
    lines = []
    for column, (step_x, step_y, step_z) in offsets():
        if step_y != 0:
            continue
        choose = chooser(near_ref, column)
        put_x, take_x = spans(step_x)
        end = 0 if step_z < 0 else 1
        strided = pl.ds(SIDE - 1 if step_z < 0 else 0, SIDE, stride=SIDE)
        if step_x == 0:
            lines.append((choose, end, strided))
        elif step_z == 0:
            core_ref[put_x.start] = choose(core_ref[take_x.start + 1])
        else:
            ends_ref[end, put_x.start] = choose(core_ref[take_x.start + 1, strided])

    def line(i):
        for choose, end, strided in lines:
            ends_ref[end, i + 1] = choose(core_ref[i + 1, strided])

    loop(SIDE, line, 4)


def assemble_edges(near_ref, rank_ref, pair_ref, other_ref, face_ref, core_ref, ends_ref):
    even = rank_ref[0] % 2 == 0
    pair = pair_ref[pair_ref.shape[0] - 256 :].astype(F32).reshape(SIDE, SIDE, LANES)
    other = other_ref[...].astype(F32).reshape(SIDE, SIDE, LANES)
    face_ref[0] = jnp.where(even, other, pair)
    face_ref[1] = jnp.where(even, pair, other)
    for column, (step_x, step_y, step_z) in offsets():
        if step_y == 0:
            continue
        choose = chooser(near_ref, column)
        put_x, take_x = spans(step_x)
        side = 0 if step_y < 0 else 1
        if step_z == 0:
            core_ref[put_x, side * SIDE : (side + 1) * SIDE] = choose(face_ref[side, take_x])
        else:
            end, row = (0, SIDE - 1) if step_z < 0 else (1, 0)
            ends_ref[end, put_x, side : side + 1] = choose(
                face_ref[side, take_x, row : row + 1]
            )


def gather_taps(core_ref, ends_ref, tap_refs, unroll):
    lower = low_half((SIDE, LANES))
    rows = lax.broadcasted_iota(jnp.int32, (8, LANES), 0)
    top, bottom = rows == 0, rows == 7

    def plane(i):
        for j in range(tap_refs[0].shape[1]):
            first = core_ref[i, j * SIDE : j * SIDE + 8]
            second = core_ref[i, j * SIDE + 8 : (j + 1) * SIDE]
            down_first, down_second = pltpu.roll(first, 1, 0), pltpu.roll(second, 1, 0)
            up_first, up_second = pltpu.roll(first, 7, 0), pltpu.roll(second, 7, 0)
            before = jnp.concatenate(
                [
                    jnp.where(top, ends_ref[0, i, j : j + 1], down_first),
                    jnp.where(top, down_first, down_second),
                ],
                axis=0,
            )
            after = jnp.concatenate(
                [
                    jnp.where(bottom, up_second, up_first),
                    jnp.where(bottom, ends_ref[1, i, j : j + 1], up_second),
                ],
                axis=0,
            )
            here = jnp.concatenate([first, second], axis=0)
            tap_refs[0][i, j] = jnp.where(lower, before, swap_halves(here)).astype(BF16)
            tap_refs[1][i, j] = jnp.where(lower, swap_halves(before), here).astype(BF16)
            tap_refs[2][i, j] = after.astype(BF16)

    loop(SIDE + 2, plane, unroll)


def window(refs, planes, b):
    inner_ref, edge_ref = refs
    if b == 0:
        parts = [edge_ref[planes, 0:1], inner_ref[planes, 0 : SIDE - 1]]
    elif b == 1:
        parts = [inner_ref[planes]]
    else:
        parts = [inner_ref[planes, 1:SIDE], edge_ref[planes, 1:2]]
    return jnp.concatenate(parts, axis=1).reshape(-1, LANES)


def convolve(tap_refs, w_ref, acc_ref, first=0, planes=SIDE + 2, group=6):
    rows = group * 256

    def clear(i):
        acc_ref[i] = jnp.zeros((256, LANES), F32)

    loop(planes + 2, clear, 4)
    lower = low_half((256, LANES))

    def step(g, carry):
        start = g * group
        results = []
        for n in range(2):
            lhs = [
                window(tap_refs[chunk], pl.ds(first + start, group), b)
                for b in range(3)
                for chunk in (n, 2)
            ]
            lhs = jnp.concatenate(lhs, axis=1)
            results.append(jnp.dot(lhs, w_ref[n], preferred_element_type=F32))
        zero, one = results
        for p in range(group):
            own = slice(p * 256, (p + 1) * 256)
            z, o = zero[own], one[own]
            acc_ref[start + p + 2] += jnp.where(lower, z[:, :LANES], o[:, :LANES])
            acc_ref[start + p + 1] += swap_halves(jnp.where(lower, o[:, :LANES], z[:, :LANES]))
            acc_ref[start + p] += z[:, LANES:] + o[:, LANES:]
        return carry

    lax.fori_loop(0, planes // group, step, 0)


def taps():
    return [(t, t // 4, t // 2 % 2, t % 2) for t in range(8)]


def inner_kernel(near_ref, v_ref, zero_ref, one_ref, both_ref, core_ref, ends_ref):
    assemble_inner(near_ref, v_ref, core_ref, ends_ref)
    gather_taps(core_ref, ends_ref, (zero_ref, one_ref, both_ref), 3)


def forward_kernel(
    near_ref,
    rank_ref,
    pair_ref,
    other_ref,
    zero_ref,
    one_ref,
    both_ref,
    w_ref,
    down_ref,
    oct_ref,
    slope_ref,
    act_ref,
    zero_edge_ref,
    one_edge_ref,
    both_edge_ref,
    face_ref,
    core_ref,
    ends_ref,
    acc_ref,
    fine_ref,
):
    edges = (zero_edge_ref, one_edge_ref, both_edge_ref)
    assemble_edges(near_ref, rank_ref, pair_ref, other_ref, face_ref, core_ref, ends_ref)
    gather_taps(core_ref, ends_ref, edges, 9)
    convolve(tuple(zip((zero_ref, one_ref, both_ref), edges)), w_ref, acc_ref)

    def activate(i):
        preact = acc_ref[i + 2]
        gate = 1.0 / (1.0 + jnp.exp(-preact))
        fine_ref[i // 2, i % 2] = (preact * gate).reshape(HALF, 2, SIDE, LANES)
        slope_ref[i] = gate * (1.0 + preact * (1.0 - gate))

    loop(SIDE, activate, 4)
    for t, a, b, c in taps():
        picked = fine_ref[:, a, :, b, pl.ds(c, HALF, stride=2), :]
        act_ref[:, t * LANES : (t + 1) * LANES] = picked.reshape(512, LANES).astype(BF16)
    octants = jnp.dot(act_ref[...], down_ref[...], preferred_element_type=F32).astype(BF16)
    oct_ref[0:512] = octants[:, :LANES]
    oct_ref[512:1024] = octants[:, LANES:]


def back_kernel(
    rank_ref,
    own_ref,
    came_ref,
    down_t_ref,
    slope_ref,
    oct_ref,
    pair_ref,
    other_ref,
    g_ref,
    turned_ref,
    spun_ref,
    fine_ref,
):
    pair_ref[0:1024] = oct_ref[...]
    grads = []
    for n in range(2):
        rows = slice(n * 512, (n + 1) * 512)
        grad = own_ref[rows].astype(F32) + came_ref[rows].astype(F32)
        spun_ref[n] = grad.T.astype(BF16)
        grads.append(grad.astype(BF16))
    grads = jnp.concatenate(grads, axis=1)
    for pair in range(4):
        lanes = slice(pair * 256, (pair + 1) * 256)
        spread = jnp.dot(grads, down_t_ref[:, lanes], preferred_element_type=F32)
        for c in range(2):
            part = spread[:, c * LANES : (c + 1) * LANES].reshape(HALF, HALF, HALF, LANES)
            fine_ref[:, pair // 2, :, pair % 2, pl.ds(c, HALF, stride=2), :] = part

    for p in (0, 1, SIDE + 2, SIDE + 3):
        turned_ref[p] = jnp.zeros((LANES, 256), BF16)

    def back(i):
        grad = fine_ref[i // 2, i % 2].reshape(256, LANES) * slope_ref[i]
        turned_ref[i + 2] = grad.T.astype(BF16)
        rounded = grad.astype(BF16).reshape(SIDE, SIDE, LANES)
        g_ref[i] = rounded
        place_faces(rank_ref, i, rounded, pair_ref, other_ref, 1024)

    loop(SIDE, back, 4)


def weigh_kernel(*refs):
    rank_ref, inner, edges = refs[0], refs[1:4], refs[4:7]
    act_ref, turned_ref, spun_ref, kept_ref, sent_ref, sums_ref, total_ref = refs[7:]
    zero, one, both_taps = zip(inner, edges)
    lower = low_half((LANES, LANES))
    whole = [jnp.dot(spun_ref[n], act_ref[...], preferred_element_type=F32) for n in range(2)]
    folded = []
    for t in range(8):
        lanes = slice(t * LANES, (t + 1) * LANES)
        both = jnp.where(lower, whole[0][:, lanes], whole[1][:, lanes])
        folded.append(both + swap_halves(both))
    for t in range(4):
        rows = slice(CONV_ROWS + t * LANES, CONV_ROWS + (t + 1) * LANES)
        sums_ref[rows] = jnp.where(lower, folded[t], folded[t + 4])

    total_ref[...] = jnp.zeros_like(total_ref)

    def weigh(g, carry):
        planes = [3 * g + p for p in range(3)]
        for n, brick in enumerate((zero, one)):
            lhs = [
                jnp.concatenate(
                    [turned_ref[i + 2 - a, n * 64 : (n + 1) * 64] for a in range(3)], axis=0
                )
                for i in planes
            ]
            rhs = [
                jnp.concatenate(
                    [
                        window(refs, pl.ds(i, 1), b)
                        for refs in (brick, both_taps)
                        for b in range(3)
                    ],
                    axis=1,
                )
                for i in planes
            ]
            total_ref[n] += jnp.dot(
                jnp.concatenate(lhs, axis=1),
                jnp.concatenate(rhs, axis=0),
                preferred_element_type=F32,
            )
        return carry

    lax.fori_loop(0, (SIDE + 2) // 3, weigh, 0)
    lower = low_half((192, LANES))
    last = []
    for b in range(3):
        lanes = slice(b * LANES, (b + 1) * LANES)
        sums_ref[b * 192 : (b + 1) * 192] = total_ref[0, :, lanes] + total_ref[1, :, lanes]
        lanes = slice((3 + b) * LANES, (4 + b) * LANES)
        both = jnp.where(lower, total_ref[0, :, lanes], total_ref[1, :, lanes])
        last.append(both + swap_halves(both))
    sums_ref[576:768] = jnp.where(lower, last[0], last[1])
    sums_ref[768:960] = jnp.where(lower, last[2], 0.0)
    core = core_of(rank_ref)
    for y in range(GROUPS // 2):
        kept_ref[y] = sums_ref[share_rows(2 * y + core)]
        sent_ref[y] = sums_ref[share_rows(2 * y + 1 - core)].astype(BF16)


def core_of(rank_ref):
    return rank_ref[0] // ROWS % 2


def y_of(rank_ref):
    return rank_ref[0] // (2 * ROWS)


def share_rows(group):
    return pl.ds(pl.multiple_of(group * SHARE, 8), SHARE)


INNER_TAPS = jax.ShapeDtypeStruct((SIDE + 2, SIDE, SIDE, LANES), BF16)
EDGE_TAPS = jax.ShapeDtypeStruct((SIDE + 2, 2, SIDE, LANES), BF16)
INNER_SCRATCH = [
    pltpu.VMEM((SIDE + 2, 256, LANES), F32),
    pltpu.VMEM((2, SIDE + 2, SIDE, LANES), F32),
]
EDGE_SCRATCH = [
    pltpu.VMEM((2, SIDE, SIDE, LANES), F32),
    pltpu.VMEM((SIDE + 2, 2 * SIDE, LANES), F32),
    pltpu.VMEM((2, SIDE + 2, 8, LANES), F32),
]
ACC_SCRATCH = pltpu.VMEM((SIDE + 4, 256, LANES), F32)
FINE_SCRATCH = pltpu.VMEM((HALF, 2, HALF, 2, SIDE, LANES), F32)


def inner_call(near, v):
    return pl.pallas_call(
        inner_kernel,
        out_shape=(INNER_TAPS,) * 3,
        in_specs=[SMEM_SPEC, VMEM_SPEC],
        out_specs=(VMEM_SPEC,) * 3,
        scratch_shapes=INNER_SCRATCH,
        compiler_params=params(20),
        cost_estimate=pl.CostEstimate(
            flops=1_000_000_000, bytes_accessed=8_000_000, transcendentals=0
        ),
        name="inner",
    )(near, v)


def forward_call(near, rank, pair, other, inner, weights, down):
    return pl.pallas_call(
        forward_kernel,
        out_shape=(
            jax.ShapeDtypeStruct((1024, LANES), BF16),
            jax.ShapeDtypeStruct((SIDE, 256, LANES), F32),
            jax.ShapeDtypeStruct((512, 8 * LANES), BF16),
        )
        + (EDGE_TAPS,) * 3,
        in_specs=[SMEM_SPEC] * 2 + [VMEM_SPEC] * 7,
        out_specs=(VMEM_SPEC,) * 6,
        scratch_shapes=EDGE_SCRATCH + [ACC_SCRATCH, FINE_SCRATCH],
        compiler_params=params(28),
        cost_estimate=pl.CostEstimate(
            flops=4_000_000_000, bytes_accessed=16_000_000, transcendentals=600_000
        ),
        name="forward",
    )(near, rank, pair, other, *inner, weights, down)


def back_call(rank, own, came, down_t, slope, octants):
    return pl.pallas_call(
        back_kernel,
        out_shape=(
            jax.ShapeDtypeStruct((1280, LANES), BF16),
            jax.ShapeDtypeStruct((256, LANES), BF16),
            jax.ShapeDtypeStruct((SIDE, SIDE, SIDE, LANES), BF16),
            jax.ShapeDtypeStruct((SIDE + 4, LANES, 256), BF16),
            jax.ShapeDtypeStruct((2, LANES, 512), BF16),
        ),
        in_specs=[SMEM_SPEC] + [VMEM_SPEC] * 5,
        out_specs=(VMEM_SPEC,) * 5,
        scratch_shapes=[FINE_SCRATCH],
        compiler_params=params(24),
        cost_estimate=pl.CostEstimate(
            flops=300_000_000, bytes_accessed=8_000_000, transcendentals=0
        ),
        name="back",
    )(rank, own, came, down_t, slope, octants)


def weigh_call(rank, inner, edges, act, turned, spun):
    return pl.pallas_call(
        weigh_kernel,
        out_shape=(
            jax.ShapeDtypeStruct((GROUPS // 2, SHARE, LANES), F32),
            jax.ShapeDtypeStruct((GROUPS // 2, SHARE, LANES), BF16),
        ),
        in_specs=[SMEM_SPEC] + [VMEM_SPEC] * 9,
        out_specs=(VMEM_SPEC,) * 2,
        scratch_shapes=[
            pltpu.VMEM((CONV_ROWS + DOWN_ROWS, LANES), F32),
            pltpu.VMEM((2, 192, 768), F32),
        ],
        compiler_params=params(20),
        cost_estimate=pl.CostEstimate(
            flops=4_000_000_000, bytes_accessed=10_000_000, transcendentals=0
        ),
        name="weigh",
    )(rank, *inner, *edges, act, turned, spun)


def input_taps_kernel(after_ref, near_ref, rank_ref, g_ref, pair_ref, other_ref, *refs):
    inner, edges, token_ref = refs[:3], refs[3:6], refs[6]
    core_ref, ends_ref, face_ref, edge_core_ref, edge_ends_ref = refs[7:]
    assemble_inner(near_ref, g_ref, core_ref, ends_ref)
    gather_taps(core_ref, ends_ref, inner, 3)
    assemble_edges(
        near_ref, rank_ref, pair_ref, other_ref, face_ref, edge_core_ref, edge_ends_ref
    )
    gather_taps(edge_core_ref, edge_ends_ref, edges, 9)
    token_ref[...] = jnp.zeros_like(token_ref)


def input_taps_call(after, near, rank, g, pair, other):
    return pl.pallas_call(
        input_taps_kernel,
        out_shape=(INNER_TAPS,) * 3 + (EDGE_TAPS,) * 3 + (TOKEN,),
        in_specs=[ANY_SPEC] + [SMEM_SPEC] * 2 + [VMEM_SPEC] * 3,
        out_specs=(VMEM_SPEC,) * 7,
        scratch_shapes=INNER_SCRATCH + EDGE_SCRATCH,
        compiler_params=params(20),
        cost_estimate=pl.CostEstimate(
            flops=1_000_000_000, bytes_accessed=8_000_000, transcendentals=0
        ),
        name="input_taps",
    )(after, near, rank, g, pair, other)


def input_half_kernel(half, *refs):
    inner, edges, w_ref = refs[1:4], refs[4:7], refs[7]
    out_ref, token_ref, acc_ref = refs[-3:]
    convolve(tuple(zip(inner, edges)), w_ref, acc_ref, half * HALF, HALF + 2, 5)

    for i in range(HALF):
        out_ref[:, i * 256 : (i + 1) * 256] = acc_ref[i + 2].T.astype(BF16)
    token_ref[...] = jnp.zeros_like(token_ref)


def input_half_call(after, taps, weights, half, begun=()):
    return pl.pallas_call(
        functools.partial(input_half_kernel, half),
        grid=(1,),
        out_shape=(jax.ShapeDtypeStruct((LANES, SIDE**3), BF16), TOKEN),
        in_specs=[ANY_SPEC] + [VMEM_SPEC] * 7 + [ANY_SPEC] * len(begun),
        out_specs=(
            pl.BlockSpec((LANES, SIDE**3 // 2), lambda g: (0, half)),
            pl.BlockSpec((8, LANES), lambda g: (0, 0)),
        ),
        input_output_aliases={8: 0} if begun else {},
        scratch_shapes=[pltpu.VMEM((HALF + 4, 256, LANES), F32)],
        compiler_params=params(16),
        cost_estimate=pl.CostEstimate(
            flops=2_500_000_000, bytes_accessed=6_000_000, transcendentals=0
        ),
        name="input_half",
    )(after, *taps, weights, *begun)


def deal_kernel(rank_ref, kept_ref, came_ref, own_ref, *refs):
    share_refs, total_ref = refs[:-1], refs[-1]
    total_ref[...] = kept_ref[...] + came_ref[...].astype(F32)
    y = y_of(rank_ref)
    own_ref[...] = total_ref[y]
    for s, share_ref in enumerate(share_refs):
        share_ref[...] = total_ref[y ^ (s + 1)].astype(BF16)


def deal_call(rank, kept, came):
    return pl.pallas_call(
        deal_kernel,
        out_shape=(jax.ShapeDtypeStruct((SHARE, LANES), F32),)
        + (jax.ShapeDtypeStruct((SHARE, LANES), BF16),) * 3,
        in_specs=[SMEM_SPEC, VMEM_SPEC, VMEM_SPEC],
        out_specs=(VMEM_SPEC,) * 4,
        scratch_shapes=[pltpu.VMEM((GROUPS // 2, SHARE, LANES), F32)],
        compiler_params=params(16),
        cost_estimate=pl.CostEstimate(flops=0, bytes_accessed=500_000, transcendentals=0),
        name="deal",
    )(rank, kept, came)


def add_kernel(after_ref, *refs):
    parts = [ref[...].astype(F32) for ref in refs[:-1]]
    while len(parts) > 1:
        parts = [first + second for first, second in zip(parts[::2], parts[1::2])]
    refs[-1][...] = parts[0].astype(refs[-1].dtype)


def add_call(after, parts, dtype=BF16):
    return pl.pallas_call(
        add_kernel,
        out_shape=jax.ShapeDtypeStruct(parts[0].shape, dtype),
        in_specs=[ANY_SPEC] + [VMEM_SPEC] * len(parts),
        out_specs=VMEM_SPEC,
        compiler_params=params(16),
        cost_estimate=pl.CostEstimate(flops=0, bytes_accessed=500_000, transcendentals=0),
        name="add",
    )(after, *parts)


def collect_kernel(after_ref, rank_ref, *refs):
    y = y_of(rank_ref)
    for s, share_ref in enumerate(refs[:-1]):
        refs[-1][y ^ s] = share_ref[...]


def collect_call(after, rank, shares):
    return pl.pallas_call(
        collect_kernel,
        out_shape=jax.ShapeDtypeStruct((GROUPS // 2, SHARE, LANES), BF16),
        in_specs=[ANY_SPEC, SMEM_SPEC] + [VMEM_SPEC] * len(shares),
        out_specs=VMEM_SPEC,
        compiler_params=params(16),
        cost_estimate=pl.CostEstimate(flops=0, bytes_accessed=500_000, transcendentals=0),
        name="collect",
    )(after, rank, *shares)


def split_kernel(rank_ref, mine_ref, theirs_ref, conv_ref, down_ref, sums_ref):
    core = core_of(rank_ref)
    for y in range(GROUPS // 2):
        sums_ref[share_rows(2 * y + core)] = mine_ref[y].astype(F32)
        sums_ref[share_rows(2 * y + 1 - core)] = theirs_ref[y].astype(F32)
    for a in range(3):
        for b in range(3):
            for c in range(3):
                chunk, upper = (b, c) if c < 2 else ((3, b) if b < 2 else (4, 0))
                base = chunk * 192 + a * 64
                block = sums_ref[base : base + 64]
                block = swap_halves(block) if upper else block
                conv_ref[9 * a + 3 * b + c] = block[:, :64]
    for t in range(4):
        block = sums_ref[CONV_ROWS + t * LANES : CONV_ROWS + (t + 1) * LANES].T
        down_ref[t] = block[:64]
        down_ref[t + 4] = block[64:]


def split_call(rank, mine, theirs):
    return pl.pallas_call(
        split_kernel,
        out_shape=(
            jax.ShapeDtypeStruct((27, 64, 64), F32),
            jax.ShapeDtypeStruct((8, 64, LANES), F32),
        ),
        in_specs=[SMEM_SPEC] + [VMEM_SPEC] * 2,
        out_specs=(VMEM_SPEC,) * 2,
        scratch_shapes=[pltpu.VMEM((CONV_ROWS + DOWN_ROWS, LANES), F32)],
        compiler_params=params(16),
        name="split",
    )(rank, mine, theirs)


def swaps(axis, step=1):
    return [(i, i ^ step) for i in range(lax.axis_size(axis))]


def swapped(array, axis, steps):
    return [lax.ppermute(array, axis, swaps(axis, step)) for step in steps]


def exchange(pair, other, axis):
    peers = lax.axis_size(axis)
    across = [(i, (i + 1) % peers) for i in range(1, peers, 2)]
    return (
        lax.ppermute(pair, axis, swaps(axis)),
        lax.ppermute(other, axis, across + [(j, i) for i, j in across]),
    )


def body(fine_input, conv_weight, down_weight, coarse_cot, neighbours, children):
    dev = ("z", "x")
    rank = lax.axis_index(("y", "core", "z", "x")).reshape(1).astype(jnp.int32)

    voxels, pair, other, token = faces_call(rank, fine_input.reshape(LANES, SIDE**3))
    own, send = cot_call(token, children, rank, coarse_cot.reshape(LANES, SIDE**3))
    pair, other = exchange(pair, other, dev)
    came = lax.ppermute(send, dev, swaps(dev))
    forward, backward, down, down_t = weights_call(conv_weight, down_weight.transpose(0, 2, 1))
    inner = inner_call(neighbours, voxels)
    octants, slope, act, *edges = forward_call(
        neighbours, rank, pair, other, inner, forward, down
    )
    mine, other_out, grads, turned, spun = back_call(rank, own, came, down_t, slope, octants)
    theirs, grad_other = exchange(mine, other_out, dev)

    kept, sent = weigh_call(rank, inner, edges, act, turned, spun)
    (came,) = swapped(sent, "core", (1,))
    own, *shares = deal_call(rank, kept, came)
    came = [lax.ppermute(share, "y", swaps("y", s + 1)) for s, share in enumerate(shares)]
    *taps_in, token = input_taps_call(own, neighbours, rank, grads, theirs, grad_other)
    part = add_call(token, [own, *came], F32)
    came = swapped(part, "x", (1, 2, 3))
    input_grad, token = input_half_call(part, taps_in, backward, 0)
    part = add_call(token, [part, *came])
    came = swapped(part, "z", (1, 2, 3))
    input_grad, token = input_half_call(part, taps_in, backward, 1, (input_grad,))
    part = add_call(token, [part, *came])
    came = swapped(part, "z", (4,))
    coarse, token = coarse_half_call(part, children, rank, mine, theirs, 0)
    part = add_call(token, [part, *came])
    came = swapped(part, "y", (1, 2, 3))
    coarse, token = coarse_half_call(part, children, rank, mine, theirs, 1, (coarse,))
    shares = collect_call(token, rank, [part, *came])
    (came,) = swapped(shares, "core", (1,))
    conv_grad, down_grad = split_call(rank, shares, came)
    return (
        coarse.reshape(1, LANES, SIDE**3),
        input_grad.reshape(2, 64, SIDE**3),
        conv_grad,
        down_grad.transpose(0, 2, 1),
    )


def solution(mesh):
    grp, dev = mesh.devices.shape
    mesh = jax.sharding.Mesh(
        mesh.devices.reshape(grp // 2, 2, dev // 4, 4), ("y", "core", "z", "x")
    )
    bricks = ("y", "core", "z", "x")
    in_specs = (P(bricks, None, None), P(), P(), P(bricks, None, None), P(bricks, None), P(bricks, None))
    out_specs = (P(bricks, None, None), P(bricks, None, None), P(), P())
    return jax.shard_map(body, mesh=mesh, in_specs=in_specs, out_specs=out_specs, check_vma=False)
```

```python
import functools

import jax
import jax.numpy as jnp
from jax import lax
from jax.experimental import pallas as pl
from jax.experimental.pallas import tpu as pltpu
from jax.sharding import PartitionSpec as P

SIDE = 16
HALF = 8
LANES = 128
F32 = jnp.float32
BF16 = jnp.bfloat16
CONV_ROWS = 960
DOWN_ROWS = 512
GROUPS = 8
ROWS = 32
SHARE = (CONV_ROWS + DOWN_ROWS) // GROUPS

VMEM_SPEC = pl.BlockSpec(memory_space=pltpu.VMEM)
SMEM_SPEC = pl.BlockSpec(memory_space=pltpu.SMEM)
ANY_SPEC = pl.BlockSpec(memory_space=pl.ANY)
TOKEN = jax.ShapeDtypeStruct((8, LANES), F32)


def params(mib):
    return pltpu.CompilerParams(vmem_limit_bytes=mib * 1024 * 1024)


def loop(count, body, unroll):
    def step(g, carry):
        for p in range(unroll):
            body(g * unroll + p)
        return carry

    lax.fori_loop(0, count // unroll, step, 0)


def low_half(shape):
    return lax.broadcasted_iota(jnp.int32, shape, len(shape) - 1) < 64


def swap_halves(x):
    return pltpu.roll(x, 64, x.ndim - 1)


def place_faces(rank_ref, i, planes, pair_ref, other_ref, first=0):
    even = rank_ref[0] % 2 == 0
    low, high = planes[0], planes[SIDE - 1]
    pair_ref[pl.ds(pl.multiple_of(first + i * SIDE, SIDE), SIDE)] = jnp.where(even, high, low)
    other_ref[pl.ds(pl.multiple_of(i * SIDE, SIDE), SIDE)] = jnp.where(even, low, high)


def faces_kernel(rank_ref, x_ref, v_ref, pair_ref, other_ref):
    def plane(i):
        columns = pl.ds(pl.multiple_of(i * 256, 256), 256)
        voxels = x_ref[:, columns].astype(F32).T.astype(BF16).reshape(SIDE, SIDE, LANES)
        v_ref[i] = voxels
        place_faces(rank_ref, i, voxels, pair_ref, other_ref)

    loop(SIDE, plane, 4)


def faces_call(rank, x):
    face = jax.ShapeDtypeStruct((256, LANES), BF16)
    return pl.pallas_call(
        faces_kernel,
        out_shape=(jax.ShapeDtypeStruct((SIDE, SIDE, SIDE, LANES), BF16), face, face),
        in_specs=[SMEM_SPEC, VMEM_SPEC],
        out_specs=(VMEM_SPEC,) * 3,
        compiler_params=params(16),
        cost_estimate=pl.CostEstimate(flops=0, bytes_accessed=4_000_000, transcendentals=0),
        name="faces",
    )(rank, x)


def find_octant(child_ref, wanted):
    place = jnp.int32(0)
    found = jnp.int32(0)
    for o in range(8):
        hit = (child_ref[0, o] == wanted).astype(jnp.int32)
        place = place + hit * o
        found = found + hit
    return place, found


def cot_kernel(face_ref, child_ref, rank_ref, cot_ref, own_ref, send_ref, turned_ref):
    send_ref[1024:1280] = face_ref[...]

    def plane(i):
        columns = pl.ds(pl.multiple_of(i * 256, 256), 256)
        turned = cot_ref[:, columns].astype(F32).T
        turned_ref[i // HALF, i % HALF] = turned.reshape(2, HALF, 2, HALF, LANES)

    loop(SIDE, plane, 4)
    rank = rank_ref[0]
    for out_ref, holder in ((own_ref, rank), (send_ref, rank ^ 1)):
        for slot in range(2):
            place, found = find_octant(child_ref, holder * 2 + slot)
            block = turned_ref[place // 4, :, place // 2 % 2, :, place % 2]
            block = jnp.where(found > 0, block, jnp.zeros_like(block))
            out_ref[slot * 512 : (slot + 1) * 512] = block.reshape(512, LANES).astype(BF16)


def cot_call(face, children, rank, cot):
    return pl.pallas_call(
        cot_kernel,
        out_shape=(
            jax.ShapeDtypeStruct((1024, LANES), BF16),
            jax.ShapeDtypeStruct((1280, LANES), BF16),
        ),
        in_specs=[VMEM_SPEC, SMEM_SPEC, SMEM_SPEC, VMEM_SPEC],
        out_specs=(VMEM_SPEC,) * 2,
        scratch_shapes=[pltpu.VMEM((2, HALF, 2, HALF, 2, HALF, LANES), F32)],
        compiler_params=params(20),
        cost_estimate=pl.CostEstimate(flops=0, bytes_accessed=8_000_000, transcendentals=0),
        name="cot",
    )(face, children, rank, cot)


def weights_kernel(
    conv_ref, down_in_ref, forward_ref, backward_ref, down_ref, down_t_ref
):
    blank = jnp.zeros((64, 64), F32)
    for b in range(3):
        for c in range(3):
            rows = slice(b * 256 + c * 64, b * 256 + (c + 1) * 64)
            ahead = [conv_ref[9 * a + 3 * b + c].astype(F32) for a in range(3)]
            behind = [conv_ref[26 - (9 * a + 3 * b + c)].astype(F32) for a in range(3)]
            for n in range(2):
                order = (0, 1, 2, None) if n == 0 else (1, 0, None, 2)
                if c == 2:
                    rows = slice(b * 256 + 128 + n * 64, b * 256 + 192 + n * 64)
                    unused = slice(b * 256 + 192 - n * 64, b * 256 + 256 - n * 64)
                    forward_ref[n, unused] = jnp.zeros((64, 256), BF16)
                    backward_ref[n, unused] = jnp.zeros((64, 256), BF16)
                for half in range(2):
                    pair = order[2 * half : 2 * half + 2]
                    lanes = slice(half * LANES, (half + 1) * LANES)
                    taps = [blank if a is None else ahead[a] for a in pair]
                    forward_ref[n, rows, lanes] = jnp.concatenate(taps, axis=0).T.astype(BF16)
                    taps = [blank if a is None else behind[a] for a in pair]
                    backward_ref[n, rows, lanes] = jnp.concatenate(taps, axis=1).astype(BF16)
    for t in range(8):
        tap = down_in_ref[t]
        blank = jnp.zeros((64, LANES), BF16)
        rows = [jnp.concatenate([tap, blank], axis=1), jnp.concatenate([blank, tap], axis=1)]
        block = jnp.concatenate(rows, axis=0)
        down_ref[t * LANES : (t + 1) * LANES] = block
        down_t_ref[:, t * LANES : (t + 1) * LANES] = block.astype(F32).T.astype(BF16)


def weights_call(conv_weight, down_weight):
    conv = jax.ShapeDtypeStruct((2, 768, 256), BF16)
    return pl.pallas_call(
        weights_kernel,
        out_shape=(
            conv,
            conv,
            jax.ShapeDtypeStruct((8 * LANES, 256), BF16),
            jax.ShapeDtypeStruct((256, 8 * LANES), BF16),
        ),
        in_specs=[VMEM_SPEC] * 2,
        out_specs=(VMEM_SPEC,) * 4,
        compiler_params=params(16),
        cost_estimate=pl.CostEstimate(flops=0, bytes_accessed=8_000_000, transcendentals=0),
        name="weights",
    )(conv_weight, down_weight)


def coarse_half_kernel(half, *refs):
    _, child_ref, rank_ref, mine_ref, theirs_ref = refs[:5]
    out_ref, token_ref, whole_ref = refs[-3:]
    token_ref[...] = jnp.zeros_like(token_ref)
    for o in range(4):
        entry = child_ref[0, half * 4 + o]
        slot = jnp.maximum(entry, 0) % 2
        here = jnp.maximum(entry, 0) // 2 == rank_ref[0]
        rows = pl.ds(pl.multiple_of(slot * 512, 512), 512)
        block = jnp.where(here, mine_ref[rows], theirs_ref[rows])
        block = jnp.where(entry >= 0, block, jnp.zeros_like(block)).astype(F32)
        whole_ref[:, o // 2, :, o % 2] = block.reshape(HALF, HALF, HALF, LANES)

    for i in range(HALF):
        turned = whole_ref[i].reshape(256, LANES).T
        out_ref[:, i * 256 : (i + 1) * 256] = turned.astype(BF16)


def coarse_half_call(after, children, rank, mine, theirs, half, begun=()):
    return pl.pallas_call(
        functools.partial(coarse_half_kernel, half),
        grid=(1,),
        out_shape=(jax.ShapeDtypeStruct((LANES, SIDE**3), BF16), TOKEN),
        in_specs=[ANY_SPEC, SMEM_SPEC, SMEM_SPEC, VMEM_SPEC, VMEM_SPEC] + [ANY_SPEC] * len(begun),
        out_specs=(
            pl.BlockSpec((LANES, SIDE**3 // 2), lambda g: (0, half)),
            pl.BlockSpec((8, LANES), lambda g: (0, 0)),
        ),
        input_output_aliases={5: 0} if begun else {},
        scratch_shapes=[pltpu.VMEM((HALF, 2, HALF, 2, HALF, LANES), F32)],
        compiler_params=params(16),
        cost_estimate=pl.CostEstimate(flops=0, bytes_accessed=4_000_000, transcendentals=0),
        name="coarse_half",
    )(after, children, rank, mine, theirs, *begun)


def spans(step):
    if step == 0:
        return slice(1, SIDE + 1), slice(0, SIDE)
    if step == 1:
        return slice(SIDE + 1, SIDE + 2), slice(0, 1)
    return slice(0, 1), slice(SIDE - 1, SIDE)


def chooser(near_ref, column):
    lower = low_half((1, LANES))
    entries = near_ref[0, column], near_ref[1, column]
    straight = [
        jnp.logical_and(e >= 0, jnp.maximum(e, 0) % 2 == n).astype(F32)
        for n, e in enumerate(entries)
    ]
    crossed = [
        jnp.logical_and(e >= 0, jnp.maximum(e, 0) % 2 != n).astype(F32)
        for n, e in enumerate(entries)
    ]
    keep = jnp.where(lower, straight[0], straight[1])
    cross = jnp.where(lower, crossed[0], crossed[1])

    def choose(x):
        shape = (1,) * (x.ndim - 1) + (LANES,)
        return x * keep.reshape(shape) + swap_halves(x) * cross.reshape(shape)

    return choose


def offsets():
    steps = [(x, y, z) for x in (-1, 0, 1) for y in (-1, 0, 1) for z in (-1, 0, 1)]
    steps.remove((0, 0, 0))
    return list(enumerate(steps))


def assemble_inner(near_ref, v_ref, core_ref, ends_ref):
    def fill(i):
        core_ref[i + 1] = v_ref[i].astype(F32).reshape(256, LANES)

    loop(SIDE, fill, 4)
    lines = []
    for column, (step_x, step_y, step_z) in offsets():
        if step_y != 0:
            continue
        choose = chooser(near_ref, column)
        put_x, take_x = spans(step_x)
        end = 0 if step_z < 0 else 1
        strided = pl.ds(SIDE - 1 if step_z < 0 else 0, SIDE, stride=SIDE)
        if step_x == 0:
            lines.append((choose, end, strided))
        elif step_z == 0:
            core_ref[put_x.start] = choose(core_ref[take_x.start + 1])
        else:
            ends_ref[end, put_x.start] = choose(core_ref[take_x.start + 1, strided])

    def line(i):
        for choose, end, strided in lines:
            ends_ref[end, i + 1] = choose(core_ref[i + 1, strided])

    loop(SIDE, line, 4)


def assemble_edges(near_ref, rank_ref, pair_ref, other_ref, face_ref, core_ref, ends_ref):
    even = rank_ref[0] % 2 == 0
    pair = pair_ref[pair_ref.shape[0] - 256 :].astype(F32).reshape(SIDE, SIDE, LANES)
    other = other_ref[...].astype(F32).reshape(SIDE, SIDE, LANES)
    face_ref[0] = jnp.where(even, other, pair)
    face_ref[1] = jnp.where(even, pair, other)
    for column, (step_x, step_y, step_z) in offsets():
        if step_y == 0:
            continue
        choose = chooser(near_ref, column)
        put_x, take_x = spans(step_x)
        side = 0 if step_y < 0 else 1
        if step_z == 0:
            core_ref[put_x, side * SIDE : (side + 1) * SIDE] = choose(face_ref[side, take_x])
        else:
            end, row = (0, SIDE - 1) if step_z < 0 else (1, 0)
            ends_ref[end, put_x, side : side + 1] = choose(
                face_ref[side, take_x, row : row + 1]
            )


def gather_taps(core_ref, ends_ref, tap_refs, unroll):
    lower = low_half((SIDE, LANES))
    rows = lax.broadcasted_iota(jnp.int32, (8, LANES), 0)
    top, bottom = rows == 0, rows == 7

    def plane(i):
        for j in range(tap_refs[0].shape[1]):
            first = core_ref[i, j * SIDE : j * SIDE + 8]
            second = core_ref[i, j * SIDE + 8 : (j + 1) * SIDE]
            down_first, down_second = pltpu.roll(first, 1, 0), pltpu.roll(second, 1, 0)
            up_first, up_second = pltpu.roll(first, 7, 0), pltpu.roll(second, 7, 0)
            before = jnp.concatenate(
                [
                    jnp.where(top, ends_ref[0, i, j : j + 1], down_first),
                    jnp.where(top, down_first, down_second),
                ],
                axis=0,
            )
            after = jnp.concatenate(
                [
                    jnp.where(bottom, up_second, up_first),
                    jnp.where(bottom, ends_ref[1, i, j : j + 1], up_second),
                ],
                axis=0,
            )
            here = jnp.concatenate([first, second], axis=0)
            tap_refs[0][i, j] = jnp.where(lower, before, swap_halves(here)).astype(BF16)
            tap_refs[1][i, j] = jnp.where(lower, swap_halves(before), here).astype(BF16)
            tap_refs[2][i, j] = after.astype(BF16)

    loop(SIDE + 2, plane, unroll)


def window(refs, planes, b):
    inner_ref, edge_ref = refs
    if b == 0:
        parts = [edge_ref[planes, 0:1], inner_ref[planes, 0 : SIDE - 1]]
    elif b == 1:
        parts = [inner_ref[planes]]
    else:
        parts = [inner_ref[planes, 1:SIDE], edge_ref[planes, 1:2]]
    return jnp.concatenate(parts, axis=1).reshape(-1, LANES)


def convolve(tap_refs, w_ref, acc_ref, first=0, planes=SIDE + 2, group=6):
    rows = group * 256

    def clear(i):
        acc_ref[i] = jnp.zeros((256, LANES), F32)

    loop(planes + 2, clear, 4)
    lower = low_half((256, LANES))

    def step(g, carry):
        start = g * group
        results = []
        for n in range(2):
            lhs = [
                window(tap_refs[chunk], pl.ds(first + start, group), b)
                for b in range(3)
                for chunk in (n, 2)
            ]
            lhs = jnp.concatenate(lhs, axis=1)
            results.append(jnp.dot(lhs, w_ref[n], preferred_element_type=F32))
        zero, one = results
        for p in range(group):
            own = slice(p * 256, (p + 1) * 256)
            z, o = zero[own], one[own]
            acc_ref[start + p + 2] += jnp.where(lower, z[:, :LANES], o[:, :LANES])
            acc_ref[start + p + 1] += swap_halves(jnp.where(lower, o[:, :LANES], z[:, :LANES]))
            acc_ref[start + p] += z[:, LANES:] + o[:, LANES:]
        return carry

    lax.fori_loop(0, planes // group, step, 0)


def taps():
    return [(t, t // 4, t // 2 % 2, t % 2) for t in range(8)]


def inner_kernel(near_ref, v_ref, zero_ref, one_ref, both_ref, core_ref, ends_ref):
    assemble_inner(near_ref, v_ref, core_ref, ends_ref)
    gather_taps(core_ref, ends_ref, (zero_ref, one_ref, both_ref), 3)


def forward_kernel(
    near_ref,
    rank_ref,
    pair_ref,
    other_ref,
    zero_ref,
    one_ref,
    both_ref,
    w_ref,
    down_ref,
    oct_ref,
    slope_ref,
    act_ref,
    zero_edge_ref,
    one_edge_ref,
    both_edge_ref,
    face_ref,
    core_ref,
    ends_ref,
    acc_ref,
    fine_ref,
):
    edges = (zero_edge_ref, one_edge_ref, both_edge_ref)
    assemble_edges(near_ref, rank_ref, pair_ref, other_ref, face_ref, core_ref, ends_ref)
    gather_taps(core_ref, ends_ref, edges, 9)
    convolve(tuple(zip((zero_ref, one_ref, both_ref), edges)), w_ref, acc_ref)

    def activate(i):
        preact = acc_ref[i + 2]
        gate = 1.0 / (1.0 + jnp.exp(-preact))
        fine_ref[i // 2, i % 2] = (preact * gate).reshape(HALF, 2, SIDE, LANES)
        slope_ref[i] = gate * (1.0 + preact * (1.0 - gate))

    loop(SIDE, activate, 4)
    for t, a, b, c in taps():
        picked = fine_ref[:, a, :, b, pl.ds(c, HALF, stride=2), :]
        act_ref[:, t * LANES : (t + 1) * LANES] = picked.reshape(512, LANES).astype(BF16)
    octants = jnp.dot(act_ref[...], down_ref[...], preferred_element_type=F32).astype(BF16)
    oct_ref[0:512] = octants[:, :LANES]
    oct_ref[512:1024] = octants[:, LANES:]


def back_kernel(
    rank_ref,
    own_ref,
    came_ref,
    down_t_ref,
    slope_ref,
    oct_ref,
    pair_ref,
    other_ref,
    g_ref,
    turned_ref,
    spun_ref,
    fine_ref,
):
    pair_ref[0:1024] = oct_ref[...]
    grads = []
    for n in range(2):
        rows = slice(n * 512, (n + 1) * 512)
        grad = own_ref[rows].astype(F32) + came_ref[rows].astype(F32)
        spun_ref[n] = grad.T.astype(BF16)
        grads.append(grad.astype(BF16))
    grads = jnp.concatenate(grads, axis=1)
    for pair in range(4):
        lanes = slice(pair * 256, (pair + 1) * 256)
        spread = jnp.dot(grads, down_t_ref[:, lanes], preferred_element_type=F32)
        for c in range(2):
            part = spread[:, c * LANES : (c + 1) * LANES].reshape(HALF, HALF, HALF, LANES)
            fine_ref[:, pair // 2, :, pair % 2, pl.ds(c, HALF, stride=2), :] = part

    for p in (0, 1, SIDE + 2, SIDE + 3):
        turned_ref[p] = jnp.zeros((LANES, 256), BF16)

    def back(i):
        grad = fine_ref[i // 2, i % 2].reshape(256, LANES) * slope_ref[i]
        turned_ref[i + 2] = grad.T.astype(BF16)
        rounded = grad.astype(BF16).reshape(SIDE, SIDE, LANES)
        g_ref[i] = rounded
        place_faces(rank_ref, i, rounded, pair_ref, other_ref, 1024)

    loop(SIDE, back, 4)


def weigh_kernel(*refs):
    rank_ref, inner, edges = refs[0], refs[1:4], refs[4:7]
    act_ref, turned_ref, spun_ref, kept_ref, sent_ref, sums_ref, total_ref = refs[7:]
    zero, one, both_taps = zip(inner, edges)
    lower = low_half((LANES, LANES))
    whole = [jnp.dot(spun_ref[n], act_ref[...], preferred_element_type=F32) for n in range(2)]
    folded = []
    for t in range(8):
        lanes = slice(t * LANES, (t + 1) * LANES)
        both = jnp.where(lower, whole[0][:, lanes], whole[1][:, lanes])
        folded.append(both + swap_halves(both))
    for t in range(4):
        rows = slice(CONV_ROWS + t * LANES, CONV_ROWS + (t + 1) * LANES)
        sums_ref[rows] = jnp.where(lower, folded[t], folded[t + 4])

    total_ref[...] = jnp.zeros_like(total_ref)

    def weigh(g, carry):
        planes = [3 * g + p for p in range(3)]
        for n, brick in enumerate((zero, one)):
            lhs = [
                jnp.concatenate(
                    [turned_ref[i + 2 - a, n * 64 : (n + 1) * 64] for a in range(3)], axis=0
                )
                for i in planes
            ]
            rhs = [
                jnp.concatenate(
                    [
                        window(refs, pl.ds(i, 1), b)
                        for refs in (brick, both_taps)
                        for b in range(3)
                    ],
                    axis=1,
                )
                for i in planes
            ]
            total_ref[n] += jnp.dot(
                jnp.concatenate(lhs, axis=1),
                jnp.concatenate(rhs, axis=0),
                preferred_element_type=F32,
            )
        return carry

    lax.fori_loop(0, (SIDE + 2) // 3, weigh, 0)
    lower = low_half((192, LANES))
    last = []
    for b in range(3):
        lanes = slice(b * LANES, (b + 1) * LANES)
        sums_ref[b * 192 : (b + 1) * 192] = total_ref[0, :, lanes] + total_ref[1, :, lanes]
        lanes = slice((3 + b) * LANES, (4 + b) * LANES)
        both = jnp.where(lower, total_ref[0, :, lanes], total_ref[1, :, lanes])
        last.append(both + swap_halves(both))
    sums_ref[576:768] = jnp.where(lower, last[0], last[1])
    sums_ref[768:960] = jnp.where(lower, last[2], 0.0)
    core = core_of(rank_ref)
    for y in range(GROUPS // 2):
        kept_ref[y] = sums_ref[share_rows(2 * y + core)]
        sent_ref[y] = sums_ref[share_rows(2 * y + 1 - core)].astype(BF16)


def core_of(rank_ref):
    return rank_ref[0] // ROWS % 2


def y_of(rank_ref):
    return rank_ref[0] // (2 * ROWS)


def share_rows(group):
    return pl.ds(pl.multiple_of(group * SHARE, 8), SHARE)


INNER_TAPS = jax.ShapeDtypeStruct((SIDE + 2, SIDE, SIDE, LANES), BF16)
EDGE_TAPS = jax.ShapeDtypeStruct((SIDE + 2, 2, SIDE, LANES), BF16)
INNER_SCRATCH = [
    pltpu.VMEM((SIDE + 2, 256, LANES), F32),
    pltpu.VMEM((2, SIDE + 2, SIDE, LANES), F32),
]
EDGE_SCRATCH = [
    pltpu.VMEM((2, SIDE, SIDE, LANES), F32),
    pltpu.VMEM((SIDE + 2, 2 * SIDE, LANES), F32),
    pltpu.VMEM((2, SIDE + 2, 8, LANES), F32),
]
ACC_SCRATCH = pltpu.VMEM((SIDE + 4, 256, LANES), F32)
FINE_SCRATCH = pltpu.VMEM((HALF, 2, HALF, 2, SIDE, LANES), F32)


def inner_call(near, v):
    return pl.pallas_call(
        inner_kernel,
        out_shape=(INNER_TAPS,) * 3,
        in_specs=[SMEM_SPEC, VMEM_SPEC],
        out_specs=(VMEM_SPEC,) * 3,
        scratch_shapes=INNER_SCRATCH,
        compiler_params=params(20),
        cost_estimate=pl.CostEstimate(
            flops=1_000_000_000, bytes_accessed=8_000_000, transcendentals=0
        ),
        name="inner",
    )(near, v)


def forward_call(near, rank, pair, other, inner, weights, down):
    return pl.pallas_call(
        forward_kernel,
        out_shape=(
            jax.ShapeDtypeStruct((1024, LANES), BF16),
            jax.ShapeDtypeStruct((SIDE, 256, LANES), F32),
            jax.ShapeDtypeStruct((512, 8 * LANES), BF16),
        )
        + (EDGE_TAPS,) * 3,
        in_specs=[SMEM_SPEC] * 2 + [VMEM_SPEC] * 7,
        out_specs=(VMEM_SPEC,) * 6,
        scratch_shapes=EDGE_SCRATCH + [ACC_SCRATCH, FINE_SCRATCH],
        compiler_params=params(28),
        cost_estimate=pl.CostEstimate(
            flops=4_000_000_000, bytes_accessed=16_000_000, transcendentals=600_000
        ),
        name="forward",
    )(near, rank, pair, other, *inner, weights, down)


def back_call(rank, own, came, down_t, slope, octants):
    return pl.pallas_call(
        back_kernel,
        out_shape=(
            jax.ShapeDtypeStruct((1280, LANES), BF16),
            jax.ShapeDtypeStruct((256, LANES), BF16),
            jax.ShapeDtypeStruct((SIDE, SIDE, SIDE, LANES), BF16),
            jax.ShapeDtypeStruct((SIDE + 4, LANES, 256), BF16),
            jax.ShapeDtypeStruct((2, LANES, 512), BF16),
        ),
        in_specs=[SMEM_SPEC] + [VMEM_SPEC] * 5,
        out_specs=(VMEM_SPEC,) * 5,
        scratch_shapes=[FINE_SCRATCH],
        compiler_params=params(24),
        cost_estimate=pl.CostEstimate(
            flops=300_000_000, bytes_accessed=8_000_000, transcendentals=0
        ),
        name="back",
    )(rank, own, came, down_t, slope, octants)


def weigh_call(rank, inner, edges, act, turned, spun):
    return pl.pallas_call(
        weigh_kernel,
        out_shape=(
            jax.ShapeDtypeStruct((GROUPS // 2, SHARE, LANES), F32),
            jax.ShapeDtypeStruct((GROUPS // 2, SHARE, LANES), BF16),
        ),
        in_specs=[SMEM_SPEC] + [VMEM_SPEC] * 9,
        out_specs=(VMEM_SPEC,) * 2,
        scratch_shapes=[
            pltpu.VMEM((CONV_ROWS + DOWN_ROWS, LANES), F32),
            pltpu.VMEM((2, 192, 768), F32),
        ],
        compiler_params=params(20),
        cost_estimate=pl.CostEstimate(
            flops=4_000_000_000, bytes_accessed=10_000_000, transcendentals=0
        ),
        name="weigh",
    )(rank, *inner, *edges, act, turned, spun)


def input_taps_kernel(after_ref, near_ref, rank_ref, g_ref, pair_ref, other_ref, *refs):
    inner, edges, token_ref = refs[:3], refs[3:6], refs[6]
    core_ref, ends_ref, face_ref, edge_core_ref, edge_ends_ref = refs[7:]
    assemble_inner(near_ref, g_ref, core_ref, ends_ref)
    gather_taps(core_ref, ends_ref, inner, 3)
    assemble_edges(
        near_ref, rank_ref, pair_ref, other_ref, face_ref, edge_core_ref, edge_ends_ref
    )
    gather_taps(edge_core_ref, edge_ends_ref, edges, 9)
    token_ref[...] = jnp.zeros_like(token_ref)


def input_taps_call(after, near, rank, g, pair, other):
    return pl.pallas_call(
        input_taps_kernel,
        out_shape=(INNER_TAPS,) * 3 + (EDGE_TAPS,) * 3 + (TOKEN,),
        in_specs=[ANY_SPEC] + [SMEM_SPEC] * 2 + [VMEM_SPEC] * 3,
        out_specs=(VMEM_SPEC,) * 7,
        scratch_shapes=INNER_SCRATCH + EDGE_SCRATCH,
        compiler_params=params(20),
        cost_estimate=pl.CostEstimate(
            flops=1_000_000_000, bytes_accessed=8_000_000, transcendentals=0
        ),
        name="input_taps",
    )(after, near, rank, g, pair, other)


def input_half_kernel(half, *refs):
    inner, edges, w_ref = refs[1:4], refs[4:7], refs[7]
    out_ref, token_ref, acc_ref = refs[-3:]
    convolve(tuple(zip(inner, edges)), w_ref, acc_ref, half * HALF, HALF + 2, 5)

    for i in range(HALF):
        out_ref[:, i * 256 : (i + 1) * 256] = acc_ref[i + 2].T.astype(BF16)
    token_ref[...] = jnp.zeros_like(token_ref)


def input_half_call(after, taps, weights, half, begun=()):
    return pl.pallas_call(
        functools.partial(input_half_kernel, half),
        grid=(1,),
        out_shape=(jax.ShapeDtypeStruct((LANES, SIDE**3), BF16), TOKEN),
        in_specs=[ANY_SPEC] + [VMEM_SPEC] * 7 + [ANY_SPEC] * len(begun),
        out_specs=(
            pl.BlockSpec((LANES, SIDE**3 // 2), lambda g: (0, half)),
            pl.BlockSpec((8, LANES), lambda g: (0, 0)),
        ),
        input_output_aliases={8: 0} if begun else {},
        scratch_shapes=[pltpu.VMEM((HALF + 4, 256, LANES), F32)],
        compiler_params=params(16),
        cost_estimate=pl.CostEstimate(
            flops=2_500_000_000, bytes_accessed=6_000_000, transcendentals=0
        ),
        name="input_half",
    )(after, *taps, weights, *begun)


def stamp_kernel(sent_ref, other_ref, out_ref):
    pass


def stamp_call(sent, other):
    return pl.pallas_call(
        stamp_kernel,
        out_shape=jax.ShapeDtypeStruct(sent.shape, sent.dtype),
        in_specs=[ANY_SPEC] * 2,
        out_specs=ANY_SPEC,
        input_output_aliases={0: 0},
        compiler_params=params(16),
        name="stamp",
    )(sent, other)


def deal_kernel(rank_ref, kept_ref, came_ref, own_ref, *refs):
    share_refs, total_ref = refs[:-1], refs[-1]
    total_ref[...] = kept_ref[...] + came_ref[...].astype(F32)
    y = y_of(rank_ref)
    own_ref[...] = total_ref[y]
    for s, share_ref in enumerate(share_refs):
        share_ref[...] = total_ref[y ^ (s + 1)].astype(BF16)


def deal_call(rank, kept, came):
    return pl.pallas_call(
        deal_kernel,
        out_shape=(jax.ShapeDtypeStruct((SHARE, LANES), F32),)
        + (jax.ShapeDtypeStruct((SHARE, LANES), BF16),) * 3,
        in_specs=[SMEM_SPEC, VMEM_SPEC, VMEM_SPEC],
        out_specs=(VMEM_SPEC,) * 4,
        scratch_shapes=[pltpu.VMEM((GROUPS // 2, SHARE, LANES), F32)],
        compiler_params=params(16),
        cost_estimate=pl.CostEstimate(flops=0, bytes_accessed=500_000, transcendentals=0),
        name="deal",
    )(rank, kept, came)


def add_kernel(after_ref, *refs):
    parts = [ref[...].astype(F32) for ref in refs[:-1]]
    while len(parts) > 1:
        parts = [first + second for first, second in zip(parts[::2], parts[1::2])]
    refs[-1][...] = parts[0].astype(refs[-1].dtype)


def add_call(after, parts, dtype=BF16):
    return pl.pallas_call(
        add_kernel,
        out_shape=jax.ShapeDtypeStruct(parts[0].shape, dtype),
        in_specs=[ANY_SPEC] + [VMEM_SPEC] * len(parts),
        out_specs=VMEM_SPEC,
        compiler_params=params(16),
        cost_estimate=pl.CostEstimate(flops=0, bytes_accessed=500_000, transcendentals=0),
        name="add",
    )(after, *parts)


def collect_kernel(after_ref, rank_ref, *refs):
    y = y_of(rank_ref)
    for s, share_ref in enumerate(refs[:-1]):
        refs[-1][y ^ s] = share_ref[...]


def collect_call(after, rank, shares):
    return pl.pallas_call(
        collect_kernel,
        out_shape=jax.ShapeDtypeStruct((GROUPS // 2, SHARE, LANES), BF16),
        in_specs=[ANY_SPEC, SMEM_SPEC] + [VMEM_SPEC] * len(shares),
        out_specs=VMEM_SPEC,
        compiler_params=params(16),
        cost_estimate=pl.CostEstimate(flops=0, bytes_accessed=500_000, transcendentals=0),
        name="collect",
    )(after, rank, *shares)


def split_kernel(rank_ref, mine_ref, theirs_ref, conv_ref, down_ref, sums_ref):
    core = core_of(rank_ref)
    for y in range(GROUPS // 2):
        sums_ref[share_rows(2 * y + core)] = mine_ref[y].astype(F32)
        sums_ref[share_rows(2 * y + 1 - core)] = theirs_ref[y].astype(F32)
    for a in range(3):
        for b in range(3):
            for c in range(3):
                chunk, upper = (b, c) if c < 2 else ((3, b) if b < 2 else (4, 0))
                base = chunk * 192 + a * 64
                block = sums_ref[base : base + 64]
                block = swap_halves(block) if upper else block
                conv_ref[9 * a + 3 * b + c] = block[:, :64]
    for t in range(4):
        block = sums_ref[CONV_ROWS + t * LANES : CONV_ROWS + (t + 1) * LANES].T
        down_ref[t] = block[:64]
        down_ref[t + 4] = block[64:]


def split_call(rank, mine, theirs):
    return pl.pallas_call(
        split_kernel,
        out_shape=(
            jax.ShapeDtypeStruct((27, 64, 64), F32),
            jax.ShapeDtypeStruct((8, 64, LANES), F32),
        ),
        in_specs=[SMEM_SPEC] + [VMEM_SPEC] * 2,
        out_specs=(VMEM_SPEC,) * 2,
        scratch_shapes=[pltpu.VMEM((CONV_ROWS + DOWN_ROWS, LANES), F32)],
        compiler_params=params(16),
        name="split",
    )(rank, mine, theirs)


def swaps(axis, step=1):
    return [(i, i ^ step) for i in range(lax.axis_size(axis))]


def swapped(array, axis, steps):
    return [lax.ppermute(array, axis, swaps(axis, step)) for step in steps]


def exchange(pair, other, axis):
    across = [(i, i + 1) for i in range(1, lax.axis_size(axis) - 1, 2)]
    return (
        lax.ppermute(pair, axis, swaps(axis)),
        lax.ppermute(other, axis, across + [(j, i) for i, j in across]),
    )


def body(fine_input, conv_weight, down_weight, coarse_cot, neighbours, children):
    dev = ("z", "x")
    rank = lax.axis_index(("y", "core", "z", "x")).reshape(1).astype(jnp.int32)

    voxels, pair, other = faces_call(rank, fine_input.reshape(LANES, SIDE**3))
    own, pair = cot_call(pair, children, rank, coarse_cot.reshape(LANES, SIDE**3))
    pair, other = exchange(pair, other, dev)
    forward, backward, down, down_t = weights_call(conv_weight, down_weight.transpose(0, 2, 1))
    inner = inner_call(neighbours, voxels)
    octants, slope, act, *edges = forward_call(
        neighbours, rank, pair, other, inner, forward, down
    )
    mine, other_out, grads, turned, spun = back_call(rank, own, pair, down_t, slope, octants)
    theirs, grad_other = exchange(mine, other_out, dev)

    kept, sent = weigh_call(rank, inner, edges, act, turned, spun)
    (came,) = swapped(stamp_call(sent, grad_other), "core", (1,))
    own, *shares = deal_call(rank, kept, came)
    came = [lax.ppermute(share, "y", swaps("y", s + 1)) for s, share in enumerate(shares)]
    *taps_in, token = input_taps_call(own, neighbours, rank, grads, theirs, grad_other)
    part = add_call(token, [own, *came], F32)
    came = swapped(part, "x", (1, 2, 3))
    input_grad, token = input_half_call(part, taps_in, backward, 0)
    part = add_call(token, [part, *came])
    came = swapped(part, "z", (1, 2, 3))
    coarse, token = coarse_half_call(part, children, rank, mine, theirs, 0)
    part = add_call(token, [part, *came])
    came = swapped(part, "z", (4,))
    input_grad, token = input_half_call(part, taps_in, backward, 1, (input_grad,))
    part = add_call(token, [part, *came])
    came = swapped(part, "y", (1, 2, 3))
    coarse, token = coarse_half_call(part, children, rank, mine, theirs, 1, (coarse,))
    shares = collect_call(token, rank, [part, *came])
    (came,) = swapped(shares, "core", (1,))
    conv_grad, down_grad = split_call(rank, shares, came)
    return (
        coarse.reshape(1, LANES, SIDE**3),
        input_grad.reshape(2, 64, SIDE**3),
        conv_grad,
        down_grad.transpose(0, 2, 1),
    )


def solution(mesh):
    grp, dev = mesh.devices.shape
    mesh = jax.sharding.Mesh(
        mesh.devices.reshape(grp // 2, 2, dev // 4, 4), ("y", "core", "z", "x")
    )
    bricks = ("y", "core", "z", "x")
    in_specs = (P(bricks, None, None), P(), P(), P(bricks, None, None), P(bricks, None), P(bricks, None))
    out_specs = (P(bricks, None, None), P(bricks, None, None), P(), P())
    return jax.shard_map(body, mesh=mesh, in_specs=in_specs, out_specs=out_specs, check_vma=False)
```

```python
import functools

import jax
import jax.numpy as jnp
from jax import lax
from jax.experimental import pallas as pl
from jax.experimental.pallas import tpu as pltpu
from jax.sharding import PartitionSpec as P

SIDE = 16
HALF = 8
LANES = 128
F32 = jnp.float32
BF16 = jnp.bfloat16
CONV_ROWS = 960
DOWN_ROWS = 512
GROUPS = 8
ROWS = 32
SHARE = (CONV_ROWS + DOWN_ROWS) // GROUPS

VMEM_SPEC = pl.BlockSpec(memory_space=pltpu.VMEM)
SMEM_SPEC = pl.BlockSpec(memory_space=pltpu.SMEM)
ANY_SPEC = pl.BlockSpec(memory_space=pl.ANY)
TOKEN = jax.ShapeDtypeStruct((8, LANES), F32)


def params(mib):
    return pltpu.CompilerParams(vmem_limit_bytes=mib * 1024 * 1024)


def loop(count, body, unroll):
    def step(g, carry):
        for p in range(unroll):
            body(g * unroll + p)
        return carry

    lax.fori_loop(0, count // unroll, step, 0)


def low_half(shape):
    return lax.broadcasted_iota(jnp.int32, shape, len(shape) - 1) < 64


def swap_halves(x):
    return pltpu.roll(x, 64, x.ndim - 1)


def place_faces(rank_ref, i, planes, pair_ref, other_ref, first=0):
    even = rank_ref[0] % 2 == 0
    low, high = planes[0], planes[SIDE - 1]
    pair_ref[pl.ds(pl.multiple_of(first + i * SIDE, SIDE), SIDE)] = jnp.where(even, high, low)
    other_ref[pl.ds(pl.multiple_of(i * SIDE, SIDE), SIDE)] = jnp.where(even, low, high)


def faces_kernel(rank_ref, x_ref, v_ref, pair_ref, other_ref, token_ref):
    def plane(i):
        columns = pl.ds(pl.multiple_of(i * 256, 256), 256)
        voxels = x_ref[:, columns].astype(F32).T.astype(BF16).reshape(SIDE, SIDE, LANES)
        v_ref[i] = voxels
        place_faces(rank_ref, i, voxels, pair_ref, other_ref)

    loop(SIDE, plane, 4)
    token_ref[...] = jnp.zeros_like(token_ref)


def faces_call(rank, x):
    face = jax.ShapeDtypeStruct((256, LANES), BF16)
    return pl.pallas_call(
        faces_kernel,
        out_shape=(jax.ShapeDtypeStruct((SIDE, SIDE, SIDE, LANES), BF16), face, face, TOKEN),
        in_specs=[SMEM_SPEC, VMEM_SPEC],
        out_specs=(VMEM_SPEC,) * 4,
        compiler_params=params(16),
        cost_estimate=pl.CostEstimate(flops=0, bytes_accessed=4_000_000, transcendentals=0),
        name="faces",
    )(rank, x)


def find_octant(child_ref, wanted):
    place = jnp.int32(0)
    found = jnp.int32(0)
    for o in range(8):
        hit = (child_ref[0, o] == wanted).astype(jnp.int32)
        place = place + hit * o
        found = found + hit
    return place, found


def cot_kernel(after_ref, child_ref, rank_ref, cot_ref, own_ref, send_ref, turned_ref):
    def plane(i):
        columns = pl.ds(pl.multiple_of(i * 256, 256), 256)
        turned = cot_ref[:, columns].astype(F32).T
        turned_ref[i // HALF, i % HALF] = turned.reshape(2, HALF, 2, HALF, LANES)

    loop(SIDE, plane, 4)
    rank = rank_ref[0]
    for out_ref, holder in ((own_ref, rank), (send_ref, rank ^ 1)):
        for slot in range(2):
            place, found = find_octant(child_ref, holder * 2 + slot)
            block = turned_ref[place // 4, :, place // 2 % 2, :, place % 2]
            block = jnp.where(found > 0, block, jnp.zeros_like(block))
            out_ref[slot * 512 : (slot + 1) * 512] = block.reshape(512, LANES).astype(BF16)


def cot_call(after, children, rank, cot):
    blocks = jax.ShapeDtypeStruct((1024, LANES), BF16)
    return pl.pallas_call(
        cot_kernel,
        out_shape=(blocks, blocks),
        in_specs=[ANY_SPEC, SMEM_SPEC, SMEM_SPEC, VMEM_SPEC],
        out_specs=(VMEM_SPEC,) * 2,
        scratch_shapes=[pltpu.VMEM((2, HALF, 2, HALF, 2, HALF, LANES), F32)],
        compiler_params=params(20),
        cost_estimate=pl.CostEstimate(flops=0, bytes_accessed=8_000_000, transcendentals=0),
        name="cot",
    )(after, children, rank, cot)


def weights_kernel(
    conv_ref, down_in_ref, forward_ref, backward_ref, down_ref, down_t_ref
):
    blank = jnp.zeros((64, 64), F32)
    for b in range(3):
        for c in range(3):
            rows = slice(b * 256 + c * 64, b * 256 + (c + 1) * 64)
            ahead = [conv_ref[9 * a + 3 * b + c].astype(F32) for a in range(3)]
            behind = [conv_ref[26 - (9 * a + 3 * b + c)].astype(F32) for a in range(3)]
            for n in range(2):
                order = (0, 1, 2, None) if n == 0 else (1, 0, None, 2)
                if c == 2:
                    rows = slice(b * 256 + 128 + n * 64, b * 256 + 192 + n * 64)
                    unused = slice(b * 256 + 192 - n * 64, b * 256 + 256 - n * 64)
                    forward_ref[n, unused] = jnp.zeros((64, 256), BF16)
                    backward_ref[n, unused] = jnp.zeros((64, 256), BF16)
                for half in range(2):
                    pair = order[2 * half : 2 * half + 2]
                    lanes = slice(half * LANES, (half + 1) * LANES)
                    taps = [blank if a is None else ahead[a] for a in pair]
                    forward_ref[n, rows, lanes] = jnp.concatenate(taps, axis=0).T.astype(BF16)
                    taps = [blank if a is None else behind[a] for a in pair]
                    backward_ref[n, rows, lanes] = jnp.concatenate(taps, axis=1).astype(BF16)
    for t in range(8):
        tap = down_in_ref[t]
        blank = jnp.zeros((64, LANES), BF16)
        rows = [jnp.concatenate([tap, blank], axis=1), jnp.concatenate([blank, tap], axis=1)]
        block = jnp.concatenate(rows, axis=0)
        down_ref[t * LANES : (t + 1) * LANES] = block
        down_t_ref[:, t * LANES : (t + 1) * LANES] = block.astype(F32).T.astype(BF16)


def weights_call(conv_weight, down_weight):
    conv = jax.ShapeDtypeStruct((2, 768, 256), BF16)
    return pl.pallas_call(
        weights_kernel,
        out_shape=(
            conv,
            conv,
            jax.ShapeDtypeStruct((8 * LANES, 256), BF16),
            jax.ShapeDtypeStruct((256, 8 * LANES), BF16),
        ),
        in_specs=[VMEM_SPEC] * 2,
        out_specs=(VMEM_SPEC,) * 4,
        compiler_params=params(16),
        cost_estimate=pl.CostEstimate(flops=0, bytes_accessed=8_000_000, transcendentals=0),
        name="weights",
    )(conv_weight, down_weight)


def coarse_half_kernel(half, *refs):
    _, child_ref, rank_ref, mine_ref, theirs_ref = refs[:5]
    out_ref, token_ref, whole_ref = refs[-3:]
    token_ref[...] = jnp.zeros_like(token_ref)
    for o in range(4):
        entry = child_ref[0, half * 4 + o]
        slot = jnp.maximum(entry, 0) % 2
        here = jnp.maximum(entry, 0) // 2 == rank_ref[0]
        rows = pl.ds(pl.multiple_of(slot * 512, 512), 512)
        block = jnp.where(here, mine_ref[rows], theirs_ref[rows])
        block = jnp.where(entry >= 0, block, jnp.zeros_like(block)).astype(F32)
        whole_ref[:, o // 2, :, o % 2] = block.reshape(HALF, HALF, HALF, LANES)

    for i in range(HALF):
        turned = whole_ref[i].reshape(256, LANES).T
        out_ref[:, i * 256 : (i + 1) * 256] = turned.astype(BF16)


def coarse_half_call(after, children, rank, mine, theirs, half, begun=()):
    return pl.pallas_call(
        functools.partial(coarse_half_kernel, half),
        grid=(1,),
        out_shape=(jax.ShapeDtypeStruct((LANES, SIDE**3), BF16), TOKEN),
        in_specs=[ANY_SPEC, SMEM_SPEC, SMEM_SPEC, VMEM_SPEC, VMEM_SPEC] + [ANY_SPEC] * len(begun),
        out_specs=(
            pl.BlockSpec((LANES, SIDE**3 // 2), lambda g: (0, half)),
            pl.BlockSpec((8, LANES), lambda g: (0, 0)),
        ),
        input_output_aliases={5: 0} if begun else {},
        scratch_shapes=[pltpu.VMEM((HALF, 2, HALF, 2, HALF, LANES), F32)],
        compiler_params=params(16),
        cost_estimate=pl.CostEstimate(flops=0, bytes_accessed=4_000_000, transcendentals=0),
        name="coarse_half",
    )(after, children, rank, mine, theirs, *begun)


def spans(step):
    if step == 0:
        return slice(1, SIDE + 1), slice(0, SIDE)
    if step == 1:
        return slice(SIDE + 1, SIDE + 2), slice(0, 1)
    return slice(0, 1), slice(SIDE - 1, SIDE)


def chooser(near_ref, column):
    lower = low_half((1, LANES))
    entries = near_ref[0, column], near_ref[1, column]
    straight = [
        jnp.logical_and(e >= 0, jnp.maximum(e, 0) % 2 == n).astype(F32)
        for n, e in enumerate(entries)
    ]
    crossed = [
        jnp.logical_and(e >= 0, jnp.maximum(e, 0) % 2 != n).astype(F32)
        for n, e in enumerate(entries)
    ]
    keep = jnp.where(lower, straight[0], straight[1])
    cross = jnp.where(lower, crossed[0], crossed[1])

    def choose(x):
        shape = (1,) * (x.ndim - 1) + (LANES,)
        return x * keep.reshape(shape) + swap_halves(x) * cross.reshape(shape)

    return choose


def offsets():
    steps = [(x, y, z) for x in (-1, 0, 1) for y in (-1, 0, 1) for z in (-1, 0, 1)]
    steps.remove((0, 0, 0))
    return list(enumerate(steps))


def assemble_inner(near_ref, v_ref, core_ref, ends_ref):
    def fill(i):
        core_ref[i + 1] = v_ref[i].astype(F32).reshape(256, LANES)

    loop(SIDE, fill, 4)
    lines = []
    for column, (step_x, step_y, step_z) in offsets():
        if step_y != 0:
            continue
        choose = chooser(near_ref, column)
        put_x, take_x = spans(step_x)
        end = 0 if step_z < 0 else 1
        strided = pl.ds(SIDE - 1 if step_z < 0 else 0, SIDE, stride=SIDE)
        if step_x == 0:
            lines.append((choose, end, strided))
        elif step_z == 0:
            core_ref[put_x.start] = choose(core_ref[take_x.start + 1])
        else:
            ends_ref[end, put_x.start] = choose(core_ref[take_x.start + 1, strided])

    def line(i):
        for choose, end, strided in lines:
            ends_ref[end, i + 1] = choose(core_ref[i + 1, strided])

    loop(SIDE, line, 4)


def assemble_edges(near_ref, rank_ref, pair_ref, other_ref, face_ref, core_ref, ends_ref):
    even = rank_ref[0] % 2 == 0
    pair = pair_ref[pair_ref.shape[0] - 256 :].astype(F32).reshape(SIDE, SIDE, LANES)
    other = other_ref[...].astype(F32).reshape(SIDE, SIDE, LANES)
    face_ref[0] = jnp.where(even, other, pair)
    face_ref[1] = jnp.where(even, pair, other)
    for column, (step_x, step_y, step_z) in offsets():
        if step_y == 0:
            continue
        choose = chooser(near_ref, column)
        put_x, take_x = spans(step_x)
        side = 0 if step_y < 0 else 1
        if step_z == 0:
            core_ref[put_x, side * SIDE : (side + 1) * SIDE] = choose(face_ref[side, take_x])
        else:
            end, row = (0, SIDE - 1) if step_z < 0 else (1, 0)
            ends_ref[end, put_x, side : side + 1] = choose(
                face_ref[side, take_x, row : row + 1]
            )


def gather_taps(core_ref, ends_ref, tap_refs, unroll):
    lower = low_half((SIDE, LANES))
    rows = lax.broadcasted_iota(jnp.int32, (8, LANES), 0)
    top, bottom = rows == 0, rows == 7

    def plane(i):
        for j in range(tap_refs[0].shape[1]):
            first = core_ref[i, j * SIDE : j * SIDE + 8]
            second = core_ref[i, j * SIDE + 8 : (j + 1) * SIDE]
            down_first, down_second = pltpu.roll(first, 1, 0), pltpu.roll(second, 1, 0)
            up_first, up_second = pltpu.roll(first, 7, 0), pltpu.roll(second, 7, 0)
            before = jnp.concatenate(
                [
                    jnp.where(top, ends_ref[0, i, j : j + 1], down_first),
                    jnp.where(top, down_first, down_second),
                ],
                axis=0,
            )
            after = jnp.concatenate(
                [
                    jnp.where(bottom, up_second, up_first),
                    jnp.where(bottom, ends_ref[1, i, j : j + 1], up_second),
                ],
                axis=0,
            )
            here = jnp.concatenate([first, second], axis=0)
            tap_refs[0][i, j] = jnp.where(lower, before, swap_halves(here)).astype(BF16)
            tap_refs[1][i, j] = jnp.where(lower, swap_halves(before), here).astype(BF16)
            tap_refs[2][i, j] = after.astype(BF16)

    loop(SIDE + 2, plane, unroll)


def window(refs, planes, b):
    inner_ref, edge_ref = refs
    if b == 0:
        parts = [edge_ref[planes, 0:1], inner_ref[planes, 0 : SIDE - 1]]
    elif b == 1:
        parts = [inner_ref[planes]]
    else:
        parts = [inner_ref[planes, 1:SIDE], edge_ref[planes, 1:2]]
    return jnp.concatenate(parts, axis=1).reshape(-1, LANES)


def convolve(tap_refs, w_ref, acc_ref, first=0, planes=SIDE + 2, group=6):
    rows = group * 256

    def clear(i):
        acc_ref[i] = jnp.zeros((256, LANES), F32)

    loop(planes + 2, clear, 4)
    lower = low_half((256, LANES))

    def step(g, carry):
        start = g * group
        results = []
        for n in range(2):
            lhs = [
                window(tap_refs[chunk], pl.ds(first + start, group), b)
                for b in range(3)
                for chunk in (n, 2)
            ]
            lhs = jnp.concatenate(lhs, axis=1)
            results.append(jnp.dot(lhs, w_ref[n], preferred_element_type=F32))
        zero, one = results
        for p in range(group):
            own = slice(p * 256, (p + 1) * 256)
            z, o = zero[own], one[own]
            acc_ref[start + p + 2] += jnp.where(lower, z[:, :LANES], o[:, :LANES])
            acc_ref[start + p + 1] += swap_halves(jnp.where(lower, o[:, :LANES], z[:, :LANES]))
            acc_ref[start + p] += z[:, LANES:] + o[:, LANES:]
        return carry

    lax.fori_loop(0, planes // group, step, 0)


def taps():
    return [(t, t // 4, t // 2 % 2, t % 2) for t in range(8)]


def inner_kernel(near_ref, v_ref, zero_ref, one_ref, both_ref, core_ref, ends_ref):
    assemble_inner(near_ref, v_ref, core_ref, ends_ref)
    gather_taps(core_ref, ends_ref, (zero_ref, one_ref, both_ref), 3)


def forward_kernel(
    near_ref,
    rank_ref,
    pair_ref,
    other_ref,
    zero_ref,
    one_ref,
    both_ref,
    w_ref,
    down_ref,
    oct_ref,
    slope_ref,
    act_ref,
    zero_edge_ref,
    one_edge_ref,
    both_edge_ref,
    face_ref,
    core_ref,
    ends_ref,
    acc_ref,
    fine_ref,
):
    edges = (zero_edge_ref, one_edge_ref, both_edge_ref)
    assemble_edges(near_ref, rank_ref, pair_ref, other_ref, face_ref, core_ref, ends_ref)
    gather_taps(core_ref, ends_ref, edges, 9)
    convolve(tuple(zip((zero_ref, one_ref, both_ref), edges)), w_ref, acc_ref)

    def activate(i):
        preact = acc_ref[i + 2]
        gate = 1.0 / (1.0 + jnp.exp(-preact))
        fine_ref[i // 2, i % 2] = (preact * gate).reshape(HALF, 2, SIDE, LANES)
        slope_ref[i] = gate * (1.0 + preact * (1.0 - gate))

    loop(SIDE, activate, 4)
    for t, a, b, c in taps():
        picked = fine_ref[:, a, :, b, pl.ds(c, HALF, stride=2), :]
        act_ref[:, t * LANES : (t + 1) * LANES] = picked.reshape(512, LANES).astype(BF16)
    octants = jnp.dot(act_ref[...], down_ref[...], preferred_element_type=F32).astype(BF16)
    oct_ref[0:512] = octants[:, :LANES]
    oct_ref[512:1024] = octants[:, LANES:]


def back_kernel(
    rank_ref,
    own_ref,
    came_ref,
    down_t_ref,
    slope_ref,
    oct_ref,
    pair_ref,
    other_ref,
    g_ref,
    turned_ref,
    spun_ref,
    fine_ref,
):
    pair_ref[0:1024] = oct_ref[...]
    grads = []
    for n in range(2):
        rows = slice(n * 512, (n + 1) * 512)
        grad = own_ref[rows].astype(F32) + came_ref[rows].astype(F32)
        spun_ref[n] = grad.T.astype(BF16)
        grads.append(grad.astype(BF16))
    grads = jnp.concatenate(grads, axis=1)
    for pair in range(4):
        lanes = slice(pair * 256, (pair + 1) * 256)
        spread = jnp.dot(grads, down_t_ref[:, lanes], preferred_element_type=F32)
        for c in range(2):
            part = spread[:, c * LANES : (c + 1) * LANES].reshape(HALF, HALF, HALF, LANES)
            fine_ref[:, pair // 2, :, pair % 2, pl.ds(c, HALF, stride=2), :] = part

    for p in (0, 1, SIDE + 2, SIDE + 3):
        turned_ref[p] = jnp.zeros((LANES, 256), BF16)

    def back(i):
        grad = fine_ref[i // 2, i % 2].reshape(256, LANES) * slope_ref[i]
        turned_ref[i + 2] = grad.T.astype(BF16)
        rounded = grad.astype(BF16).reshape(SIDE, SIDE, LANES)
        g_ref[i] = rounded
        place_faces(rank_ref, i, rounded, pair_ref, other_ref, 1024)

    loop(SIDE, back, 4)


def weigh_kernel(*refs):
    rank_ref, inner, edges = refs[0], refs[1:4], refs[4:7]
    act_ref, turned_ref, spun_ref, kept_ref, sent_ref, sums_ref, total_ref = refs[7:]
    zero, one, both_taps = zip(inner, edges)
    lower = low_half((LANES, LANES))
    whole = [jnp.dot(spun_ref[n], act_ref[...], preferred_element_type=F32) for n in range(2)]
    folded = []
    for t in range(8):
        lanes = slice(t * LANES, (t + 1) * LANES)
        both = jnp.where(lower, whole[0][:, lanes], whole[1][:, lanes])
        folded.append(both + swap_halves(both))
    for t in range(4):
        rows = slice(CONV_ROWS + t * LANES, CONV_ROWS + (t + 1) * LANES)
        sums_ref[rows] = jnp.where(lower, folded[t], folded[t + 4])

    total_ref[...] = jnp.zeros_like(total_ref)

    def weigh(g, carry):
        planes = [6 * g + p for p in range(6)]
        for n, brick in enumerate((zero, one)):
            lhs = [
                jnp.concatenate(
                    [turned_ref[i + 2 - a, n * 64 : (n + 1) * 64] for a in range(3)], axis=0
                )
                for i in planes
            ]
            rhs = [
                jnp.concatenate(
                    [
                        window(refs, pl.ds(i, 1), b)
                        for refs in (brick, both_taps)
                        for b in range(3)
                    ],
                    axis=1,
                )
                for i in planes
            ]
            total_ref[n] += jnp.dot(
                jnp.concatenate(lhs, axis=1),
                jnp.concatenate(rhs, axis=0),
                preferred_element_type=F32,
            )
        return carry

    lax.fori_loop(0, (SIDE + 2) // 6, weigh, 0)
    lower = low_half((192, LANES))
    last = []
    for b in range(3):
        lanes = slice(b * LANES, (b + 1) * LANES)
        sums_ref[b * 192 : (b + 1) * 192] = total_ref[0, :, lanes] + total_ref[1, :, lanes]
        lanes = slice((3 + b) * LANES, (4 + b) * LANES)
        both = jnp.where(lower, total_ref[0, :, lanes], total_ref[1, :, lanes])
        last.append(both + swap_halves(both))
    sums_ref[576:768] = jnp.where(lower, last[0], last[1])
    sums_ref[768:960] = jnp.where(lower, last[2], 0.0)
    core = core_of(rank_ref)
    for y in range(GROUPS // 2):
        kept_ref[y] = sums_ref[share_rows(2 * y + core)]
        sent_ref[y] = sums_ref[share_rows(2 * y + 1 - core)].astype(BF16)


def core_of(rank_ref):
    return rank_ref[0] // ROWS % 2


def y_of(rank_ref):
    return rank_ref[0] // (2 * ROWS)


def share_rows(group):
    return pl.ds(pl.multiple_of(group * SHARE, 8), SHARE)


INNER_TAPS = jax.ShapeDtypeStruct((SIDE + 2, SIDE, SIDE, LANES), BF16)
EDGE_TAPS = jax.ShapeDtypeStruct((SIDE + 2, 2, SIDE, LANES), BF16)
INNER_SCRATCH = [
    pltpu.VMEM((SIDE + 2, 256, LANES), F32),
    pltpu.VMEM((2, SIDE + 2, SIDE, LANES), F32),
]
EDGE_SCRATCH = [
    pltpu.VMEM((2, SIDE, SIDE, LANES), F32),
    pltpu.VMEM((SIDE + 2, 2 * SIDE, LANES), F32),
    pltpu.VMEM((2, SIDE + 2, 8, LANES), F32),
]
ACC_SCRATCH = pltpu.VMEM((SIDE + 4, 256, LANES), F32)
FINE_SCRATCH = pltpu.VMEM((HALF, 2, HALF, 2, SIDE, LANES), F32)


def inner_call(near, v):
    return pl.pallas_call(
        inner_kernel,
        out_shape=(INNER_TAPS,) * 3,
        in_specs=[SMEM_SPEC, VMEM_SPEC],
        out_specs=(VMEM_SPEC,) * 3,
        scratch_shapes=INNER_SCRATCH,
        compiler_params=params(20),
        cost_estimate=pl.CostEstimate(
            flops=1_000_000_000, bytes_accessed=8_000_000, transcendentals=0
        ),
        name="inner",
    )(near, v)


def forward_call(near, rank, pair, other, inner, weights, down):
    return pl.pallas_call(
        forward_kernel,
        out_shape=(
            jax.ShapeDtypeStruct((1024, LANES), BF16),
            jax.ShapeDtypeStruct((SIDE, 256, LANES), F32),
            jax.ShapeDtypeStruct((512, 8 * LANES), BF16),
        )
        + (EDGE_TAPS,) * 3,
        in_specs=[SMEM_SPEC] * 2 + [VMEM_SPEC] * 7,
        out_specs=(VMEM_SPEC,) * 6,
        scratch_shapes=EDGE_SCRATCH + [ACC_SCRATCH, FINE_SCRATCH],
        compiler_params=params(28),
        cost_estimate=pl.CostEstimate(
            flops=4_000_000_000, bytes_accessed=16_000_000, transcendentals=600_000
        ),
        name="forward",
    )(near, rank, pair, other, *inner, weights, down)


def back_call(rank, own, came, down_t, slope, octants):
    return pl.pallas_call(
        back_kernel,
        out_shape=(
            jax.ShapeDtypeStruct((1280, LANES), BF16),
            jax.ShapeDtypeStruct((256, LANES), BF16),
            jax.ShapeDtypeStruct((SIDE, SIDE, SIDE, LANES), BF16),
            jax.ShapeDtypeStruct((SIDE + 4, LANES, 256), BF16),
            jax.ShapeDtypeStruct((2, LANES, 512), BF16),
        ),
        in_specs=[SMEM_SPEC] + [VMEM_SPEC] * 5,
        out_specs=(VMEM_SPEC,) * 5,
        scratch_shapes=[FINE_SCRATCH],
        compiler_params=params(24),
        cost_estimate=pl.CostEstimate(
            flops=300_000_000, bytes_accessed=8_000_000, transcendentals=0
        ),
        name="back",
    )(rank, own, came, down_t, slope, octants)


def weigh_call(rank, inner, edges, act, turned, spun):
    return pl.pallas_call(
        weigh_kernel,
        out_shape=(
            jax.ShapeDtypeStruct((GROUPS // 2, SHARE, LANES), F32),
            jax.ShapeDtypeStruct((GROUPS // 2, SHARE, LANES), BF16),
        ),
        in_specs=[SMEM_SPEC] + [VMEM_SPEC] * 9,
        out_specs=(VMEM_SPEC,) * 2,
        scratch_shapes=[
            pltpu.VMEM((CONV_ROWS + DOWN_ROWS, LANES), F32),
            pltpu.VMEM((2, 192, 768), F32),
        ],
        compiler_params=params(20),
        cost_estimate=pl.CostEstimate(
            flops=4_000_000_000, bytes_accessed=10_000_000, transcendentals=0
        ),
        name="weigh",
    )(rank, *inner, *edges, act, turned, spun)


def input_taps_kernel(after_ref, near_ref, rank_ref, g_ref, pair_ref, other_ref, *refs):
    inner, edges, token_ref = refs[:3], refs[3:6], refs[6]
    core_ref, ends_ref, face_ref, edge_core_ref, edge_ends_ref = refs[7:]
    assemble_inner(near_ref, g_ref, core_ref, ends_ref)
    gather_taps(core_ref, ends_ref, inner, 3)
    assemble_edges(
        near_ref, rank_ref, pair_ref, other_ref, face_ref, edge_core_ref, edge_ends_ref
    )
    gather_taps(edge_core_ref, edge_ends_ref, edges, 9)
    token_ref[...] = jnp.zeros_like(token_ref)


def input_taps_call(after, near, rank, g, pair, other):
    return pl.pallas_call(
        input_taps_kernel,
        out_shape=(INNER_TAPS,) * 3 + (EDGE_TAPS,) * 3 + (TOKEN,),
        in_specs=[ANY_SPEC] + [SMEM_SPEC] * 2 + [VMEM_SPEC] * 3,
        out_specs=(VMEM_SPEC,) * 7,
        scratch_shapes=INNER_SCRATCH + EDGE_SCRATCH,
        compiler_params=params(20),
        cost_estimate=pl.CostEstimate(
            flops=1_000_000_000, bytes_accessed=8_000_000, transcendentals=0
        ),
        name="input_taps",
    )(after, near, rank, g, pair, other)


def input_half_kernel(half, *refs):
    inner, edges, w_ref = refs[1:4], refs[4:7], refs[7]
    out_ref, token_ref, acc_ref = refs[-3:]
    convolve(tuple(zip(inner, edges)), w_ref, acc_ref, half * HALF, HALF + 2, 5)

    for i in range(HALF):
        out_ref[:, i * 256 : (i + 1) * 256] = acc_ref[i + 2].T.astype(BF16)
    token_ref[...] = jnp.zeros_like(token_ref)


def input_half_call(after, taps, weights, half, begun=()):
    return pl.pallas_call(
        functools.partial(input_half_kernel, half),
        grid=(1,),
        out_shape=(jax.ShapeDtypeStruct((LANES, SIDE**3), BF16), TOKEN),
        in_specs=[ANY_SPEC] + [VMEM_SPEC] * 7 + [ANY_SPEC] * len(begun),
        out_specs=(
            pl.BlockSpec((LANES, SIDE**3 // 2), lambda g: (0, half)),
            pl.BlockSpec((8, LANES), lambda g: (0, 0)),
        ),
        input_output_aliases={8: 0} if begun else {},
        scratch_shapes=[pltpu.VMEM((HALF + 4, 256, LANES), F32)],
        compiler_params=params(16),
        cost_estimate=pl.CostEstimate(
            flops=2_500_000_000, bytes_accessed=6_000_000, transcendentals=0
        ),
        name="input_half",
    )(after, *taps, weights, *begun)


def deal_kernel(rank_ref, kept_ref, came_ref, own_ref, *refs):
    share_refs, total_ref = refs[:-1], refs[-1]
    total_ref[...] = kept_ref[...] + came_ref[...].astype(F32)
    y = y_of(rank_ref)
    own_ref[...] = total_ref[y]
    for s, share_ref in enumerate(share_refs):
        share_ref[...] = total_ref[y ^ (s + 1)].astype(BF16)


def deal_call(rank, kept, came):
    return pl.pallas_call(
        deal_kernel,
        out_shape=(jax.ShapeDtypeStruct((SHARE, LANES), F32),)
        + (jax.ShapeDtypeStruct((SHARE, LANES), BF16),) * 3,
        in_specs=[SMEM_SPEC, VMEM_SPEC, VMEM_SPEC],
        out_specs=(VMEM_SPEC,) * 4,
        scratch_shapes=[pltpu.VMEM((GROUPS // 2, SHARE, LANES), F32)],
        compiler_params=params(16),
        cost_estimate=pl.CostEstimate(flops=0, bytes_accessed=500_000, transcendentals=0),
        name="deal",
    )(rank, kept, came)


def add_kernel(after_ref, *refs):
    parts = [ref[...].astype(F32) for ref in refs[:-1]]
    while len(parts) > 1:
        parts = [first + second for first, second in zip(parts[::2], parts[1::2])]
    refs[-1][...] = parts[0].astype(refs[-1].dtype)


def add_call(after, parts, dtype=BF16):
    return pl.pallas_call(
        add_kernel,
        out_shape=jax.ShapeDtypeStruct(parts[0].shape, dtype),
        in_specs=[ANY_SPEC] + [VMEM_SPEC] * len(parts),
        out_specs=VMEM_SPEC,
        compiler_params=params(16),
        cost_estimate=pl.CostEstimate(flops=0, bytes_accessed=500_000, transcendentals=0),
        name="add",
    )(after, *parts)


def collect_kernel(after_ref, rank_ref, *refs):
    y = y_of(rank_ref)
    for s, share_ref in enumerate(refs[:-1]):
        refs[-1][y ^ s] = share_ref[...]


def collect_call(after, rank, shares):
    return pl.pallas_call(
        collect_kernel,
        out_shape=jax.ShapeDtypeStruct((GROUPS // 2, SHARE, LANES), BF16),
        in_specs=[ANY_SPEC, SMEM_SPEC] + [VMEM_SPEC] * len(shares),
        out_specs=VMEM_SPEC,
        compiler_params=params(16),
        cost_estimate=pl.CostEstimate(flops=0, bytes_accessed=500_000, transcendentals=0),
        name="collect",
    )(after, rank, *shares)


def split_kernel(rank_ref, mine_ref, theirs_ref, conv_ref, down_ref, sums_ref):
    core = core_of(rank_ref)
    for y in range(GROUPS // 2):
        sums_ref[share_rows(2 * y + core)] = mine_ref[y].astype(F32)
        sums_ref[share_rows(2 * y + 1 - core)] = theirs_ref[y].astype(F32)
    for a in range(3):
        for b in range(3):
            for c in range(3):
                chunk, upper = (b, c) if c < 2 else ((3, b) if b < 2 else (4, 0))
                base = chunk * 192 + a * 64
                block = sums_ref[base : base + 64]
                block = swap_halves(block) if upper else block
                conv_ref[9 * a + 3 * b + c] = block[:, :64]
    for t in range(4):
        block = sums_ref[CONV_ROWS + t * LANES : CONV_ROWS + (t + 1) * LANES].T
        down_ref[t] = block[:64]
        down_ref[t + 4] = block[64:]


def split_call(rank, mine, theirs):
    return pl.pallas_call(
        split_kernel,
        out_shape=(
            jax.ShapeDtypeStruct((27, 64, 64), F32),
            jax.ShapeDtypeStruct((8, 64, LANES), F32),
        ),
        in_specs=[SMEM_SPEC] + [VMEM_SPEC] * 2,
        out_specs=(VMEM_SPEC,) * 2,
        scratch_shapes=[pltpu.VMEM((CONV_ROWS + DOWN_ROWS, LANES), F32)],
        compiler_params=params(16),
        name="split",
    )(rank, mine, theirs)


def swaps(axis, step=1):
    return [(i, i ^ step) for i in range(lax.axis_size(axis))]


def swapped(array, axis, steps):
    return [lax.ppermute(array, axis, swaps(axis, step)) for step in steps]


def exchange(pair, other):
    bricks = ("y", "core", "z", "x")
    rows = lax.axis_size(("z", "x"))
    across = []
    for device in range(lax.axis_size(bricks)):
        row = device % rows
        if row in (0, rows - 1):
            across.append((device, device ^ rows))
        else:
            across.append((device, device + 1 if row % 2 else device - 1))
    return lax.ppermute(pair, ("z", "x"), swaps(("z", "x"))), lax.ppermute(other, bricks, across)


def body(fine_input, conv_weight, down_weight, coarse_cot, neighbours, children):
    dev = ("z", "x")
    rank = lax.axis_index(("y", "core", "z", "x")).reshape(1).astype(jnp.int32)

    voxels, pair, other, token = faces_call(rank, fine_input.reshape(LANES, SIDE**3))
    own, send = cot_call(token, children, rank, coarse_cot.reshape(LANES, SIDE**3))
    pair, other = exchange(pair, other)
    came = lax.ppermute(send, dev, swaps(dev))
    forward, backward, down, down_t = weights_call(conv_weight, down_weight.transpose(0, 2, 1))
    inner = inner_call(neighbours, voxels)
    octants, slope, act, *edges = forward_call(
        neighbours, rank, pair, other, inner, forward, down
    )
    mine, other_out, grads, turned, spun = back_call(rank, own, came, down_t, slope, octants)
    theirs, grad_other = exchange(mine, other_out)

    kept, sent = weigh_call(rank, inner, edges, act, turned, spun)
    (came,) = swapped(sent, "core", (1,))
    own, *shares = deal_call(rank, kept, came)
    came = [lax.ppermute(share, "y", swaps("y", s + 1)) for s, share in enumerate(shares)]
    *taps_in, token = input_taps_call(own, neighbours, rank, grads, theirs, grad_other)
    part = add_call(token, [own, *came], F32)
    came = swapped(part, "x", (1, 2, 3))
    input_grad, token = input_half_call(part, taps_in, backward, 0)
    part = add_call(token, [part, *came])
    came = swapped(part, "z", (1, 2, 3))
    coarse, token = coarse_half_call(part, children, rank, mine, theirs, 0)
    part = add_call(token, [part, *came])
    came = swapped(part, "z", (4,))
    input_grad, token = input_half_call(part, taps_in, backward, 1, (input_grad,))
    part = add_call(token, [part, *came])
    came = swapped(part, "y", (1, 2, 3))
    coarse, token = coarse_half_call(part, children, rank, mine, theirs, 1, (coarse,))
    shares = collect_call(token, rank, [part, *came])
    (came,) = swapped(shares, "core", (1,))
    conv_grad, down_grad = split_call(rank, shares, came)
    return (
        coarse.reshape(1, LANES, SIDE**3),
        input_grad.reshape(2, 64, SIDE**3),
        conv_grad,
        down_grad.transpose(0, 2, 1),
    )


def solution(mesh):
    grp, dev = mesh.devices.shape
    mesh = jax.sharding.Mesh(
        mesh.devices.reshape(grp // 2, 2, dev // 4, 4), ("y", "core", "z", "x")
    )
    bricks = ("y", "core", "z", "x")
    in_specs = (P(bricks, None, None), P(), P(), P(bricks, None, None), P(bricks, None), P(bricks, None))
    out_specs = (P(bricks, None, None), P(bricks, None, None), P(), P())
    return jax.shard_map(body, mesh=mesh, in_specs=in_specs, out_specs=out_specs, check_vma=False)
```

```python
import functools

import jax
import jax.numpy as jnp
from jax import lax
from jax.experimental import pallas as pl
from jax.experimental.pallas import tpu as pltpu
from jax.sharding import PartitionSpec as P

SIDE = 16
HALF = 8
LANES = 128
F32 = jnp.float32
BF16 = jnp.bfloat16
CONV_ROWS = 960
DOWN_ROWS = 512
GROUPS = 8
ROWS = 32
SHARE = (CONV_ROWS + DOWN_ROWS) // GROUPS

VMEM_SPEC = pl.BlockSpec(memory_space=pltpu.VMEM)
SMEM_SPEC = pl.BlockSpec(memory_space=pltpu.SMEM)
ANY_SPEC = pl.BlockSpec(memory_space=pl.ANY)
TOKEN = jax.ShapeDtypeStruct((8, LANES), F32)


def params(mib):
    return pltpu.CompilerParams(vmem_limit_bytes=mib * 1024 * 1024)


def loop(count, body, unroll):
    def step(g, carry):
        for p in range(unroll):
            body(g * unroll + p)
        return carry

    lax.fori_loop(0, count // unroll, step, 0)


def low_half(shape):
    return lax.broadcasted_iota(jnp.int32, shape, len(shape) - 1) < 64


def swap_halves(x):
    return pltpu.roll(x, 64, x.ndim - 1)


def place_faces(rank_ref, i, planes, pair_ref, other_ref, first=0):
    even = rank_ref[0] % 2 == 0
    low, high = planes[0], planes[SIDE - 1]
    pair_ref[pl.ds(pl.multiple_of(first + i * SIDE, SIDE), SIDE)] = jnp.where(even, high, low)
    other_ref[pl.ds(pl.multiple_of(i * SIDE, SIDE), SIDE)] = jnp.where(even, low, high)


def faces_kernel(rank_ref, x_ref, v_ref, pair_ref, other_ref, token_ref):
    def plane(i):
        columns = pl.ds(pl.multiple_of(i * 256, 256), 256)
        voxels = x_ref[:, columns].astype(F32).T.astype(BF16).reshape(SIDE, SIDE, LANES)
        v_ref[i] = voxels
        place_faces(rank_ref, i, voxels, pair_ref, other_ref)

    loop(SIDE, plane, 4)
    token_ref[...] = jnp.zeros_like(token_ref)


def faces_call(rank, x):
    face = jax.ShapeDtypeStruct((256, LANES), BF16)
    return pl.pallas_call(
        faces_kernel,
        out_shape=(jax.ShapeDtypeStruct((SIDE, SIDE, SIDE, LANES), BF16), face, face, TOKEN),
        in_specs=[SMEM_SPEC, VMEM_SPEC],
        out_specs=(VMEM_SPEC,) * 4,
        compiler_params=params(16),
        cost_estimate=pl.CostEstimate(flops=0, bytes_accessed=4_000_000, transcendentals=0),
        name="faces",
    )(rank, x)


def find_octant(child_ref, wanted):
    place = jnp.int32(0)
    found = jnp.int32(0)
    for o in range(8):
        hit = (child_ref[0, o] == wanted).astype(jnp.int32)
        place = place + hit * o
        found = found + hit
    return place, found


def cot_kernel(after_ref, child_ref, rank_ref, cot_ref, own_ref, send_ref, turned_ref):
    def plane(i):
        columns = pl.ds(pl.multiple_of(i * 256, 256), 256)
        turned = cot_ref[:, columns].astype(F32).T
        turned_ref[i // HALF, i % HALF] = turned.reshape(2, HALF, 2, HALF, LANES)

    loop(SIDE, plane, 4)
    rank = rank_ref[0]
    for out_ref, holder in ((own_ref, rank), (send_ref, rank ^ 1)):
        for slot in range(2):
            place, found = find_octant(child_ref, holder * 2 + slot)
            block = turned_ref[place // 4, :, place // 2 % 2, :, place % 2]
            block = jnp.where(found > 0, block, jnp.zeros_like(block))
            out_ref[slot * 512 : (slot + 1) * 512] = block.reshape(512, LANES).astype(BF16)


def cot_call(after, children, rank, cot):
    blocks = jax.ShapeDtypeStruct((1024, LANES), BF16)
    return pl.pallas_call(
        cot_kernel,
        out_shape=(blocks, blocks),
        in_specs=[ANY_SPEC, SMEM_SPEC, SMEM_SPEC, VMEM_SPEC],
        out_specs=(VMEM_SPEC,) * 2,
        scratch_shapes=[pltpu.VMEM((2, HALF, 2, HALF, 2, HALF, LANES), F32)],
        compiler_params=params(20),
        cost_estimate=pl.CostEstimate(flops=0, bytes_accessed=8_000_000, transcendentals=0),
        name="cot",
    )(after, children, rank, cot)


def weights_kernel(
    conv_ref, down_in_ref, forward_ref, backward_ref, down_ref, down_t_ref
):
    blank = jnp.zeros((64, 64), F32)
    for b in range(3):
        for c in range(3):
            rows = slice(b * 256 + c * 64, b * 256 + (c + 1) * 64)
            ahead = [conv_ref[9 * a + 3 * b + c].astype(F32) for a in range(3)]
            behind = [conv_ref[26 - (9 * a + 3 * b + c)].astype(F32) for a in range(3)]
            for n in range(2):
                order = (0, 1, 2, None) if n == 0 else (1, 0, None, 2)
                if c == 2:
                    rows = slice(b * 256 + 128 + n * 64, b * 256 + 192 + n * 64)
                    unused = slice(b * 256 + 192 - n * 64, b * 256 + 256 - n * 64)
                    forward_ref[n, unused] = jnp.zeros((64, 256), BF16)
                    backward_ref[n, unused] = jnp.zeros((64, 256), BF16)
                for half in range(2):
                    pair = order[2 * half : 2 * half + 2]
                    lanes = slice(half * LANES, (half + 1) * LANES)
                    taps = [blank if a is None else ahead[a] for a in pair]
                    forward_ref[n, rows, lanes] = jnp.concatenate(taps, axis=0).T.astype(BF16)
                    taps = [blank if a is None else behind[a] for a in pair]
                    backward_ref[n, rows, lanes] = jnp.concatenate(taps, axis=1).astype(BF16)
    for t in range(8):
        tap = down_in_ref[t]
        blank = jnp.zeros((64, LANES), BF16)
        rows = [jnp.concatenate([tap, blank], axis=1), jnp.concatenate([blank, tap], axis=1)]
        block = jnp.concatenate(rows, axis=0)
        down_ref[t * LANES : (t + 1) * LANES] = block
        down_t_ref[:, t * LANES : (t + 1) * LANES] = block.astype(F32).T.astype(BF16)


def weights_call(conv_weight, down_weight):
    conv = jax.ShapeDtypeStruct((2, 768, 256), BF16)
    return pl.pallas_call(
        weights_kernel,
        out_shape=(
            conv,
            conv,
            jax.ShapeDtypeStruct((8 * LANES, 256), BF16),
            jax.ShapeDtypeStruct((256, 8 * LANES), BF16),
        ),
        in_specs=[VMEM_SPEC] * 2,
        out_specs=(VMEM_SPEC,) * 4,
        compiler_params=params(16),
        cost_estimate=pl.CostEstimate(flops=0, bytes_accessed=8_000_000, transcendentals=0),
        name="weights",
    )(conv_weight, down_weight)


def coarse_half_kernel(half, *refs):
    _, child_ref, rank_ref, mine_ref, theirs_ref = refs[:5]
    out_ref, token_ref, whole_ref = refs[-3:]
    token_ref[...] = jnp.zeros_like(token_ref)
    for o in range(4):
        entry = child_ref[0, half * 4 + o]
        slot = jnp.maximum(entry, 0) % 2
        here = jnp.maximum(entry, 0) // 2 == rank_ref[0]
        rows = pl.ds(pl.multiple_of(slot * 512, 512), 512)
        block = jnp.where(here, mine_ref[rows], theirs_ref[rows])
        block = jnp.where(entry >= 0, block, jnp.zeros_like(block)).astype(F32)
        whole_ref[:, o // 2, :, o % 2] = block.reshape(HALF, HALF, HALF, LANES)

    for i in range(HALF):
        turned = whole_ref[i].reshape(256, LANES).T
        out_ref[:, i * 256 : (i + 1) * 256] = turned.astype(BF16)


def coarse_half_call(after, children, rank, mine, theirs, half, begun=()):
    return pl.pallas_call(
        functools.partial(coarse_half_kernel, half),
        grid=(1,),
        out_shape=(jax.ShapeDtypeStruct((LANES, SIDE**3), BF16), TOKEN),
        in_specs=[ANY_SPEC, SMEM_SPEC, SMEM_SPEC, VMEM_SPEC, VMEM_SPEC] + [ANY_SPEC] * len(begun),
        out_specs=(
            pl.BlockSpec((LANES, SIDE**3 // 2), lambda g: (0, half)),
            pl.BlockSpec((8, LANES), lambda g: (0, 0)),
        ),
        input_output_aliases={5: 0} if begun else {},
        scratch_shapes=[pltpu.VMEM((HALF, 2, HALF, 2, HALF, LANES), F32)],
        compiler_params=params(16),
        cost_estimate=pl.CostEstimate(flops=0, bytes_accessed=4_000_000, transcendentals=0),
        name="coarse_half",
    )(after, children, rank, mine, theirs, *begun)


def spans(step):
    if step == 0:
        return slice(1, SIDE + 1), slice(0, SIDE)
    if step == 1:
        return slice(SIDE + 1, SIDE + 2), slice(0, 1)
    return slice(0, 1), slice(SIDE - 1, SIDE)


def chooser(near_ref, column):
    lower = low_half((1, LANES))
    entries = near_ref[0, column], near_ref[1, column]
    straight = [
        jnp.logical_and(e >= 0, jnp.maximum(e, 0) % 2 == n).astype(F32)
        for n, e in enumerate(entries)
    ]
    crossed = [
        jnp.logical_and(e >= 0, jnp.maximum(e, 0) % 2 != n).astype(F32)
        for n, e in enumerate(entries)
    ]
    keep = jnp.where(lower, straight[0], straight[1])
    cross = jnp.where(lower, crossed[0], crossed[1])

    def choose(x):
        shape = (1,) * (x.ndim - 1) + (LANES,)
        return x * keep.reshape(shape) + swap_halves(x) * cross.reshape(shape)

    return choose


def offsets():
    steps = [(x, y, z) for x in (-1, 0, 1) for y in (-1, 0, 1) for z in (-1, 0, 1)]
    steps.remove((0, 0, 0))
    return list(enumerate(steps))


def assemble_inner(near_ref, v_ref, core_ref, ends_ref):
    def fill(i):
        core_ref[i + 1] = v_ref[i].astype(F32).reshape(256, LANES)

    loop(SIDE, fill, 4)
    lines = []
    for column, (step_x, step_y, step_z) in offsets():
        if step_y != 0:
            continue
        choose = chooser(near_ref, column)
        put_x, take_x = spans(step_x)
        end = 0 if step_z < 0 else 1
        strided = pl.ds(SIDE - 1 if step_z < 0 else 0, SIDE, stride=SIDE)
        if step_x == 0:
            lines.append((choose, end, strided))
        elif step_z == 0:
            core_ref[put_x.start] = choose(core_ref[take_x.start + 1])
        else:
            ends_ref[end, put_x.start] = choose(core_ref[take_x.start + 1, strided])

    def line(i):
        for choose, end, strided in lines:
            ends_ref[end, i + 1] = choose(core_ref[i + 1, strided])

    loop(SIDE, line, 4)


def assemble_edges(near_ref, rank_ref, pair_ref, other_ref, face_ref, core_ref, ends_ref):
    even = rank_ref[0] % 2 == 0
    pair = pair_ref[pair_ref.shape[0] - 256 :].astype(F32).reshape(SIDE, SIDE, LANES)
    other = other_ref[...].astype(F32).reshape(SIDE, SIDE, LANES)
    face_ref[0] = jnp.where(even, other, pair)
    face_ref[1] = jnp.where(even, pair, other)
    for column, (step_x, step_y, step_z) in offsets():
        if step_y == 0:
            continue
        choose = chooser(near_ref, column)
        put_x, take_x = spans(step_x)
        side = 0 if step_y < 0 else 1
        if step_z == 0:
            core_ref[put_x, side * SIDE : (side + 1) * SIDE] = choose(face_ref[side, take_x])
        else:
            end, row = (0, SIDE - 1) if step_z < 0 else (1, 0)
            ends_ref[end, put_x, side : side + 1] = choose(
                face_ref[side, take_x, row : row + 1]
            )


def gather_taps(core_ref, ends_ref, tap_refs, unroll):
    lower = low_half((SIDE, LANES))
    rows = lax.broadcasted_iota(jnp.int32, (8, LANES), 0)
    top, bottom = rows == 0, rows == 7

    def plane(i):
        for j in range(tap_refs[0].shape[1]):
            first = core_ref[i, j * SIDE : j * SIDE + 8]
            second = core_ref[i, j * SIDE + 8 : (j + 1) * SIDE]
            down_first, down_second = pltpu.roll(first, 1, 0), pltpu.roll(second, 1, 0)
            up_first, up_second = pltpu.roll(first, 7, 0), pltpu.roll(second, 7, 0)
            before = jnp.concatenate(
                [
                    jnp.where(top, ends_ref[0, i, j : j + 1], down_first),
                    jnp.where(top, down_first, down_second),
                ],
                axis=0,
            )
            after = jnp.concatenate(
                [
                    jnp.where(bottom, up_second, up_first),
                    jnp.where(bottom, ends_ref[1, i, j : j + 1], up_second),
                ],
                axis=0,
            )
            here = jnp.concatenate([first, second], axis=0)
            tap_refs[0][i, j] = jnp.where(lower, before, swap_halves(here)).astype(BF16)
            tap_refs[1][i, j] = jnp.where(lower, swap_halves(before), here).astype(BF16)
            tap_refs[2][i, j] = after.astype(BF16)

    loop(SIDE + 2, plane, unroll)


def window(refs, planes, b):
    inner_ref, edge_ref = refs
    if b == 0:
        parts = [edge_ref[planes, 0:1], inner_ref[planes, 0 : SIDE - 1]]
    elif b == 1:
        parts = [inner_ref[planes]]
    else:
        parts = [inner_ref[planes, 1:SIDE], edge_ref[planes, 1:2]]
    return jnp.concatenate(parts, axis=1).reshape(-1, LANES)


def convolve(tap_refs, w_ref, acc_ref, first=0, planes=SIDE + 2, group=9):
    rows = group * 256

    def clear(i):
        acc_ref[i] = jnp.zeros((256, LANES), F32)

    loop(planes + 2, clear, 4)
    lower = low_half((256, LANES))

    def step(g, carry):
        start = g * group
        results = []
        for n in range(2):
            lhs = [
                window(tap_refs[chunk], pl.ds(first + start, group), b)
                for b in range(3)
                for chunk in (n, 2)
            ]
            lhs = jnp.concatenate(lhs, axis=1)
            results.append(jnp.dot(lhs, w_ref[n], preferred_element_type=F32))
        zero, one = results
        for p in range(group):
            own = slice(p * 256, (p + 1) * 256)
            z, o = zero[own], one[own]
            acc_ref[start + p + 2] += jnp.where(lower, z[:, :LANES], o[:, :LANES])
            acc_ref[start + p + 1] += swap_halves(jnp.where(lower, o[:, :LANES], z[:, :LANES]))
            acc_ref[start + p] += z[:, LANES:] + o[:, LANES:]
        return carry

    lax.fori_loop(0, planes // group, step, 0)


def taps():
    return [(t, t // 4, t // 2 % 2, t % 2) for t in range(8)]


def inner_kernel(near_ref, v_ref, zero_ref, one_ref, both_ref, core_ref, ends_ref):
    assemble_inner(near_ref, v_ref, core_ref, ends_ref)
    gather_taps(core_ref, ends_ref, (zero_ref, one_ref, both_ref), 6)


def forward_kernel(
    near_ref,
    rank_ref,
    pair_ref,
    other_ref,
    zero_ref,
    one_ref,
    both_ref,
    w_ref,
    down_ref,
    oct_ref,
    slope_ref,
    act_ref,
    zero_edge_ref,
    one_edge_ref,
    both_edge_ref,
    face_ref,
    core_ref,
    ends_ref,
    acc_ref,
    fine_ref,
):
    edges = (zero_edge_ref, one_edge_ref, both_edge_ref)
    assemble_edges(near_ref, rank_ref, pair_ref, other_ref, face_ref, core_ref, ends_ref)
    gather_taps(core_ref, ends_ref, edges, 18)
    convolve(tuple(zip((zero_ref, one_ref, both_ref), edges)), w_ref, acc_ref)

    def activate(i):
        preact = acc_ref[i + 2]
        gate = 1.0 / (1.0 + jnp.exp(-preact))
        fine_ref[i // 2, i % 2] = (preact * gate).reshape(HALF, 2, SIDE, LANES)
        slope_ref[i] = gate * (1.0 + preact * (1.0 - gate))

    loop(SIDE, activate, 8)
    for t, a, b, c in taps():
        picked = fine_ref[:, a, :, b, pl.ds(c, HALF, stride=2), :]
        act_ref[:, t * LANES : (t + 1) * LANES] = picked.reshape(512, LANES).astype(BF16)
    octants = jnp.dot(act_ref[...], down_ref[...], preferred_element_type=F32).astype(BF16)
    oct_ref[0:512] = octants[:, :LANES]
    oct_ref[512:1024] = octants[:, LANES:]


def back_kernel(
    rank_ref,
    own_ref,
    came_ref,
    down_t_ref,
    slope_ref,
    oct_ref,
    pair_ref,
    other_ref,
    g_ref,
    turned_ref,
    spun_ref,
    fine_ref,
):
    pair_ref[0:1024] = oct_ref[...]
    grads = []
    for n in range(2):
        rows = slice(n * 512, (n + 1) * 512)
        grad = own_ref[rows].astype(F32) + came_ref[rows].astype(F32)
        spun_ref[n] = grad.T.astype(BF16)
        grads.append(grad.astype(BF16))
    grads = jnp.concatenate(grads, axis=1)
    for pair in range(4):
        lanes = slice(pair * 256, (pair + 1) * 256)
        spread = jnp.dot(grads, down_t_ref[:, lanes], preferred_element_type=F32)
        for c in range(2):
            part = spread[:, c * LANES : (c + 1) * LANES].reshape(HALF, HALF, HALF, LANES)
            fine_ref[:, pair // 2, :, pair % 2, pl.ds(c, HALF, stride=2), :] = part

    for p in (0, 1, SIDE + 2, SIDE + 3):
        turned_ref[p] = jnp.zeros((LANES, 256), BF16)

    def back(i):
        grad = fine_ref[i // 2, i % 2].reshape(256, LANES) * slope_ref[i]
        turned_ref[i + 2] = grad.T.astype(BF16)
        rounded = grad.astype(BF16).reshape(SIDE, SIDE, LANES)
        g_ref[i] = rounded
        place_faces(rank_ref, i, rounded, pair_ref, other_ref, 1024)

    loop(SIDE, back, 8)


def weigh_kernel(*refs):
    rank_ref, inner, edges = refs[0], refs[1:4], refs[4:7]
    act_ref, turned_ref, spun_ref, kept_ref, sent_ref, sums_ref, total_ref = refs[7:]
    zero, one, both_taps = zip(inner, edges)
    lower = low_half((LANES, LANES))
    whole = [jnp.dot(spun_ref[n], act_ref[...], preferred_element_type=F32) for n in range(2)]
    folded = []
    for t in range(8):
        lanes = slice(t * LANES, (t + 1) * LANES)
        both = jnp.where(lower, whole[0][:, lanes], whole[1][:, lanes])
        folded.append(both + swap_halves(both))
    for t in range(4):
        rows = slice(CONV_ROWS + t * LANES, CONV_ROWS + (t + 1) * LANES)
        sums_ref[rows] = jnp.where(lower, folded[t], folded[t + 4])

    total_ref[...] = jnp.zeros_like(total_ref)

    def weigh(g, carry):
        planes = [9 * g + p for p in range(9)]
        for n, brick in enumerate((zero, one)):
            lhs = [
                jnp.concatenate(
                    [turned_ref[i + 2 - a, n * 64 : (n + 1) * 64] for a in range(3)], axis=0
                )
                for i in planes
            ]
            rhs = [
                jnp.concatenate(
                    [
                        window(refs, pl.ds(i, 1), b)
                        for refs in (brick, both_taps)
                        for b in range(3)
                    ],
                    axis=1,
                )
                for i in planes
            ]
            total_ref[n] += jnp.dot(
                jnp.concatenate(lhs, axis=1),
                jnp.concatenate(rhs, axis=0),
                preferred_element_type=F32,
            )
        return carry

    lax.fori_loop(0, (SIDE + 2) // 9, weigh, 0)
    lower = low_half((192, LANES))
    last = []
    for b in range(3):
        lanes = slice(b * LANES, (b + 1) * LANES)
        sums_ref[b * 192 : (b + 1) * 192] = total_ref[0, :, lanes] + total_ref[1, :, lanes]
        lanes = slice((3 + b) * LANES, (4 + b) * LANES)
        both = jnp.where(lower, total_ref[0, :, lanes], total_ref[1, :, lanes])
        last.append(both + swap_halves(both))
    sums_ref[576:768] = jnp.where(lower, last[0], last[1])
    sums_ref[768:960] = jnp.where(lower, last[2], 0.0)
    core = core_of(rank_ref)
    for y in range(GROUPS // 2):
        kept_ref[y] = sums_ref[share_rows(2 * y + core)]
        sent_ref[y] = sums_ref[share_rows(2 * y + 1 - core)].astype(BF16)


def core_of(rank_ref):
    return rank_ref[0] // ROWS % 2


def y_of(rank_ref):
    return rank_ref[0] // (2 * ROWS)


def share_rows(group):
    return pl.ds(pl.multiple_of(group * SHARE, 8), SHARE)


INNER_TAPS = jax.ShapeDtypeStruct((SIDE + 2, SIDE, SIDE, LANES), BF16)
EDGE_TAPS = jax.ShapeDtypeStruct((SIDE + 2, 2, SIDE, LANES), BF16)
INNER_SCRATCH = [
    pltpu.VMEM((SIDE + 2, 256, LANES), F32),
    pltpu.VMEM((2, SIDE + 2, SIDE, LANES), F32),
]
EDGE_SCRATCH = [
    pltpu.VMEM((2, SIDE, SIDE, LANES), F32),
    pltpu.VMEM((SIDE + 2, 2 * SIDE, LANES), F32),
    pltpu.VMEM((2, SIDE + 2, 8, LANES), F32),
]
ACC_SCRATCH = pltpu.VMEM((SIDE + 4, 256, LANES), F32)
FINE_SCRATCH = pltpu.VMEM((HALF, 2, HALF, 2, SIDE, LANES), F32)


def inner_call(near, v):
    return pl.pallas_call(
        inner_kernel,
        out_shape=(INNER_TAPS,) * 3,
        in_specs=[SMEM_SPEC, VMEM_SPEC],
        out_specs=(VMEM_SPEC,) * 3,
        scratch_shapes=INNER_SCRATCH,
        compiler_params=params(20),
        cost_estimate=pl.CostEstimate(
            flops=1_000_000_000, bytes_accessed=8_000_000, transcendentals=0
        ),
        name="inner",
    )(near, v)


def forward_call(near, rank, pair, other, inner, weights, down):
    return pl.pallas_call(
        forward_kernel,
        out_shape=(
            jax.ShapeDtypeStruct((1024, LANES), BF16),
            jax.ShapeDtypeStruct((SIDE, 256, LANES), F32),
            jax.ShapeDtypeStruct((512, 8 * LANES), BF16),
        )
        + (EDGE_TAPS,) * 3,
        in_specs=[SMEM_SPEC] * 2 + [VMEM_SPEC] * 7,
        out_specs=(VMEM_SPEC,) * 6,
        scratch_shapes=EDGE_SCRATCH + [ACC_SCRATCH, FINE_SCRATCH],
        compiler_params=params(28),
        cost_estimate=pl.CostEstimate(
            flops=4_000_000_000, bytes_accessed=16_000_000, transcendentals=600_000
        ),
        name="forward",
    )(near, rank, pair, other, *inner, weights, down)


def back_call(rank, own, came, down_t, slope, octants):
    return pl.pallas_call(
        back_kernel,
        out_shape=(
            jax.ShapeDtypeStruct((1280, LANES), BF16),
            jax.ShapeDtypeStruct((256, LANES), BF16),
            jax.ShapeDtypeStruct((SIDE, SIDE, SIDE, LANES), BF16),
            jax.ShapeDtypeStruct((SIDE + 4, LANES, 256), BF16),
            jax.ShapeDtypeStruct((2, LANES, 512), BF16),
        ),
        in_specs=[SMEM_SPEC] + [VMEM_SPEC] * 5,
        out_specs=(VMEM_SPEC,) * 5,
        scratch_shapes=[FINE_SCRATCH],
        compiler_params=params(24),
        cost_estimate=pl.CostEstimate(
            flops=300_000_000, bytes_accessed=8_000_000, transcendentals=0
        ),
        name="back",
    )(rank, own, came, down_t, slope, octants)


def weigh_call(rank, inner, edges, act, turned, spun):
    return pl.pallas_call(
        weigh_kernel,
        out_shape=(
            jax.ShapeDtypeStruct((GROUPS // 2, SHARE, LANES), F32),
            jax.ShapeDtypeStruct((GROUPS // 2, SHARE, LANES), BF16),
        ),
        in_specs=[SMEM_SPEC] + [VMEM_SPEC] * 9,
        out_specs=(VMEM_SPEC,) * 2,
        scratch_shapes=[
            pltpu.VMEM((CONV_ROWS + DOWN_ROWS, LANES), F32),
            pltpu.VMEM((2, 192, 768), F32),
        ],
        compiler_params=params(20),
        cost_estimate=pl.CostEstimate(
            flops=4_000_000_000, bytes_accessed=10_000_000, transcendentals=0
        ),
        name="weigh",
    )(rank, *inner, *edges, act, turned, spun)


def input_taps_kernel(after_ref, near_ref, rank_ref, g_ref, pair_ref, other_ref, *refs):
    inner, edges, token_ref = refs[:3], refs[3:6], refs[6]
    core_ref, ends_ref, face_ref, edge_core_ref, edge_ends_ref = refs[7:]
    assemble_inner(near_ref, g_ref, core_ref, ends_ref)
    gather_taps(core_ref, ends_ref, inner, 6)
    assemble_edges(
        near_ref, rank_ref, pair_ref, other_ref, face_ref, edge_core_ref, edge_ends_ref
    )
    gather_taps(edge_core_ref, edge_ends_ref, edges, 18)
    token_ref[...] = jnp.zeros_like(token_ref)


def input_taps_call(after, near, rank, g, pair, other):
    return pl.pallas_call(
        input_taps_kernel,
        out_shape=(INNER_TAPS,) * 3 + (EDGE_TAPS,) * 3 + (TOKEN,),
        in_specs=[ANY_SPEC] + [SMEM_SPEC] * 2 + [VMEM_SPEC] * 3,
        out_specs=(VMEM_SPEC,) * 7,
        scratch_shapes=INNER_SCRATCH + EDGE_SCRATCH,
        compiler_params=params(20),
        cost_estimate=pl.CostEstimate(
            flops=1_000_000_000, bytes_accessed=8_000_000, transcendentals=0
        ),
        name="input_taps",
    )(after, near, rank, g, pair, other)


def input_half_kernel(half, *refs):
    inner, edges, w_ref = refs[1:4], refs[4:7], refs[7]
    out_ref, token_ref, acc_ref = refs[-3:]
    convolve(tuple(zip(inner, edges)), w_ref, acc_ref, half * HALF, HALF + 2, 10)

    for i in range(HALF):
        out_ref[:, i * 256 : (i + 1) * 256] = acc_ref[i + 2].T.astype(BF16)
    token_ref[...] = jnp.zeros_like(token_ref)


def input_half_call(after, taps, weights, half, begun=()):
    return pl.pallas_call(
        functools.partial(input_half_kernel, half),
        grid=(1,),
        out_shape=(jax.ShapeDtypeStruct((LANES, SIDE**3), BF16), TOKEN),
        in_specs=[ANY_SPEC] + [VMEM_SPEC] * 7 + [ANY_SPEC] * len(begun),
        out_specs=(
            pl.BlockSpec((LANES, SIDE**3 // 2), lambda g: (0, half)),
            pl.BlockSpec((8, LANES), lambda g: (0, 0)),
        ),
        input_output_aliases={8: 0} if begun else {},
        scratch_shapes=[pltpu.VMEM((HALF + 4, 256, LANES), F32)],
        compiler_params=params(16),
        cost_estimate=pl.CostEstimate(
            flops=2_500_000_000, bytes_accessed=6_000_000, transcendentals=0
        ),
        name="input_half",
    )(after, *taps, weights, *begun)


def deal_kernel(rank_ref, kept_ref, came_ref, own_ref, *refs):
    share_refs, total_ref = refs[:-1], refs[-1]
    total_ref[...] = kept_ref[...] + came_ref[...].astype(F32)
    y = y_of(rank_ref)
    own_ref[...] = total_ref[y]
    for s, share_ref in enumerate(share_refs):
        share_ref[...] = total_ref[y ^ (s + 1)].astype(BF16)


def deal_call(rank, kept, came):
    return pl.pallas_call(
        deal_kernel,
        out_shape=(jax.ShapeDtypeStruct((SHARE, LANES), F32),)
        + (jax.ShapeDtypeStruct((SHARE, LANES), BF16),) * 3,
        in_specs=[SMEM_SPEC, VMEM_SPEC, VMEM_SPEC],
        out_specs=(VMEM_SPEC,) * 4,
        scratch_shapes=[pltpu.VMEM((GROUPS // 2, SHARE, LANES), F32)],
        compiler_params=params(16),
        cost_estimate=pl.CostEstimate(flops=0, bytes_accessed=500_000, transcendentals=0),
        name="deal",
    )(rank, kept, came)


def add_kernel(after_ref, *refs):
    parts = [ref[...].astype(F32) for ref in refs[:-1]]
    while len(parts) > 1:
        parts = [first + second for first, second in zip(parts[::2], parts[1::2])]
    refs[-1][...] = parts[0].astype(refs[-1].dtype)


def add_call(after, parts, dtype=BF16):
    return pl.pallas_call(
        add_kernel,
        out_shape=jax.ShapeDtypeStruct(parts[0].shape, dtype),
        in_specs=[ANY_SPEC] + [VMEM_SPEC] * len(parts),
        out_specs=VMEM_SPEC,
        compiler_params=params(16),
        cost_estimate=pl.CostEstimate(flops=0, bytes_accessed=500_000, transcendentals=0),
        name="add",
    )(after, *parts)


def collect_kernel(after_ref, rank_ref, *refs):
    y = y_of(rank_ref)
    for s, share_ref in enumerate(refs[:-1]):
        refs[-1][y ^ s] = share_ref[...]


def collect_call(after, rank, shares):
    return pl.pallas_call(
        collect_kernel,
        out_shape=jax.ShapeDtypeStruct((GROUPS // 2, SHARE, LANES), BF16),
        in_specs=[ANY_SPEC, SMEM_SPEC] + [VMEM_SPEC] * len(shares),
        out_specs=VMEM_SPEC,
        compiler_params=params(16),
        cost_estimate=pl.CostEstimate(flops=0, bytes_accessed=500_000, transcendentals=0),
        name="collect",
    )(after, rank, *shares)


def split_kernel(rank_ref, mine_ref, theirs_ref, conv_ref, down_ref, sums_ref):
    core = core_of(rank_ref)
    for y in range(GROUPS // 2):
        sums_ref[share_rows(2 * y + core)] = mine_ref[y].astype(F32)
        sums_ref[share_rows(2 * y + 1 - core)] = theirs_ref[y].astype(F32)
    for a in range(3):
        for b in range(3):
            for c in range(3):
                chunk, upper = (b, c) if c < 2 else ((3, b) if b < 2 else (4, 0))
                base = chunk * 192 + a * 64
                block = sums_ref[base : base + 64]
                block = swap_halves(block) if upper else block
                conv_ref[9 * a + 3 * b + c] = block[:, :64]
    for t in range(4):
        block = sums_ref[CONV_ROWS + t * LANES : CONV_ROWS + (t + 1) * LANES].T
        down_ref[t] = block[:64]
        down_ref[t + 4] = block[64:]


def split_call(rank, mine, theirs):
    return pl.pallas_call(
        split_kernel,
        out_shape=(
            jax.ShapeDtypeStruct((27, 64, 64), F32),
            jax.ShapeDtypeStruct((8, 64, LANES), F32),
        ),
        in_specs=[SMEM_SPEC] + [VMEM_SPEC] * 2,
        out_specs=(VMEM_SPEC,) * 2,
        scratch_shapes=[pltpu.VMEM((CONV_ROWS + DOWN_ROWS, LANES), F32)],
        compiler_params=params(16),
        name="split",
    )(rank, mine, theirs)


def swaps(axis, step=1):
    return [(i, i ^ step) for i in range(lax.axis_size(axis))]


def swapped(array, axis, steps):
    return [lax.ppermute(array, axis, swaps(axis, step)) for step in steps]


def exchange(pair, other):
    bricks = ("y", "core", "z", "x")
    rows = lax.axis_size(("z", "x"))
    across = []
    for device in range(lax.axis_size(bricks)):
        row = device % rows
        if row in (0, rows - 1):
            across.append((device, device ^ rows))
        else:
            across.append((device, device + 1 if row % 2 else device - 1))
    return lax.ppermute(pair, ("z", "x"), swaps(("z", "x"))), lax.ppermute(other, bricks, across)


def body(fine_input, conv_weight, down_weight, coarse_cot, neighbours, children):
    dev = ("z", "x")
    rank = lax.axis_index(("y", "core", "z", "x")).reshape(1).astype(jnp.int32)

    voxels, pair, other, token = faces_call(rank, fine_input.reshape(LANES, SIDE**3))
    own, send = cot_call(token, children, rank, coarse_cot.reshape(LANES, SIDE**3))
    pair, other = exchange(pair, other)
    came = lax.ppermute(send, dev, swaps(dev))
    forward, backward, down, down_t = weights_call(conv_weight, down_weight.transpose(0, 2, 1))
    inner = inner_call(neighbours, voxels)
    octants, slope, act, *edges = forward_call(
        neighbours, rank, pair, other, inner, forward, down
    )
    mine, other_out, grads, turned, spun = back_call(rank, own, came, down_t, slope, octants)
    theirs, grad_other = exchange(mine, other_out)

    kept, sent = weigh_call(rank, inner, edges, act, turned, spun)
    (came,) = swapped(sent, "core", (1,))
    own, *shares = deal_call(rank, kept, came)
    came = [lax.ppermute(share, "y", swaps("y", s + 1)) for s, share in enumerate(shares)]
    *taps_in, token = input_taps_call(own, neighbours, rank, grads, theirs, grad_other)
    part = add_call(token, [own, *came], F32)
    came = swapped(part, "x", (1, 2, 3))
    input_grad, token = input_half_call(part, taps_in, backward, 0)
    part = add_call(token, [part, *came])
    came = swapped(part, "z", (1, 2, 3))
    coarse, token = coarse_half_call(part, children, rank, mine, theirs, 0)
    part = add_call(token, [part, *came])
    came = swapped(part, "z", (4,))
    input_grad, token = input_half_call(part, taps_in, backward, 1, (input_grad,))
    part = add_call(token, [part, *came])
    came = swapped(part, "y", (1, 2, 3))
    coarse, token = coarse_half_call(part, children, rank, mine, theirs, 1, (coarse,))
    shares = collect_call(token, rank, [part, *came])
    (came,) = swapped(shares, "core", (1,))
    conv_grad, down_grad = split_call(rank, shares, came)
    return (
        coarse.reshape(1, LANES, SIDE**3),
        input_grad.reshape(2, 64, SIDE**3),
        conv_grad,
        down_grad.transpose(0, 2, 1),
    )


def solution(mesh):
    grp, dev = mesh.devices.shape
    mesh = jax.sharding.Mesh(
        mesh.devices.reshape(grp // 2, 2, dev // 4, 4), ("y", "core", "z", "x")
    )
    bricks = ("y", "core", "z", "x")
    in_specs = (P(bricks, None, None), P(), P(), P(bricks, None, None), P(bricks, None), P(bricks, None))
    out_specs = (P(bricks, None, None), P(bricks, None, None), P(), P())
    return jax.shard_map(body, mesh=mesh, in_specs=in_specs, out_specs=out_specs, check_vma=False)
```

```python
import functools

import jax
import jax.numpy as jnp
from jax import lax
from jax.experimental import pallas as pl
from jax.experimental.pallas import tpu as pltpu
from jax.sharding import PartitionSpec as P

SIDE = 16
HALF = 8
LANES = 128
F32 = jnp.float32
BF16 = jnp.bfloat16
CONV_ROWS = 960
DOWN_ROWS = 512
GROUPS = 8
ROWS = 32
SHARE = (CONV_ROWS + DOWN_ROWS) // GROUPS

VMEM_SPEC = pl.BlockSpec(memory_space=pltpu.VMEM)
SMEM_SPEC = pl.BlockSpec(memory_space=pltpu.SMEM)
ANY_SPEC = pl.BlockSpec(memory_space=pl.ANY)
TOKEN = jax.ShapeDtypeStruct((8, LANES), F32)


def params(mib):
    return pltpu.CompilerParams(vmem_limit_bytes=mib * 1024 * 1024)


def loop(count, body, unroll):
    def step(g, carry):
        for p in range(unroll):
            body(g * unroll + p)
        return carry

    lax.fori_loop(0, count // unroll, step, 0)


def low_half(shape):
    return lax.broadcasted_iota(jnp.int32, shape, len(shape) - 1) < 64


def swap_halves(x):
    return pltpu.roll(x, 64, x.ndim - 1)


def place_faces(rank_ref, i, planes, pair_ref, other_ref, first=0):
    even = rank_ref[0] % 2 == 0
    low, high = planes[0], planes[SIDE - 1]
    pair_ref[pl.ds(pl.multiple_of(first + i * SIDE, SIDE), SIDE)] = jnp.where(even, high, low)
    other_ref[pl.ds(pl.multiple_of(i * SIDE, SIDE), SIDE)] = jnp.where(even, low, high)


def faces_kernel(rank_ref, x_ref, v_ref, pair_ref, other_ref, token_ref):
    def plane(i):
        columns = pl.ds(pl.multiple_of(i * 256, 256), 256)
        voxels = x_ref[:, columns].astype(F32).T.astype(BF16).reshape(SIDE, SIDE, LANES)
        v_ref[i] = voxels
        place_faces(rank_ref, i, voxels, pair_ref, other_ref)

    loop(SIDE, plane, 8)
    token_ref[...] = jnp.zeros_like(token_ref)


def faces_call(rank, x):
    face = jax.ShapeDtypeStruct((256, LANES), BF16)
    return pl.pallas_call(
        faces_kernel,
        out_shape=(jax.ShapeDtypeStruct((SIDE, SIDE, SIDE, LANES), BF16), face, face, TOKEN),
        in_specs=[SMEM_SPEC, VMEM_SPEC],
        out_specs=(VMEM_SPEC,) * 4,
        compiler_params=params(16),
        cost_estimate=pl.CostEstimate(flops=0, bytes_accessed=4_000_000, transcendentals=0),
        name="faces",
    )(rank, x)


def find_octant(child_ref, wanted):
    place = jnp.int32(0)
    found = jnp.int32(0)
    for o in range(8):
        hit = (child_ref[0, o] == wanted).astype(jnp.int32)
        place = place + hit * o
        found = found + hit
    return place, found


def cot_kernel(after_ref, child_ref, rank_ref, cot_ref, own_ref, send_ref, turned_ref):
    def plane(i):
        columns = pl.ds(pl.multiple_of(i * 256, 256), 256)
        turned = cot_ref[:, columns].astype(F32).T
        turned_ref[i // HALF, i % HALF] = turned.reshape(2, HALF, 2, HALF, LANES)

    loop(SIDE, plane, 8)
    rank = rank_ref[0]
    for out_ref, holder in ((own_ref, rank), (send_ref, rank ^ 1)):
        for slot in range(2):
            place, found = find_octant(child_ref, holder * 2 + slot)
            block = turned_ref[place // 4, :, place // 2 % 2, :, place % 2]
            block = jnp.where(found > 0, block, jnp.zeros_like(block))
            out_ref[slot * 512 : (slot + 1) * 512] = block.reshape(512, LANES).astype(BF16)


def cot_call(after, children, rank, cot):
    blocks = jax.ShapeDtypeStruct((1024, LANES), BF16)
    return pl.pallas_call(
        cot_kernel,
        out_shape=(blocks, blocks),
        in_specs=[ANY_SPEC, SMEM_SPEC, SMEM_SPEC, VMEM_SPEC],
        out_specs=(VMEM_SPEC,) * 2,
        scratch_shapes=[pltpu.VMEM((2, HALF, 2, HALF, 2, HALF, LANES), F32)],
        compiler_params=params(20),
        cost_estimate=pl.CostEstimate(flops=0, bytes_accessed=8_000_000, transcendentals=0),
        name="cot",
    )(after, children, rank, cot)


def weights_kernel(
    conv_ref, down_in_ref, forward_ref, backward_ref, down_ref, down_t_ref
):
    blank = jnp.zeros((64, 64), F32)
    for b in range(3):
        for c in range(3):
            rows = slice(b * 256 + c * 64, b * 256 + (c + 1) * 64)
            ahead = [conv_ref[9 * a + 3 * b + c].astype(F32) for a in range(3)]
            behind = [conv_ref[26 - (9 * a + 3 * b + c)].astype(F32) for a in range(3)]
            for n in range(2):
                order = (0, 1, 2, None) if n == 0 else (1, 0, None, 2)
                if c == 2:
                    rows = slice(b * 256 + 128 + n * 64, b * 256 + 192 + n * 64)
                    unused = slice(b * 256 + 192 - n * 64, b * 256 + 256 - n * 64)
                    forward_ref[n, unused] = jnp.zeros((64, 256), BF16)
                    backward_ref[n, unused] = jnp.zeros((64, 256), BF16)
                for half in range(2):
                    pair = order[2 * half : 2 * half + 2]
                    lanes = slice(half * LANES, (half + 1) * LANES)
                    taps = [blank if a is None else ahead[a] for a in pair]
                    forward_ref[n, rows, lanes] = jnp.concatenate(taps, axis=0).T.astype(BF16)
                    taps = [blank if a is None else behind[a] for a in pair]
                    backward_ref[n, rows, lanes] = jnp.concatenate(taps, axis=1).astype(BF16)
    for t in range(8):
        tap = down_in_ref[t]
        blank = jnp.zeros((64, LANES), BF16)
        rows = [jnp.concatenate([tap, blank], axis=1), jnp.concatenate([blank, tap], axis=1)]
        block = jnp.concatenate(rows, axis=0)
        down_ref[t * LANES : (t + 1) * LANES] = block
        down_t_ref[:, t * LANES : (t + 1) * LANES] = block.astype(F32).T.astype(BF16)


def weights_call(conv_weight, down_weight):
    conv = jax.ShapeDtypeStruct((2, 768, 256), BF16)
    return pl.pallas_call(
        weights_kernel,
        out_shape=(
            conv,
            conv,
            jax.ShapeDtypeStruct((8 * LANES, 256), BF16),
            jax.ShapeDtypeStruct((256, 8 * LANES), BF16),
        ),
        in_specs=[VMEM_SPEC] * 2,
        out_specs=(VMEM_SPEC,) * 4,
        compiler_params=params(16),
        cost_estimate=pl.CostEstimate(flops=0, bytes_accessed=8_000_000, transcendentals=0),
        name="weights",
    )(conv_weight, down_weight)


def coarse_half_kernel(half, *refs):
    _, child_ref, rank_ref, mine_ref, theirs_ref = refs[:5]
    out_ref, token_ref, whole_ref = refs[-3:]
    token_ref[...] = jnp.zeros_like(token_ref)
    for o in range(4):
        entry = child_ref[0, half * 4 + o]
        slot = jnp.maximum(entry, 0) % 2
        here = jnp.maximum(entry, 0) // 2 == rank_ref[0]
        rows = pl.ds(pl.multiple_of(slot * 512, 512), 512)
        block = jnp.where(here, mine_ref[rows], theirs_ref[rows])
        block = jnp.where(entry >= 0, block, jnp.zeros_like(block)).astype(F32)
        whole_ref[:, o // 2, :, o % 2] = block.reshape(HALF, HALF, HALF, LANES)

    for i in range(HALF):
        turned = whole_ref[i].reshape(256, LANES).T
        out_ref[:, i * 256 : (i + 1) * 256] = turned.astype(BF16)


def coarse_half_call(after, children, rank, mine, theirs, half, begun=()):
    return pl.pallas_call(
        functools.partial(coarse_half_kernel, half),
        grid=(1,),
        out_shape=(jax.ShapeDtypeStruct((LANES, SIDE**3), BF16), TOKEN),
        in_specs=[ANY_SPEC, SMEM_SPEC, SMEM_SPEC, VMEM_SPEC, VMEM_SPEC] + [ANY_SPEC] * len(begun),
        out_specs=(
            pl.BlockSpec((LANES, SIDE**3 // 2), lambda g: (0, half)),
            pl.BlockSpec((8, LANES), lambda g: (0, 0)),
        ),
        input_output_aliases={5: 0} if begun else {},
        scratch_shapes=[pltpu.VMEM((HALF, 2, HALF, 2, HALF, LANES), F32)],
        compiler_params=params(16),
        cost_estimate=pl.CostEstimate(flops=0, bytes_accessed=4_000_000, transcendentals=0),
        name="coarse_half",
    )(after, children, rank, mine, theirs, *begun)


def spans(step):
    if step == 0:
        return slice(1, SIDE + 1), slice(0, SIDE)
    if step == 1:
        return slice(SIDE + 1, SIDE + 2), slice(0, 1)
    return slice(0, 1), slice(SIDE - 1, SIDE)


def chooser(near_ref, column):
    lower = low_half((1, LANES))
    entries = near_ref[0, column], near_ref[1, column]
    straight = [
        jnp.logical_and(e >= 0, jnp.maximum(e, 0) % 2 == n).astype(F32)
        for n, e in enumerate(entries)
    ]
    crossed = [
        jnp.logical_and(e >= 0, jnp.maximum(e, 0) % 2 != n).astype(F32)
        for n, e in enumerate(entries)
    ]
    keep = jnp.where(lower, straight[0], straight[1])
    cross = jnp.where(lower, crossed[0], crossed[1])

    def choose(x):
        shape = (1,) * (x.ndim - 1) + (LANES,)
        return x * keep.reshape(shape) + swap_halves(x) * cross.reshape(shape)

    return choose


def offsets():
    steps = [(x, y, z) for x in (-1, 0, 1) for y in (-1, 0, 1) for z in (-1, 0, 1)]
    steps.remove((0, 0, 0))
    return list(enumerate(steps))


def assemble_inner(near_ref, v_ref, core_ref, ends_ref):
    def fill(i):
        core_ref[i + 1] = v_ref[i].astype(F32).reshape(256, LANES)

    loop(SIDE, fill, 4)
    lines = []
    for column, (step_x, step_y, step_z) in offsets():
        if step_y != 0:
            continue
        choose = chooser(near_ref, column)
        put_x, take_x = spans(step_x)
        end = 0 if step_z < 0 else 1
        strided = pl.ds(SIDE - 1 if step_z < 0 else 0, SIDE, stride=SIDE)
        if step_x == 0:
            lines.append((choose, end, strided))
        elif step_z == 0:
            core_ref[put_x.start] = choose(core_ref[take_x.start + 1])
        else:
            ends_ref[end, put_x.start] = choose(core_ref[take_x.start + 1, strided])

    def line(i):
        for choose, end, strided in lines:
            ends_ref[end, i + 1] = choose(core_ref[i + 1, strided])

    loop(SIDE, line, 4)


def assemble_edges(near_ref, rank_ref, pair_ref, other_ref, face_ref, core_ref, ends_ref):
    even = rank_ref[0] % 2 == 0
    pair = pair_ref[pair_ref.shape[0] - 256 :].astype(F32).reshape(SIDE, SIDE, LANES)
    other = other_ref[...].astype(F32).reshape(SIDE, SIDE, LANES)
    face_ref[0] = jnp.where(even, other, pair)
    face_ref[1] = jnp.where(even, pair, other)
    for column, (step_x, step_y, step_z) in offsets():
        if step_y == 0:
            continue
        choose = chooser(near_ref, column)
        put_x, take_x = spans(step_x)
        side = 0 if step_y < 0 else 1
        if step_z == 0:
            core_ref[put_x, side * SIDE : (side + 1) * SIDE] = choose(face_ref[side, take_x])
        else:
            end, row = (0, SIDE - 1) if step_z < 0 else (1, 0)
            ends_ref[end, put_x, side : side + 1] = choose(
                face_ref[side, take_x, row : row + 1]
            )


def gather_taps(core_ref, ends_ref, tap_refs, unroll):
    lower = low_half((SIDE, LANES))
    rows = lax.broadcasted_iota(jnp.int32, (8, LANES), 0)
    top, bottom = rows == 0, rows == 7

    def plane(i):
        for j in range(tap_refs[0].shape[1]):
            first = core_ref[i, j * SIDE : j * SIDE + 8]
            second = core_ref[i, j * SIDE + 8 : (j + 1) * SIDE]
            down_first, down_second = pltpu.roll(first, 1, 0), pltpu.roll(second, 1, 0)
            up_first, up_second = pltpu.roll(first, 7, 0), pltpu.roll(second, 7, 0)
            before = jnp.concatenate(
                [
                    jnp.where(top, ends_ref[0, i, j : j + 1], down_first),
                    jnp.where(top, down_first, down_second),
                ],
                axis=0,
            )
            after = jnp.concatenate(
                [
                    jnp.where(bottom, up_second, up_first),
                    jnp.where(bottom, ends_ref[1, i, j : j + 1], up_second),
                ],
                axis=0,
            )
            here = jnp.concatenate([first, second], axis=0)
            tap_refs[0][i, j] = jnp.where(lower, before, swap_halves(here)).astype(BF16)
            tap_refs[1][i, j] = jnp.where(lower, swap_halves(before), here).astype(BF16)
            tap_refs[2][i, j] = after.astype(BF16)

    loop(SIDE + 2, plane, unroll)


def window(refs, planes, b):
    inner_ref, edge_ref = refs
    if b == 0:
        parts = [edge_ref[planes, 0:1], inner_ref[planes, 0 : SIDE - 1]]
    elif b == 1:
        parts = [inner_ref[planes]]
    else:
        parts = [inner_ref[planes, 1:SIDE], edge_ref[planes, 1:2]]
    return jnp.concatenate(parts, axis=1).reshape(-1, LANES)


def convolve(tap_refs, w_ref, acc_ref, first=0, planes=SIDE + 2, group=18):
    rows = group * 256

    def clear(i):
        acc_ref[i] = jnp.zeros((256, LANES), F32)

    loop(planes + 2, clear, 4)
    lower = low_half((256, LANES))

    def step(g, carry):
        start = g * group
        results = []
        for n in range(2):
            lhs = [
                window(tap_refs[chunk], pl.ds(first + start, group), b)
                for b in range(3)
                for chunk in (n, 2)
            ]
            lhs = jnp.concatenate(lhs, axis=1)
            results.append(jnp.dot(lhs, w_ref[n], preferred_element_type=F32))
        zero, one = results
        for p in range(group):
            own = slice(p * 256, (p + 1) * 256)
            z, o = zero[own], one[own]
            acc_ref[start + p + 2] += jnp.where(lower, z[:, :LANES], o[:, :LANES])
            acc_ref[start + p + 1] += swap_halves(jnp.where(lower, o[:, :LANES], z[:, :LANES]))
            acc_ref[start + p] += z[:, LANES:] + o[:, LANES:]
        return carry

    lax.fori_loop(0, planes // group, step, 0)


def taps():
    return [(t, t // 4, t // 2 % 2, t % 2) for t in range(8)]


def inner_kernel(near_ref, v_ref, zero_ref, one_ref, both_ref, core_ref, ends_ref):
    assemble_inner(near_ref, v_ref, core_ref, ends_ref)
    gather_taps(core_ref, ends_ref, (zero_ref, one_ref, both_ref), 9)


def forward_kernel(
    near_ref,
    rank_ref,
    pair_ref,
    other_ref,
    zero_ref,
    one_ref,
    both_ref,
    w_ref,
    down_ref,
    oct_ref,
    slope_ref,
    act_ref,
    zero_edge_ref,
    one_edge_ref,
    both_edge_ref,
    face_ref,
    core_ref,
    ends_ref,
    acc_ref,
    fine_ref,
):
    edges = (zero_edge_ref, one_edge_ref, both_edge_ref)
    assemble_edges(near_ref, rank_ref, pair_ref, other_ref, face_ref, core_ref, ends_ref)
    gather_taps(core_ref, ends_ref, edges, 18)
    convolve(tuple(zip((zero_ref, one_ref, both_ref), edges)), w_ref, acc_ref)

    def activate(i):
        preact = acc_ref[i + 2]
        gate = 1.0 / (1.0 + jnp.exp(-preact))
        fine_ref[i // 2, i % 2] = (preact * gate).reshape(HALF, 2, SIDE, LANES)
        slope_ref[i] = gate * (1.0 + preact * (1.0 - gate))

    loop(SIDE, activate, 16)
    for t, a, b, c in taps():
        picked = fine_ref[:, a, :, b, pl.ds(c, HALF, stride=2), :]
        act_ref[:, t * LANES : (t + 1) * LANES] = picked.reshape(512, LANES).astype(BF16)
    octants = jnp.dot(act_ref[...], down_ref[...], preferred_element_type=F32).astype(BF16)
    oct_ref[0:512] = octants[:, :LANES]
    oct_ref[512:1024] = octants[:, LANES:]


def back_kernel(
    rank_ref,
    own_ref,
    came_ref,
    down_t_ref,
    slope_ref,
    oct_ref,
    pair_ref,
    other_ref,
    g_ref,
    turned_ref,
    spun_ref,
    fine_ref,
):
    pair_ref[0:1024] = oct_ref[...]
    grads = []
    for n in range(2):
        rows = slice(n * 512, (n + 1) * 512)
        grad = own_ref[rows].astype(F32) + came_ref[rows].astype(F32)
        spun_ref[n] = grad.T.astype(BF16)
        grads.append(grad.astype(BF16))
    grads = jnp.concatenate(grads, axis=1)
    for pair in range(4):
        lanes = slice(pair * 256, (pair + 1) * 256)
        spread = jnp.dot(grads, down_t_ref[:, lanes], preferred_element_type=F32)
        for c in range(2):
            part = spread[:, c * LANES : (c + 1) * LANES].reshape(HALF, HALF, HALF, LANES)
            fine_ref[:, pair // 2, :, pair % 2, pl.ds(c, HALF, stride=2), :] = part

    for p in (0, 1, SIDE + 2, SIDE + 3):
        turned_ref[p] = jnp.zeros((LANES, 256), BF16)

    def back(i):
        grad = fine_ref[i // 2, i % 2].reshape(256, LANES) * slope_ref[i]
        turned_ref[i + 2] = grad.T.astype(BF16)
        rounded = grad.astype(BF16).reshape(SIDE, SIDE, LANES)
        g_ref[i] = rounded
        place_faces(rank_ref, i, rounded, pair_ref, other_ref, 1024)

    loop(SIDE, back, 16)


def weigh_kernel(*refs):
    rank_ref, inner, edges = refs[0], refs[1:4], refs[4:7]
    act_ref, turned_ref, spun_ref, kept_ref, sent_ref, sums_ref, total_ref = refs[7:]
    zero, one, both_taps = zip(inner, edges)
    lower = low_half((LANES, LANES))
    whole = [jnp.dot(spun_ref[n], act_ref[...], preferred_element_type=F32) for n in range(2)]
    folded = []
    for t in range(8):
        lanes = slice(t * LANES, (t + 1) * LANES)
        both = jnp.where(lower, whole[0][:, lanes], whole[1][:, lanes])
        folded.append(both + swap_halves(both))
    for t in range(4):
        rows = slice(CONV_ROWS + t * LANES, CONV_ROWS + (t + 1) * LANES)
        sums_ref[rows] = jnp.where(lower, folded[t], folded[t + 4])

    total_ref[...] = jnp.zeros_like(total_ref)

    def weigh(g, carry):
        planes = [18 * g + p for p in range(18)]
        for n, brick in enumerate((zero, one)):
            lhs = [
                jnp.concatenate(
                    [turned_ref[i + 2 - a, n * 64 : (n + 1) * 64] for a in range(3)], axis=0
                )
                for i in planes
            ]
            rhs = [
                jnp.concatenate(
                    [
                        window(refs, pl.ds(i, 1), b)
                        for refs in (brick, both_taps)
                        for b in range(3)
                    ],
                    axis=1,
                )
                for i in planes
            ]
            total_ref[n] += jnp.dot(
                jnp.concatenate(lhs, axis=1),
                jnp.concatenate(rhs, axis=0),
                preferred_element_type=F32,
            )
        return carry

    lax.fori_loop(0, (SIDE + 2) // 18, weigh, 0)
    lower = low_half((192, LANES))
    last = []
    for b in range(3):
        lanes = slice(b * LANES, (b + 1) * LANES)
        sums_ref[b * 192 : (b + 1) * 192] = total_ref[0, :, lanes] + total_ref[1, :, lanes]
        lanes = slice((3 + b) * LANES, (4 + b) * LANES)
        both = jnp.where(lower, total_ref[0, :, lanes], total_ref[1, :, lanes])
        last.append(both + swap_halves(both))
    sums_ref[576:768] = jnp.where(lower, last[0], last[1])
    sums_ref[768:960] = jnp.where(lower, last[2], 0.0)
    core = core_of(rank_ref)
    for y in range(GROUPS // 2):
        kept_ref[y] = sums_ref[share_rows(2 * y + core)]
        sent_ref[y] = sums_ref[share_rows(2 * y + 1 - core)].astype(BF16)


def core_of(rank_ref):
    return rank_ref[0] // ROWS % 2


def y_of(rank_ref):
    return rank_ref[0] // (2 * ROWS)


def share_rows(group):
    return pl.ds(pl.multiple_of(group * SHARE, 8), SHARE)


INNER_TAPS = jax.ShapeDtypeStruct((SIDE + 2, SIDE, SIDE, LANES), BF16)
EDGE_TAPS = jax.ShapeDtypeStruct((SIDE + 2, 2, SIDE, LANES), BF16)
INNER_SCRATCH = [
    pltpu.VMEM((SIDE + 2, 256, LANES), F32),
    pltpu.VMEM((2, SIDE + 2, SIDE, LANES), F32),
]
EDGE_SCRATCH = [
    pltpu.VMEM((2, SIDE, SIDE, LANES), F32),
    pltpu.VMEM((SIDE + 2, 2 * SIDE, LANES), F32),
    pltpu.VMEM((2, SIDE + 2, 8, LANES), F32),
]
ACC_SCRATCH = pltpu.VMEM((SIDE + 4, 256, LANES), F32)
FINE_SCRATCH = pltpu.VMEM((HALF, 2, HALF, 2, SIDE, LANES), F32)


def inner_call(near, v):
    return pl.pallas_call(
        inner_kernel,
        out_shape=(INNER_TAPS,) * 3,
        in_specs=[SMEM_SPEC, VMEM_SPEC],
        out_specs=(VMEM_SPEC,) * 3,
        scratch_shapes=INNER_SCRATCH,
        compiler_params=params(20),
        cost_estimate=pl.CostEstimate(
            flops=1_000_000_000, bytes_accessed=8_000_000, transcendentals=0
        ),
        name="inner",
    )(near, v)


def forward_call(near, rank, pair, other, inner, weights, down):
    return pl.pallas_call(
        forward_kernel,
        out_shape=(
            jax.ShapeDtypeStruct((1024, LANES), BF16),
            jax.ShapeDtypeStruct((SIDE, 256, LANES), F32),
            jax.ShapeDtypeStruct((512, 8 * LANES), BF16),
        )
        + (EDGE_TAPS,) * 3,
        in_specs=[SMEM_SPEC] * 2 + [VMEM_SPEC] * 7,
        out_specs=(VMEM_SPEC,) * 6,
        scratch_shapes=EDGE_SCRATCH + [ACC_SCRATCH, FINE_SCRATCH],
        compiler_params=params(28),
        cost_estimate=pl.CostEstimate(
            flops=4_000_000_000, bytes_accessed=16_000_000, transcendentals=600_000
        ),
        name="forward",
    )(near, rank, pair, other, *inner, weights, down)


def back_call(rank, own, came, down_t, slope, octants):
    return pl.pallas_call(
        back_kernel,
        out_shape=(
            jax.ShapeDtypeStruct((1280, LANES), BF16),
            jax.ShapeDtypeStruct((256, LANES), BF16),
            jax.ShapeDtypeStruct((SIDE, SIDE, SIDE, LANES), BF16),
            jax.ShapeDtypeStruct((SIDE + 4, LANES, 256), BF16),
            jax.ShapeDtypeStruct((2, LANES, 512), BF16),
        ),
        in_specs=[SMEM_SPEC] + [VMEM_SPEC] * 5,
        out_specs=(VMEM_SPEC,) * 5,
        scratch_shapes=[FINE_SCRATCH],
        compiler_params=params(24),
        cost_estimate=pl.CostEstimate(
            flops=300_000_000, bytes_accessed=8_000_000, transcendentals=0
        ),
        name="back",
    )(rank, own, came, down_t, slope, octants)


def weigh_call(rank, inner, edges, act, turned, spun):
    return pl.pallas_call(
        weigh_kernel,
        out_shape=(
            jax.ShapeDtypeStruct((GROUPS // 2, SHARE, LANES), F32),
            jax.ShapeDtypeStruct((GROUPS // 2, SHARE, LANES), BF16),
        ),
        in_specs=[SMEM_SPEC] + [VMEM_SPEC] * 9,
        out_specs=(VMEM_SPEC,) * 2,
        scratch_shapes=[
            pltpu.VMEM((CONV_ROWS + DOWN_ROWS, LANES), F32),
            pltpu.VMEM((2, 192, 768), F32),
        ],
        compiler_params=params(20),
        cost_estimate=pl.CostEstimate(
            flops=4_000_000_000, bytes_accessed=10_000_000, transcendentals=0
        ),
        name="weigh",
    )(rank, *inner, *edges, act, turned, spun)


def input_taps_kernel(after_ref, near_ref, rank_ref, g_ref, pair_ref, other_ref, *refs):
    inner, edges, token_ref = refs[:3], refs[3:6], refs[6]
    core_ref, ends_ref, face_ref, edge_core_ref, edge_ends_ref = refs[7:]
    assemble_inner(near_ref, g_ref, core_ref, ends_ref)
    gather_taps(core_ref, ends_ref, inner, 9)
    assemble_edges(
        near_ref, rank_ref, pair_ref, other_ref, face_ref, edge_core_ref, edge_ends_ref
    )
    gather_taps(edge_core_ref, edge_ends_ref, edges, 18)
    token_ref[...] = jnp.zeros_like(token_ref)


def input_taps_call(after, near, rank, g, pair, other):
    return pl.pallas_call(
        input_taps_kernel,
        out_shape=(INNER_TAPS,) * 3 + (EDGE_TAPS,) * 3 + (TOKEN,),
        in_specs=[ANY_SPEC] + [SMEM_SPEC] * 2 + [VMEM_SPEC] * 3,
        out_specs=(VMEM_SPEC,) * 7,
        scratch_shapes=INNER_SCRATCH + EDGE_SCRATCH,
        compiler_params=params(20),
        cost_estimate=pl.CostEstimate(
            flops=1_000_000_000, bytes_accessed=8_000_000, transcendentals=0
        ),
        name="input_taps",
    )(after, near, rank, g, pair, other)


def input_half_kernel(half, *refs):
    inner, edges, w_ref = refs[1:4], refs[4:7], refs[7]
    out_ref, token_ref, acc_ref = refs[-3:]
    convolve(tuple(zip(inner, edges)), w_ref, acc_ref, half * HALF, HALF + 2, 10)

    for i in range(HALF):
        out_ref[:, i * 256 : (i + 1) * 256] = acc_ref[i + 2].T.astype(BF16)
    token_ref[...] = jnp.zeros_like(token_ref)


def input_half_call(after, taps, weights, half, begun=()):
    return pl.pallas_call(
        functools.partial(input_half_kernel, half),
        grid=(1,),
        out_shape=(jax.ShapeDtypeStruct((LANES, SIDE**3), BF16), TOKEN),
        in_specs=[ANY_SPEC] + [VMEM_SPEC] * 7 + [ANY_SPEC] * len(begun),
        out_specs=(
            pl.BlockSpec((LANES, SIDE**3 // 2), lambda g: (0, half)),
            pl.BlockSpec((8, LANES), lambda g: (0, 0)),
        ),
        input_output_aliases={8: 0} if begun else {},
        scratch_shapes=[pltpu.VMEM((HALF + 4, 256, LANES), F32)],
        compiler_params=params(16),
        cost_estimate=pl.CostEstimate(
            flops=2_500_000_000, bytes_accessed=6_000_000, transcendentals=0
        ),
        name="input_half",
    )(after, *taps, weights, *begun)


def deal_kernel(rank_ref, kept_ref, came_ref, own_ref, *refs):
    share_refs, total_ref = refs[:-1], refs[-1]
    total_ref[...] = kept_ref[...] + came_ref[...].astype(F32)
    y = y_of(rank_ref)
    own_ref[...] = total_ref[y]
    for s, share_ref in enumerate(share_refs):
        share_ref[...] = total_ref[y ^ (s + 1)].astype(BF16)


def deal_call(rank, kept, came):
    return pl.pallas_call(
        deal_kernel,
        out_shape=(jax.ShapeDtypeStruct((SHARE, LANES), F32),)
        + (jax.ShapeDtypeStruct((SHARE, LANES), BF16),) * 3,
        in_specs=[SMEM_SPEC, VMEM_SPEC, VMEM_SPEC],
        out_specs=(VMEM_SPEC,) * 4,
        scratch_shapes=[pltpu.VMEM((GROUPS // 2, SHARE, LANES), F32)],
        compiler_params=params(16),
        cost_estimate=pl.CostEstimate(flops=0, bytes_accessed=500_000, transcendentals=0),
        name="deal",
    )(rank, kept, came)


def add_kernel(after_ref, *refs):
    parts = [ref[...].astype(F32) for ref in refs[:-1]]
    while len(parts) > 1:
        parts = [first + second for first, second in zip(parts[::2], parts[1::2])]
    refs[-1][...] = parts[0].astype(refs[-1].dtype)


def add_call(after, parts, dtype=BF16):
    return pl.pallas_call(
        add_kernel,
        out_shape=jax.ShapeDtypeStruct(parts[0].shape, dtype),
        in_specs=[ANY_SPEC] + [VMEM_SPEC] * len(parts),
        out_specs=VMEM_SPEC,
        compiler_params=params(16),
        cost_estimate=pl.CostEstimate(flops=0, bytes_accessed=500_000, transcendentals=0),
        name="add",
    )(after, *parts)


def collect_kernel(after_ref, rank_ref, *refs):
    y = y_of(rank_ref)
    for s, share_ref in enumerate(refs[:-1]):
        refs[-1][y ^ s] = share_ref[...]


def collect_call(after, rank, shares):
    return pl.pallas_call(
        collect_kernel,
        out_shape=jax.ShapeDtypeStruct((GROUPS // 2, SHARE, LANES), BF16),
        in_specs=[ANY_SPEC, SMEM_SPEC] + [VMEM_SPEC] * len(shares),
        out_specs=VMEM_SPEC,
        compiler_params=params(16),
        cost_estimate=pl.CostEstimate(flops=0, bytes_accessed=500_000, transcendentals=0),
        name="collect",
    )(after, rank, *shares)


def split_kernel(rank_ref, mine_ref, theirs_ref, conv_ref, down_ref, sums_ref):
    core = core_of(rank_ref)
    for y in range(GROUPS // 2):
        sums_ref[share_rows(2 * y + core)] = mine_ref[y].astype(F32)
        sums_ref[share_rows(2 * y + 1 - core)] = theirs_ref[y].astype(F32)
    for a in range(3):
        for b in range(3):
            for c in range(3):
                chunk, upper = (b, c) if c < 2 else ((3, b) if b < 2 else (4, 0))
                base = chunk * 192 + a * 64
                block = sums_ref[base : base + 64]
                block = swap_halves(block) if upper else block
                conv_ref[9 * a + 3 * b + c] = block[:, :64]
    for t in range(4):
        block = sums_ref[CONV_ROWS + t * LANES : CONV_ROWS + (t + 1) * LANES].T
        down_ref[t] = block[:64]
        down_ref[t + 4] = block[64:]


def split_call(rank, mine, theirs):
    return pl.pallas_call(
        split_kernel,
        out_shape=(
            jax.ShapeDtypeStruct((27, 64, 64), F32),
            jax.ShapeDtypeStruct((8, 64, LANES), F32),
        ),
        in_specs=[SMEM_SPEC] + [VMEM_SPEC] * 2,
        out_specs=(VMEM_SPEC,) * 2,
        scratch_shapes=[pltpu.VMEM((CONV_ROWS + DOWN_ROWS, LANES), F32)],
        compiler_params=params(16),
        name="split",
    )(rank, mine, theirs)


def swaps(axis, step=1):
    return [(i, i ^ step) for i in range(lax.axis_size(axis))]


def swapped(array, axis, steps):
    return [lax.ppermute(array, axis, swaps(axis, step)) for step in steps]


def exchange(pair, other):
    bricks = ("y", "core", "z", "x")
    rows = lax.axis_size(("z", "x"))
    across = []
    for device in range(lax.axis_size(bricks)):
        row = device % rows
        if row in (0, rows - 1):
            across.append((device, device ^ rows))
        else:
            across.append((device, device + 1 if row % 2 else device - 1))
    return lax.ppermute(pair, ("z", "x"), swaps(("z", "x"))), lax.ppermute(other, bricks, across)


def body(fine_input, conv_weight, down_weight, coarse_cot, neighbours, children):
    dev = ("z", "x")
    rank = lax.axis_index(("y", "core", "z", "x")).reshape(1).astype(jnp.int32)

    voxels, pair, other, token = faces_call(rank, fine_input.reshape(LANES, SIDE**3))
    own, send = cot_call(token, children, rank, coarse_cot.reshape(LANES, SIDE**3))
    pair, other = exchange(pair, other)
    came = lax.ppermute(send, dev, swaps(dev))
    forward, backward, down, down_t = weights_call(conv_weight, down_weight.transpose(0, 2, 1))
    inner = inner_call(neighbours, voxels)
    octants, slope, act, *edges = forward_call(
        neighbours, rank, pair, other, inner, forward, down
    )
    mine, other_out, grads, turned, spun = back_call(rank, own, came, down_t, slope, octants)
    theirs, grad_other = exchange(mine, other_out)

    kept, sent = weigh_call(rank, inner, edges, act, turned, spun)
    (came,) = swapped(sent, "core", (1,))
    own, *shares = deal_call(rank, kept, came)
    came = [lax.ppermute(share, "y", swaps("y", s + 1)) for s, share in enumerate(shares)]
    *taps_in, token = input_taps_call(own, neighbours, rank, grads, theirs, grad_other)
    part = add_call(token, [own, *came], F32)
    came = swapped(part, "x", (1, 2, 3))
    input_grad, token = input_half_call(part, taps_in, backward, 0)
    part = add_call(token, [part, *came])
    came = swapped(part, "z", (1, 2, 3))
    coarse, token = coarse_half_call(part, children, rank, mine, theirs, 0)
    part = add_call(token, [part, *came])
    came = swapped(part, "z", (4,))
    input_grad, token = input_half_call(part, taps_in, backward, 1, (input_grad,))
    part = add_call(token, [part, *came])
    came = swapped(part, "y", (1, 2, 3))
    coarse, token = coarse_half_call(part, children, rank, mine, theirs, 1, (coarse,))
    shares = collect_call(token, rank, [part, *came])
    (came,) = swapped(shares, "core", (1,))
    conv_grad, down_grad = split_call(rank, shares, came)
    return (
        coarse.reshape(1, LANES, SIDE**3),
        input_grad.reshape(2, 64, SIDE**3),
        conv_grad,
        down_grad.transpose(0, 2, 1),
    )


def solution(mesh):
    grp, dev = mesh.devices.shape
    mesh = jax.sharding.Mesh(
        mesh.devices.reshape(grp // 2, 2, dev // 4, 4), ("y", "core", "z", "x")
    )
    bricks = ("y", "core", "z", "x")
    in_specs = (P(bricks, None, None), P(), P(), P(bricks, None, None), P(bricks, None), P(bricks, None))
    out_specs = (P(bricks, None, None), P(bricks, None, None), P(), P())
    return jax.shard_map(body, mesh=mesh, in_specs=in_specs, out_specs=out_specs, check_vma=False)
```
